256 devices in a mesh: expert: 32 (over x, y, core), etp: 8 (over z).
Axes of the slice: x: 4, y: 4, z: 8, core: 2. Of those that a mesh axis runs over, the one named last changes fastest.
Arguments:
- tokens: bfloat16 [4096, 2048], P('expert', 'etp'), may hold values from -6 to 6
- grad_output: bfloat16 [4096, 2048], P('expert', 'etp'), may hold values from -2 to 2
- gates: bfloat16 [4096, 8], P('expert'), may hold values from 0.049804688 to 0.5
- ids: int32 [4096, 8], P('expert'), may hold values from 0 to 63, all different within a row; in each aligned block of 128 rows (0 to 127, 128 to 255, ...) at most 24 rows name the same one
- gate_weight: bfloat16 [64, 2048, 1024], P('expert', None, 'etp'), may hold values from -0.125 to 0.125
- up_weight: bfloat16 [64, 2048, 1024], P('expert', None, 'etp'), may hold values from -0.125 to 0.125
- down_weight: bfloat16 [64, 1024, 2048], P('expert', 'etp'), may hold values from -0.1875 to 0.1875
Outputs:
- grad_tokens: bfloat16 [4096, 2048], P('expert', 'etp')
- grad_gates: float32 [4096, 8], P('expert')
- grad_gate_weight: float32 [64, 2048, 1024], P('expert', None, 'etp')
- grad_up_weight: float32 [64, 2048, 1024], P('expert', None, 'etp')
- grad_down_weight: float32 [64, 1024, 2048], P('expert', 'etp')
The draws below stay inside these ranges and needn't reach their ends.
Inputs may be any that keep to these rules, and one draw needn't show every extreme that they name: `ids`: in each aligned block of 128 tokens (those of one index of expert), no expert is named by more than 24 entries, a bound that some block reaches. The 8 experts of a token differ.
All inputs are finite; a program needn't handle non-finite values.
Results may differ from the reference program's by a relative error of at most 0.019.
Values may be sent and summed in bfloat16 or wider, within the bound.
A program may use at most 128 MiB of HBM per device.

```python
import math
import jax
import jax.numpy as jnp
import numpy as np
from jax import lax

D = 2048
FF = 1024
TOP = 8
TOK_DEV = 128
EXPERTS = 64
CAP = 24
TOKENS = 4096
N_EXPERT = 32
N_ETP = 8


def steps_of(stream_key, shape, split, least, largest):
    def one(dim, blocks):
        draws = jax.random.uniform(jax.random.fold_in(jax.random.fold_in(stream_key, 6), dim), (blocks,), jnp.float32, least / len(split), largest / len(split))
        return jnp.repeat(jnp.exp(draws), shape[dim] // blocks).reshape((-1,) + (1,) * (len(shape) - dim - 1))

    level = one(*split[0])
    for cut in split[1:]:
        level = level * one(*cut)
    return level


def shared_out(stream_key, own, number, rows, amount, top, limit, slope):
    order = jax.random.permutation(stream_key, amount)
    packed, ordinary = shares(amount, rows * top, limit, slope, True), shares(amount, rows * top, limit, slope, False)
    places = jnp.arange(amount)

    def named(tallies, rotation):
        used = int((tallies > 0).sum())
        fixed = max(1, used // 4)
        shifted = fixed + (places - fixed + rotation * (used - fixed)) % max(1, amount - fixed)
        return jnp.zeros((amount,), jnp.int32).at[order[jnp.where(places < fixed, places, shifted)]].set(jnp.asarray(tallies, jnp.int32))

    tallies = jnp.where(number % 4 == 0, named(packed, number // 4), named(ordinary, number - number // 4 - 1))
    mixed = jax.random.permutation(jax.random.fold_in(own, 3), amount)
    donor, receiver = mixed[0:amount // 2 * 2:2], mixed[1:amount // 2 * 2:2]
    slack = jnp.minimum(tallies[donor] - 1, limit - tallies[receiver]) // 2
    slack = jnp.where((donor == order[0]) | (receiver == order[0]) | (tallies[receiver] == 0), 0, jnp.maximum(slack, 0))
    shifted = jax.random.randint(jax.random.fold_in(own, 4), (amount // 2,), 0, 1 << 20) % (slack + 1)
    tallies = tallies.at[donor].add(-shifted).at[receiver].add(shifted)
    labels = jnp.searchsorted(jnp.cumsum(tallies), jnp.arange(rows * top), side="right").astype(jnp.int32)
    listing = labels.reshape(top, rows).T
    listing = listing[jax.random.permutation(jax.random.fold_in(own, 1), rows)]
    rotation = jax.random.randint(jax.random.fold_in(own, 2), (rows, 1), 0, top)
    return jnp.take_along_axis(listing, (jnp.arange(top)[None, :] + rotation) % top, axis=1)


def shares(count, total, limit, lean, full):
    loads = [(1 << 20) // math.isqrt(standing ** lean) + 1 for standing in range(1, count + 1)]
    largest = limit if full else min(limit, max(-(-total // count), total * loads[0] // sum(loads)))
    least = 1 if total - largest >= count - 1 else 0
    given, spare = [largest] + [least] * (count - 1), total - largest - least * (count - 1)
    while spare > 0:
        candidates = [i for i in range(1, count) if given[i] < largest] or [i for i in range(1, count) if given[i] < limit]
        mass, budget = sum([loads[i] for i in candidates]), spare
        for i in candidates:
            extra = min(limit - given[i], max(1, budget * loads[i] // mass), spare)
            given[i] = given[i] + extra
            spare = spare - extra
    return np.array(given)


def normal_values(stream_key, extent, spread, most, cuts=(), kind=jnp.bfloat16):
    level = steps_of(stream_key, extent, cuts, -0.22, 0.18) if cuts else 1.0
    values = jax.random.normal(stream_key, extent, jnp.float32) * spread * level
    return jnp.minimum(jnp.maximum(values, -most), most).astype(kind)


def setup_inputs(seed: int = 0) -> dict:
    keys = jax.random.split(jax.random.key(seed), 8)
    tokens = normal_values(keys[0], (TOKENS, D), 1.0, 6.0, ((0, 32), (1, 8)))
    grad_output = normal_values(keys[1], (TOKENS, D), 0.25, 2.0, ((0, 32), (1, 8)))
    gates = jnp.clip(0.049804688 + 0.4501953 * jax.random.uniform(keys[2], (TOKENS, TOP), jnp.float32) ** steps_of(keys[2], (TOKENS, TOP), ((0, 32),), -0.2, 0.2), 0.049804688, 0.5).astype(jnp.bfloat16)
    ids_keys = jax.random.split(jax.random.fold_in(keys[3], 1), TOKENS // TOK_DEV)
    ids_turns = jax.random.permutation(jax.random.fold_in(keys[3], 3), TOKENS // TOK_DEV)
    ids = jax.vmap(lambda own, number: shared_out(jax.random.fold_in(keys[3], 2), own, number, TOK_DEV, EXPERTS, TOP, CAP, 1))(ids_keys, ids_turns).reshape((TOKENS, TOP))
    gate_weight = normal_values(keys[4], (EXPERTS, D, FF), D ** -0.5, 0.125, ((0, 32), (2, 8)))
    up_weight = normal_values(keys[5], (EXPERTS, D, FF), D ** -0.5, 0.125, ((0, 32), (2, 8)))
    down_weight = normal_values(keys[6], (EXPERTS, FF, D), FF ** -0.5, 0.1875, ((0, 32), (1, 8)))
    return dict(tokens=tokens, grad_output=grad_output, gates=gates, ids=ids, gate_weight=gate_weight, up_weight=up_weight, down_weight=down_weight)


def route_slots(id_block, expert_count, capacity):
    flat_ids = id_block.reshape(-1)
    onehot = (flat_ids[:, None] == jnp.arange(expert_count, dtype=jnp.int32)[None, :]).astype(jnp.int32)
    before = jnp.cumsum(onehot, axis=0) - onehot
    return flat_ids * capacity + jnp.sum(before * onehot, axis=1)


def reference(tokens, grad_output, gates, ids, gate_weight, up_weight, down_weight):
    assigned = TOK_DEV * TOP
    slot_total = EXPERTS * CAP
    pad_index = N_EXPERT * assigned
    blocks = ids.reshape(N_EXPERT, TOK_DEV, TOP)

    def block_table(id_block, offset):
        slots = route_slots(id_block, EXPERTS, CAP)
        filled = jnp.full((slot_total,), pad_index, jnp.int32)
        return filled.at[slots].set(offset + jnp.arange(assigned, dtype=jnp.int32))

    offsets = (jnp.arange(N_EXPERT, dtype=jnp.int32) * assigned).astype(jnp.int32)
    tables = jax.vmap(block_table)(blocks, offsets)
    tables = tables.reshape(N_EXPERT, EXPERTS, CAP).transpose(1, 0, 2).reshape(EXPERTS, N_EXPERT * CAP)
    token_of = jnp.where(tables < pad_index, tables // TOP, TOKENS).astype(jnp.int32)
    tokens_pad = jnp.concatenate([tokens, jnp.zeros((1, D), jnp.bfloat16)], axis=0)
    grads_pad = jnp.concatenate([grad_output, jnp.zeros((1, D), jnp.bfloat16)], axis=0)
    gate_pad = jnp.concatenate([gates.reshape(-1), jnp.zeros((1,), jnp.bfloat16)])
    block_width = FF // N_ETP

    def expert_step(carry, inputs):
        token_grads, gate_grads = carry
        assign_index, token_index, w_gate, w_up, w_down = inputs
        token_rows = tokens_pad[token_index]
        grad_rows = grads_pad[token_index]
        gate_col = gate_pad[assign_index].astype(jnp.float32)[:, None]
        gate_pre = jnp.dot(token_rows, w_gate, preferred_element_type=jnp.float32)
        up_pre = jnp.dot(token_rows, w_up, preferred_element_type=jnp.float32)
        hidden_raw = jnp.dot(grad_rows, w_down.T, preferred_element_type=jnp.float32)
        sigmoid_gate = jax.nn.sigmoid(gate_pre)
        swish = gate_pre * sigmoid_gate
        hidden = swish * up_pre
        gate_terms = jnp.sum(hidden * hidden_raw, axis=1)
        hidden_grad = gate_col * hidden_raw
        pre_up_grad = (hidden_grad * swish).astype(jnp.bfloat16)
        pre_gate_grad = (hidden_grad * up_pre * sigmoid_gate * (1.0 + gate_pre * (1.0 - sigmoid_gate))).astype(jnp.bfloat16)
        scaled_hidden = (gate_col * hidden).astype(jnp.bfloat16)
        grad_down = jnp.dot(scaled_hidden.T, grad_rows, preferred_element_type=jnp.float32)
        grad_gate = jnp.dot(token_rows.T, pre_gate_grad, preferred_element_type=jnp.float32)
        grad_up = jnp.dot(token_rows.T, pre_up_grad, preferred_element_type=jnp.float32)
        row_count = token_index.shape[0]
        gate_blocks = pre_gate_grad.astype(jnp.float32).reshape(row_count, N_ETP, block_width)
        up_blocks = pre_up_grad.astype(jnp.float32).reshape(row_count, N_ETP, block_width)
        wg_blocks = w_gate.astype(jnp.float32).reshape(D, N_ETP, block_width)
        wu_blocks = w_up.astype(jnp.float32).reshape(D, N_ETP, block_width)
        partial_value = jnp.einsum("rpf,dpf->prd", gate_blocks, wg_blocks) + jnp.einsum("rpf,dpf->prd", up_blocks, wu_blocks)
        partial_value = lax.optimization_barrier(partial_value.astype(jnp.bfloat16))
        slot_grads = jnp.sum(partial_value.astype(jnp.float32), axis=0)
        token_grads = token_grads.at[token_index].add(slot_grads)
        gate_grads = gate_grads.at[assign_index].add(gate_terms)
        return (token_grads, gate_grads), (grad_gate, grad_up, grad_down)

    init = (jnp.zeros((TOKENS + 1, D), jnp.float32), jnp.zeros((pad_index + 1,), jnp.float32))
    (token_grads, gate_grads), (grad_gate, grad_up, grad_down) = lax.scan(
        expert_step, init, (tables, token_of, gate_weight, up_weight, down_weight))
    grad_tokens = token_grads[:TOKENS].astype(jnp.bfloat16)
    grad_gates = gate_grads[:pad_index].reshape(TOKENS, TOP)
    return (grad_tokens, grad_gates, grad_gate, grad_up, grad_down)
```

```python
import functools

import jax
import jax.numpy as jnp
from jax import lax
from jax.experimental import pallas as pl
from jax.experimental.pallas import tpu as pltpu
from jax.sharding import PartitionSpec as P

MESH = pl.DeviceIdType.MESH
BF = jnp.bfloat16
F32 = jnp.float32
NX, NY, NZ = 4, 4, 8
TOK = 128
W = 256
D = 2048
H = 128
TOP = 8
CAP = 24
E4 = 4
PAIRS = 8
ROWS = 2 * CAP * PAIRS
SPLIT_T = (48, 32, 48)
SPLIT_G = (32, 48, 48)
SPLIT_R = (48, 32, 48)
COMPUTE = True


class Net:
    def __init__(self, send, recv):
        self.send_sem, self.recv_sem = send, recv
        self.count = 0
        self.pending = []

    def send(self, src, dst, device):
        k = self.count
        self.count += 1
        copy = pltpu.make_async_remote_copy(
            src_ref=src,
            dst_ref=dst,
            send_sem=self.send_sem.at[k],
            recv_sem=self.recv_sem.at[k],
            device_id=device,
            device_id_type=MESH,
        )
        copy.start()
        self.pending.append(copy)
        return copy

    def drain(self):
        for copy in self.pending:
            copy.wait_send()
        self.pending = []


def half16(n):
    return (n // 2 + 15) // 16 * 16


def ring4_gather(net, i, full, h0, h1, right, left):
    a = net.send(full(i), full(i), right)
    b = net.send(full(i), full(i), left)
    yield
    prev, following = lax.rem(i + 3, 4), lax.rem(i + 1, 4)
    a.wait_recv()
    c = net.send(h0(prev), h0(prev), right)
    b.wait_recv()
    d = net.send(h1(following), h1(following), left)
    yield
    c.wait_recv()
    d.wait_recv()
    yield


def ring8_gather(net, i, full, h0, h1, right, left):
    a = net.send(full(i), full(i), right)
    b = net.send(full(i), full(i), left)
    yield
    for step in (1, 2, 3):
        prev, following = lax.rem(i + 8 - step, 8), lax.rem(i + step, 8)
        va, vb = (full, full) if step < 3 else (h0, h1)
        a.wait_recv()
        a = net.send(va(prev), va(prev), right)
        b.wait_recv()
        b = net.send(vb(following), vb(following), left)
        yield
    a.wait_recv()
    b.wait_recv()
    yield


def add_into(dst, src):
    dst[...] = (dst[...].astype(F32) + src[...].astype(F32)).astype(BF)


def ring_scatter(net, n, i, full, h0, h1, slots, right, left):
    far = lax.rem(i + n // 2, n)
    ra, rb = slots[0]
    a = net.send(h0(far), ra, right)
    b = net.send(h1(far), rb, left)
    yield
    for step in range(1, n // 2):
        to_r, to_l = lax.rem(i + n // 2 - step, n), lax.rem(i + n // 2 + step, n)
        va, vb = (h0, h1) if step == 1 else (full, full)
        a.wait_recv()
        add_into(va(to_r), ra)
        ra, rb_next = slots[step]
        a = net.send(full(to_r), ra, right)
        b.wait_recv()
        add_into(vb(to_l), rb)
        rb = rb_next
        b = net.send(full(to_l), rb, left)
        yield
    a.wait_recv()
    b.wait_recv()
    dst = full(i)
    dst[...] = (dst[...].astype(F32) + ra[...].astype(F32) + rb[...].astype(F32)).astype(BF)
    yield


def run(*gens):
    for g in gens:
        next(g)


def scatter_slots():
    ra, rb, rc = SPLIT_R
    bc = rb + rc
    h = half16
    out = []

    def ring(n, half0, half1, whole):
        out.append([(half0, half1)] + [(whole, whole)] * (n // 2 - 1))

    ring(8, (2, 4, ra, W), (2, 4, ra, W), (4, 4, ra, W))
    ring(4, (2, ra, W), (2, ra, W), (4, ra, W))
    ring(4, (h(ra), W), (ra - h(ra), W), (ra, W))
    ring(4, (2, 8, rb, W), (2, 8, rb, W), (4, 8, rb, W))
    ring(4, (4, rb, W), (4, rb, W), (8, rb, W))
    ring(4, (2, 8, rc, W), (2, 8, rc, W), (4, 8, rc, W))
    ring(4, (4, rc, W), (4, rc, W), (8, rc, W))
    ring(8, (h(bc), W), (bc - h(bc), W), (bc, W))
    return out


N_SEM = 256
N_LOC = 32


def kernel(*refs):
    it = iter(refs)
    take = lambda n: [next(it) for _ in range(n)]
    tok_in, grad_in, rt_in, wg_in, wu_in, wd_in = take(6)
    tok_out, gg_out, dg_out, du_out, dd_out = take(5)
    gt, gg, xs, gxs, wgu, wd, sel, selt = take(8)
    pgu, sh, gp, member, target, gatev = take(6)
    rt, ggd, gg_rx, gg_rz = take(4)
    osg, osd, org, ord_ = take(4)
    stg, std = take(2)
    slots = [[tuple(take(2)) for _ in ring] for ring in scatter_slots()]
    send_sem, recv_sem, loc_sem, stg_sem = take(4)

    e_idx = lax.axis_index("expert")
    z = lax.axis_index("etp")
    core = lax.rem(e_idx, 2)
    y = lax.rem(e_idx // 2, 4)
    x = e_idx // 8

    def dev(dx=0, dy=0, xx=None, yy=None, cc=None, zz=None):
        px = lax.rem(x + dx + 4, 4) if xx is None else xx
        py = lax.rem(y + dy + 4, 4) if yy is None else yy
        pc = core if cc is None else cc
        return ((px * 4 + py) * 2 + pc, z if zz is None else zz)

    xr, xl = dev(dx=1), dev(dx=-1)
    yr, yl = dev(dy=1), dev(dy=-1)
    zr, zl = dev(zz=lax.rem(z + 1, 8)), dev(zz=lax.rem(z + 7, 8))
    x_far, y_far = dev(dx=2), dev(dy=2)
    x_near = dev(xx=x + 1 - 2 * lax.rem(x, 2))
    y_near = dev(yy=y + 1 - 2 * lax.rem(y, 2))
    z1 = dev(zz=z + 1 - 2 * lax.rem(z, 2))
    z2 = dev(zz=z + 2 - 4 * lax.rem(z // 2, 2))
    z4 = dev(zz=lax.rem(z + 4, 8))
    sibling = dev(cc=1 - core)

    own_copies = [
        pltpu.make_async_copy(tok_in, gt.at[x, y, z], loc_sem.at[0]),
        pltpu.make_async_copy(grad_in, gg.at[x, y, z], loc_sem.at[1]),
        pltpu.make_async_copy(rt_in, rt.at[x, y], loc_sem.at[2]),
    ]
    for j in range(2):
        ce = 2 * core + j
        own_copies.append(pltpu.make_async_copy(wg_in.at[j], wgu.at[ce, :, 0:H], loc_sem.at[3 + 3 * j]))
        own_copies.append(pltpu.make_async_copy(wu_in.at[j], wgu.at[ce, :, H : 2 * H], loc_sem.at[4 + 3 * j]))
        own_copies.append(pltpu.make_async_copy(wd_in.at[j], wd.at[ce], loc_sem.at[5 + 3 * j]))
    for c in own_copies:
        c.start()

    barrier = pltpu.get_barrier_semaphore()
    peers = (xr, xl, x_far, yr, yl, y_far, zr, zl, z2, z4, sibling)
    for p in peers:
        pl.semaphore_signal(barrier, inc=1, device_id=p, device_id_type=MESH)
    for c in own_copies[:3]:
        c.wait()
    pl.semaphore_wait(barrier, len(peers))

    net = Net(send_sem, recv_sem)

    class Wave:
        pass

    waves = []
    for buf, (ra, rb, rc) in ((gt, SPLIT_T), (gg, SPLIT_G)):
        w = Wave()
        a0, b0, c0 = 0, ra, ra + rb
        bc = rb + rc
        ha, hbc = half16(ra), half16(bc)
        w.xa = ring4_gather(
            net, x,
            lambda i, buf=buf, ra=ra: buf.at[i, y, z, pl.ds(0, ra)],
            lambda i, buf=buf, ha=ha: buf.at[i, y, z, pl.ds(0, ha)],
            lambda i, buf=buf, ha=ha, ra=ra: buf.at[i, y, z, pl.ds(ha, ra - ha)],
            xr, xl)
        w.ya = ring4_gather(
            net, y,
            lambda i, buf=buf, ra=ra: buf.at[:, i, z, pl.ds(0, ra)],
            lambda i, buf=buf, ra=ra: buf.at[pl.ds(0, 2), i, z, pl.ds(0, ra)],
            lambda i, buf=buf, ra=ra: buf.at[pl.ds(2, 2), i, z, pl.ds(0, ra)],
            yr, yl)
        w.za = ring8_gather(
            net, z,
            lambda i, buf=buf, ra=ra: buf.at[:, :, i, pl.ds(0, ra)],
            lambda i, buf=buf, ra=ra: buf.at[pl.ds(0, 2), :, i, pl.ds(0, ra)],
            lambda i, buf=buf, ra=ra: buf.at[pl.ds(2, 2), :, i, pl.ds(0, ra)],
            zr, zl)
        w.zbc = ring8_gather(
            net, z,
            lambda i, buf=buf, b0=b0, bc=bc: buf.at[x, y, i, pl.ds(b0, bc)],
            lambda i, buf=buf, b0=b0, h=hbc: buf.at[x, y, i, pl.ds(b0, h)],
            lambda i, buf=buf, b0=b0, h=hbc, bc=bc: buf.at[x, y, i, pl.ds(b0 + h, bc - h)],
            zr, zl)
        w.xb = ring4_gather(
            net, x,
            lambda i, buf=buf, b0=b0, rb=rb: buf.at[i, y, :, pl.ds(b0, rb)],
            lambda i, buf=buf, b0=b0, rb=rb: buf.at[i, y, pl.ds(0, 4), pl.ds(b0, rb)],
            lambda i, buf=buf, b0=b0, rb=rb: buf.at[i, y, pl.ds(4, 4), pl.ds(b0, rb)],
            xr, xl)
        w.yb = ring4_gather(
            net, y,
            lambda i, buf=buf, b0=b0, rb=rb: buf.at[:, i, :, pl.ds(b0, rb)],
            lambda i, buf=buf, b0=b0, rb=rb: buf.at[pl.ds(0, 2), i, :, pl.ds(b0, rb)],
            lambda i, buf=buf, b0=b0, rb=rb: buf.at[pl.ds(2, 2), i, :, pl.ds(b0, rb)],
            yr, yl)
        w.yc = ring4_gather(
            net, y,
            lambda i, buf=buf, c0=c0, rc=rc: buf.at[x, i, :, pl.ds(c0, rc)],
            lambda i, buf=buf, c0=c0, rc=rc: buf.at[x, i, pl.ds(0, 4), pl.ds(c0, rc)],
            lambda i, buf=buf, c0=c0, rc=rc: buf.at[x, i, pl.ds(4, 4), pl.ds(c0, rc)],
            yr, yl)
        w.xc = ring4_gather(
            net, x,
            lambda i, buf=buf, c0=c0, rc=rc: buf.at[i, :, :, pl.ds(c0, rc)],
            lambda i, buf=buf, c0=c0, rc=rc: buf.at[i, pl.ds(0, 2), :, pl.ds(c0, rc)],
            lambda i, buf=buf, c0=c0, rc=rc: buf.at[i, pl.ds(2, 2), :, pl.ds(c0, rc)],
            xr, xl)
        waves.append(w)
    wt, wgr = waves

    def both(name):
        run(*[getattr(w, name) for w in waves])

    both("xa")
    both("zbc")
    r = net.send(rt.at[x, y], rt.at[x, y], y_near)
    both("zbc")
    both("xa")
    r.wait_recv()
    yh = 2 * (y // 2)
    r = net.send(rt.at[x, pl.ds(yh, 2)], rt.at[x, pl.ds(yh, 2)], y_far)
    both("zbc")
    both("xa")
    both("ya")
    both("zbc")
    r.wait_recv()
    r = net.send(rt.at[x], rt.at[x], x_near)
    both("zbc")
    both("xb")
    both("yc")
    both("ya")
    both("ya")
    both("za")
    r.wait_recv()
    xh = 2 * (x // 2)
    r = net.send(rt.at[pl.ds(xh, 2)], rt.at[pl.ds(xh, 2)], x_far)
    for c in own_copies[3:]:
        c.wait()
    weight_copies = []
    for j in range(2):
        ce = 2 * core + j
        weight_copies.append(net.send(wgu.at[ce], wgu.at[ce], sibling))
        weight_copies.append(net.send(wd.at[ce], wd.at[ce], sibling))
    both("xb")
    both("yc")
    both("xb")
    both("yc")
    run(wt.yb, wt.xc)
    run(wgr.yb, wgr.xc)
    r.wait_recv()
    first_expert = 4 * (x * 4 + y)

    def route():
        for b in range(16):
            tile = rt[b // 4, b % 4]
            for e in range(E4):
                hit = tile[0:8, :] == (first_expert + e).astype(F32)
                member[e * 16 + b, :] = jnp.sum(jnp.where(hit, 1.0, 0.0), axis=0)
                gatev[e * 16 + b, :] = jnp.sum(jnp.where(hit, tile[8:16, :], 0.0), axis=0)
        tri = jnp.where(
            lax.broadcasted_iota(jnp.int32, (TOK, TOK), 0) < lax.broadcasted_iota(jnp.int32, (TOK, TOK), 1),
            1.0, 0.0).astype(BF)
        m = member[...]
        pos = jnp.dot(m.astype(BF), tri, preferred_element_type=F32)
        target[...] = jnp.where(m > 0.5, pos, -1.0)

        for p in range(PAIRS):
            row = lax.broadcasted_iota(jnp.int32, (CAP, TOK), 0).astype(F32)
            zero = jnp.zeros((CAP, TOK), F32)
            parts = []
            for e in range(E4):
                r0, r1 = e * 16 + 2 * p, e * 16 + 2 * p + 1
                s0 = jnp.where(row == target[r0 : r0 + 1, :], 1.0, 0.0)
                s1 = jnp.where(row == target[r1 : r1 + 1, :], 1.0, 0.0)
                parts.append(jnp.concatenate([s0, zero], axis=1))
                parts.append(jnp.concatenate([zero, s1], axis=1))
            full = jnp.concatenate(parts, axis=0)
            sel[p] = full.astype(BF)
            selt[p] = full.T.astype(BF)

    def pick(src, dst):
        def body(p, _):
            s = sel[p]
            px, py = p // 2, 2 * (p % 2)
            for zz in range(NZ):
                t = src[px, pl.ds(py, 2), zz].reshape(2 * TOK, W)
                o = jnp.dot(s, t, preferred_element_type=F32).astype(BF)
                for e in range(E4):
                    dst[e, pl.ds(pl.multiple_of(p * 48, 16), 48), zz * W : (zz + 1) * W] = o[e * 48 : (e + 1) * 48]
            return 0

        lax.fori_loop(0, PAIRS, body, 0)

    def forward(e):
        xe, ge = xs[e], gxs[e]
        gu = jnp.dot(xe, wgu[e], preferred_element_type=F32)
        raw = lax.dot_general(ge, wd[e], (((1,), (1,)), ((), ())), preferred_element_type=F32)
        gate_pre, up_pre = gu[:, :H], gu[:, H:]
        sig = 1.0 / (1.0 + jnp.exp(-gate_pre))
        swish = gate_pre * sig
        hidden = swish * up_pre
        gp[e] = jnp.broadcast_to(jnp.sum(hidden * raw, axis=1, keepdims=True), (ROWS, H))
        cols = []
        for p in range(PAIRS):
            for k in range(2):
                s = sel[p, pl.ds(pl.multiple_of(e * 48, 16), 48), k * TOK : (k + 1) * TOK].astype(F32)
                g = gatev[pl.ds(e * 16 + 2 * p + k, 1), :]
                cols.append(jnp.sum((s * g)[k * CAP : (k + 1) * CAP], axis=1, keepdims=True))
        gate = jnp.concatenate(cols, axis=0)
        hg = gate * raw
        pgu[e, :, H:] = (hg * swish).astype(BF)
        pgu[e, :, :H] = (hg * up_pre * sig * (1.0 + gate_pre * (1.0 - sig))).astype(BF)
        sh[e] = (gate * hidden).astype(BF)

    def partial(e):
        lhs = pgu[e]
        for zz in range(NZ):
            o = lax.dot_general(lhs, wgu[e, zz * W : (zz + 1) * W, :], (((1,), (1,)), ((), ())),
                                preferred_element_type=F32).astype(BF)
            for p in range(PAIRS):
                gg[p // 2, 2 * (p % 2) + e // 2, zz, pl.ds(pl.multiple_of((e % 2) * 48, 16), 48), :] = o[p * 48 : (p + 1) * 48]

    def spread(p):
        st = selt[p]
        px, py = p // 2, 2 * (p % 2)
        for zz in range(NZ):
            v = gg[px, pl.ds(py, 2), zz, 0:96, :].reshape(192, W)
            o = jnp.dot(st, v, preferred_element_type=F32).astype(BF)
            gt[px, pl.ds(py, 2), zz] = o.reshape(2, TOK, W)

    def gate_terms(p):
        for k in range(2):
            rows = []
            px, py = p // 2, 2 * (p % 2) + k
            tile = rt[px, py][0:8, :]
            acc = jnp.zeros((8, TOK), F32)
            for e in range(E4):
                s = sel[p, e * 48 : (e + 1) * 48, k * TOK : (k + 1) * TOK].astype(F32)
                v = jnp.sum(s * gp[e, pl.ds(pl.multiple_of(p * 48, 16), 48), :], axis=0, keepdims=True)
                acc = acc + jnp.where(tile == (first_expert + e).astype(F32), v, 0.0)
            ggd[px, py] = acc

    def loop(n, f):
        def body(i, _):
            f(i)
            return 0

        lax.fori_loop(0, n, body, 0)

    if COMPUTE:
        route()
    for _ in range(4):
        run(wt.za, wgr.za)
        if _ == 0:
            run(wt.yb, wt.xc, wgr.yb, wgr.xc)
    run(wt.yb, wt.xc, wgr.yb, wgr.xc)
    for c in weight_copies:
        c.wait_recv()
    net.drain()
    if COMPUTE:
        pick(gt, xs)
        pick(gg, gxs)
        loop(E4, forward)
        loop(E4, partial)
        loop(PAIRS, spread)
        loop(PAIRS, gate_terms)

    ra, rb, rc = SPLIT_R
    b0, c0, bc = ra, ra + rb, rb + rc
    ha, hbc = half16(ra), half16(bc)
    sz = pl.ds
    sza = ring_scatter(
        net, 8, z,
        lambda i: gt.at[:, :, i, sz(0, ra)],
        lambda i: gt.at[sz(0, 2), :, i, sz(0, ra)],
        lambda i: gt.at[sz(2, 2), :, i, sz(0, ra)],
        slots[0], zr, zl)
    sya = ring_scatter(
        net, 4, y,
        lambda i: gt.at[:, i, z, sz(0, ra)],
        lambda i: gt.at[sz(0, 2), i, z, sz(0, ra)],
        lambda i: gt.at[sz(2, 2), i, z, sz(0, ra)],
        slots[1], yr, yl)
    sxa = ring_scatter(
        net, 4, x,
        lambda i: gt.at[i, y, z, sz(0, ra)],
        lambda i: gt.at[i, y, z, sz(0, ha)],
        lambda i: gt.at[i, y, z, sz(ha, ra - ha)],
        slots[2], xr, xl)
    syb = ring_scatter(
        net, 4, y,
        lambda i: gt.at[:, i, :, sz(b0, rb)],
        lambda i: gt.at[sz(0, 2), i, :, sz(b0, rb)],
        lambda i: gt.at[sz(2, 2), i, :, sz(b0, rb)],
        slots[3], yr, yl)
    sxb = ring_scatter(
        net, 4, x,
        lambda i: gt.at[i, y, :, sz(b0, rb)],
        lambda i: gt.at[i, y, sz(0, 4), sz(b0, rb)],
        lambda i: gt.at[i, y, sz(4, 4), sz(b0, rb)],
        slots[4], xr, xl)
    sxc = ring_scatter(
        net, 4, x,
        lambda i: gt.at[i, :, :, sz(c0, rc)],
        lambda i: gt.at[i, sz(0, 2), :, sz(c0, rc)],
        lambda i: gt.at[i, sz(2, 2), :, sz(c0, rc)],
        slots[5], xr, xl)
    syc = ring_scatter(
        net, 4, y,
        lambda i: gt.at[x, i, :, sz(c0, rc)],
        lambda i: gt.at[x, i, sz(0, 4), sz(c0, rc)],
        lambda i: gt.at[x, i, sz(4, 4), sz(c0, rc)],
        slots[6], yr, yl)
    szbc = ring_scatter(
        net, 8, z,
        lambda i: gt.at[x, y, i, sz(b0, bc)],
        lambda i: gt.at[x, y, i, sz(b0, hbc)],
        lambda i: gt.at[x, y, i, sz(b0 + hbc, bc - hbc)],
        slots[7], zr, zl)

    def gate_ring():
        xo = 2 - 2 * (x // 2)
        c = net.send(ggd.at[sz(xo, 2)], gg_rx.at[sz(0, 2)], x_far)
        yield
        c.wait_recv()
        xm = 2 * (x // 2)
        for k in range(2):
            for j in range(4):
                ggd[xm + k, j] = ggd[xm + k, j] + gg_rx[k, j]
        xn = x + 1 - 2 * lax.rem(x, 2)
        c = net.send(ggd.at[xn], gg_rx.at[2], x_near)
        yield
        c.wait_recv()
        for j in range(4):
            ggd[x, j] = ggd[x, j] + gg_rx[2, j]
        yo = 2 - 2 * (y // 2)
        c = net.send(ggd.at[x, sz(yo, 2)], gg_rx.at[3, sz(0, 2)], y_far)
        yield
        c.wait_recv()
        ym = 2 * (y // 2)
        for k in range(2):
            ggd[x, ym + k] = ggd[x, ym + k] + gg_rx[3, k]
        yn = y + 1 - 2 * lax.rem(y, 2)
        c = net.send(ggd.at[x, yn], gg_rx.at[3, 2], y_near)
        yield
        c.wait_recv()
        gg_rz[0] = ggd[x, y] + gg_rx[3, 2]
        for k, d in enumerate((z1, z2, z4)):
            c = net.send(gg_rz.at[2 * k], gg_rz.at[2 * k + 1], d)
            yield
            c.wait_recv()
            gg_rz[2 * k + 2] = gg_rz[2 * k] + gg_rz[2 * k + 1]
        yield

    ring = gate_ring()
    run(sza, sxc, syb)
    run(ring)

    tn = (((0,), (0,)), ((), ()))

    def other_grads(j):
        e = 2 * (1 - core) + j

        def body(m, _):
            f = pl.ds(pl.multiple_of(m * W, W), W)
            osg[j, f, :] = lax.dot_general(xs[e, :, f], pgu[e], tn, preferred_element_type=F32).astype(BF)
            osd[j, :, f] = lax.dot_general(sh[e], gxs[e, :, f], tn, preferred_element_type=F32).astype(BF)
            return 0

        lax.fori_loop(0, NZ, body, 0)

    grad_copies = []
    if COMPUTE:
        for j in range(2):
            other_grads(j)
            grad_copies.append(net.send(osg.at[j], org.at[j], sibling))
            grad_copies.append(net.send(osd.at[j], ord_.at[j], sibling))
    run(sza, sxc, syb, ring)
    run(sza, ring)
    run(sxc, syb, ring)
    run(syc, sxb)
    run(sza, ring)
    run(syc, sxb, ring)
    run(sza, ring)
    run(syc, sxb, ring)
    run(sya, szbc)
    run(sya, szbc)
    run(sya, szbc)
    run(sxa, szbc)
    run(sxa, szbc)
    run(sxa)

    if COMPUTE:
        for c in grad_copies:
            c.wait_recv()

        def own_grads(t, _):
            j, m = t // NZ, t % NZ
            e = 2 * core + j
            f = pl.ds(pl.multiple_of(m * W, W), W)
            slot = lax.rem(t, 2)

            def outs(j, m, slot):
                f = pl.ds(pl.multiple_of(m * W, W), W)
                return [
                    pltpu.make_async_copy(stg.at[slot, :, 0:H], dg_out.at[j, f, :], stg_sem.at[slot, 0]),
                    pltpu.make_async_copy(stg.at[slot, :, H : 2 * H], du_out.at[j, f, :], stg_sem.at[slot, 1]),
                    pltpu.make_async_copy(std.at[slot], dd_out.at[j, :, f], stg_sem.at[slot, 2]),
                ]

            @pl.when(t >= 2)
            def _():
                for c in outs(j, m, slot):
                    c.wait()

            a = lax.dot_general(xs[e, :, f], pgu[e], tn, preferred_element_type=F32)
            stg[slot] = a + org[j, f, :].astype(F32)
            b = lax.dot_general(sh[e], gxs[e, :, f], tn, preferred_element_type=F32)
            std[slot] = b + ord_[j, :, f].astype(F32)
            for c in outs(j, m, slot):
                c.start()
            return 0

        lax.fori_loop(0, 2 * NZ, own_grads, 0)
        for slot in range(2):
            for c in (
                pltpu.make_async_copy(stg.at[slot, :, 0:H], dg_out.at[0, 0:W, :], stg_sem.at[slot, 0]),
                pltpu.make_async_copy(stg.at[slot, :, H : 2 * H], du_out.at[0, 0:W, :], stg_sem.at[slot, 1]),
                pltpu.make_async_copy(std.at[slot], dd_out.at[0, :, 0:W], stg_sem.at[slot, 2]),
            ):
                c.wait()

    tok_out[...] = gt[x, y, z]
    gg_out[...] = gg_rz[6]
    net.drain()


def local(tokens, grad_output, gates, ids, gate_weight, up_weight, down_weight):
    rt = jnp.concatenate([ids.astype(F32), gates.astype(F32)], axis=1).T
    any_spec = pl.BlockSpec(memory_space=pl.ANY)
    vmem = pl.BlockSpec(memory_space=pltpu.VMEM)
    big = (NX, NY, NZ, TOK, W)
    scratch = [
        pltpu.VMEM(big, BF),
        pltpu.VMEM(big, BF),
        pltpu.VMEM((E4, ROWS, D), BF),
        pltpu.VMEM((E4, ROWS, D), BF),
        pltpu.VMEM((E4, D, 2 * H), BF),
        pltpu.VMEM((E4, H, D), BF),
        pltpu.VMEM((PAIRS, 192, 2 * TOK), BF),
        pltpu.VMEM((PAIRS, 2 * TOK, 192), BF),
        pltpu.VMEM((E4, ROWS, 2 * H), BF),
        pltpu.VMEM((E4, ROWS, H), BF),
        pltpu.VMEM((E4, ROWS, H), F32),
        pltpu.VMEM((64, TOK), F32),
        pltpu.VMEM((64, TOK), F32),
        pltpu.VMEM((64, TOK), F32),
        pltpu.VMEM((NX, NY, 16, TOK), F32),
        pltpu.VMEM((NX, NY, 8, TOK), F32),
        pltpu.VMEM((4, 4, 8, TOK), F32),
        pltpu.VMEM((7, 8, TOK), F32),
        pltpu.VMEM((2, D, 2 * H), BF),
        pltpu.VMEM((2, H, D), BF),
        pltpu.VMEM((2, D, 2 * H), BF),
        pltpu.VMEM((2, H, D), BF),
        pltpu.VMEM((2, W, 2 * H), F32),
        pltpu.VMEM((2, H, W), F32),
    ]
    for ring in scatter_slots():
        for pair in ring:
            for shape in pair:
                scratch.append(pltpu.VMEM(shape, BF))
    scratch += [
        pltpu.SemaphoreType.DMA((N_SEM,)),
        pltpu.SemaphoreType.DMA((N_SEM,)),
        pltpu.SemaphoreType.DMA((N_LOC,)),
        pltpu.SemaphoreType.DMA((2, 3)),
    ]
    outs = pl.pallas_call(
        kernel,
        out_shape=(
            jax.ShapeDtypeStruct((TOK, W), BF),
            jax.ShapeDtypeStruct((8, TOK), F32),
            jax.ShapeDtypeStruct((2, D, H), F32),
            jax.ShapeDtypeStruct((2, D, H), F32),
            jax.ShapeDtypeStruct((2, H, D), F32),
        ),
        in_specs=[any_spec] * 6,
        out_specs=(vmem, vmem, any_spec, any_spec, any_spec),
        scratch_shapes=scratch,
        compiler_params=pltpu.CompilerParams(
            collective_id=0, has_side_effects=True, vmem_limit_bytes=63 * 1024 * 1024
        ),
    )(tokens, grad_output, rt, gate_weight, up_weight, down_weight)
    grad_tokens, gate_grads, grad_gate, grad_up, grad_down = outs
    return (grad_tokens, gate_grads.T, grad_gate, grad_up, grad_down)


def solution(mesh):
    return jax.shard_map(
        local,
        mesh=mesh,
        in_specs=(
            P("expert", "etp"),
            P("expert", "etp"),
            P("expert", None),
            P("expert", None),
            P("expert", None, "etp"),
            P("expert", None, "etp"),
            P("expert", "etp", None),
        ),
        out_specs=(
            P("expert", "etp"),
            P("expert", None),
            P("expert", None, "etp"),
            P("expert", None, "etp"),
            P("expert", "etp", None),
        ),
        check_vma=False,
    )
```

```python
import functools

import jax
import jax.numpy as jnp
from jax import lax
from jax.experimental import pallas as pl
from jax.experimental.pallas import tpu as pltpu
from jax.sharding import PartitionSpec as P

MESH = pl.DeviceIdType.MESH
BF = jnp.bfloat16
F32 = jnp.float32
NX, NY, NZ = 4, 4, 8
TOK = 128
W = 256
D = 2048
H = 128
TOP = 8
CAP = 24
E4 = 4
PAIRS = 8
ROWS = 2 * CAP * PAIRS
SPLIT_G = (48, 96, 112)
SPLIT_R = (32, 48, 48)
COMPUTE = True


class Net:
    def __init__(self, send, recv):
        self.send_sem, self.recv_sem = send, recv
        self.count = 0
        self.pending = []

    def send(self, src, dst, device):
        k = self.count
        self.count += 1
        copy = pltpu.make_async_remote_copy(
            src_ref=src,
            dst_ref=dst,
            send_sem=self.send_sem.at[k],
            recv_sem=self.recv_sem.at[k],
            device_id=device,
            device_id_type=MESH,
        )
        copy.start()
        self.pending.append(copy)
        return copy

    def drain(self):
        for copy in self.pending:
            copy.wait_send()
        self.pending = []


def half16(n):
    return (n // 2 + 15) // 16 * 16


def ring4_gather(net, i, full, h0, h1, right, left):
    a = net.send(full(i), full(i), right)
    b = net.send(full(i), full(i), left)
    yield
    prev, following = lax.rem(i + 3, 4), lax.rem(i + 1, 4)
    a.wait_recv()
    c = net.send(h0(prev), h0(prev), right)
    b.wait_recv()
    d = net.send(h1(following), h1(following), left)
    yield
    c.wait_recv()
    d.wait_recv()
    yield


def ring8_gather(net, i, full, h0, h1, right, left):
    a = net.send(full(i), full(i), right)
    b = net.send(full(i), full(i), left)
    yield
    for step in (1, 2, 3):
        prev, following = lax.rem(i + 8 - step, 8), lax.rem(i + step, 8)
        va, vb = (full, full) if step < 3 else (h0, h1)
        a.wait_recv()
        a = net.send(va(prev), va(prev), right)
        b.wait_recv()
        b = net.send(vb(following), vb(following), left)
        yield
    a.wait_recv()
    b.wait_recv()
    yield


def add_into(dst, src):
    dst[...] = (dst[...].astype(F32) + src[...].astype(F32)).astype(BF)


def ring_scatter(net, n, i, full, h0, h1, slots, right, left):
    far = lax.rem(i + n // 2, n)
    ra, rb = slots[0]
    a = net.send(h0(far), ra, right)
    b = net.send(h1(far), rb, left)
    yield
    for step in range(1, n // 2):
        to_r, to_l = lax.rem(i + n // 2 - step, n), lax.rem(i + n // 2 + step, n)
        va, vb = (h0, h1) if step == 1 else (full, full)
        a.wait_recv()
        add_into(va(to_r), ra)
        ra, rb_next = slots[step]
        a = net.send(full(to_r), ra, right)
        b.wait_recv()
        add_into(vb(to_l), rb)
        rb = rb_next
        b = net.send(full(to_l), rb, left)
        yield
    a.wait_recv()
    b.wait_recv()
    dst = full(i)
    dst[...] = (dst[...].astype(F32) + ra[...].astype(F32) + rb[...].astype(F32)).astype(BF)
    yield


def run(*gens):
    for g in gens:
        next(g)


def scatter_slots():
    ra, rb, rc = SPLIT_R
    h = half16
    out = []

    def ring(n, half0, half1, whole):
        out.append([(half0, half1)] + [(whole, whole)] * (n // 2 - 1))

    for _ in range(NZ):
        ring(4, (2, rc, W), (2, rc, W), (4, rc, W))
        ring(4, (2, rb, W), (2, rb, W), (4, rb, W))
    ring(8, (2, 4, ra, W), (2, 4, ra, W), (4, 4, ra, W))
    ring(8, (2, rb, W), (2, rb, W), (4, rb, W))
    ring(8, (2, rc, W), (2, rc, W), (4, rc, W))
    ring(4, (2, ra, W), (2, ra, W), (4, ra, W))
    ring(4, (h(ra), W), (ra - h(ra), W), (ra, W))
    ring(4, (h(rb), W), (rb - h(rb), W), (rb, W))
    ring(4, (h(rc), W), (rc - h(rc), W), (rc, W))
    return out


N_SEM = 320
N_LOC = 32


def kernel(*refs):
    it = iter(refs)
    take = lambda n: [next(it) for _ in range(n)]
    tok_in, grad_in, ids_in, gates_in, wg_in, wu_in, wd_in = take(7)
    tok_out, gg_out, dgu_out, dd_out = take(4)
    buf, xs, gxs, wgu, wd, sel, selt, part = take(8)
    agu, araw, pgu, sh, gp, member, target, gatev = take(8)
    rt, ggd, gg_rx, gg_rz = take(4)
    osg, osd, org, ord_ = take(4)
    stg, std = take(2)
    slots = [[tuple(take(2)) for _ in ring] for ring in scatter_slots()]
    send_sem, recv_sem, loc_sem, stg_sem = take(4)

    e_idx = lax.axis_index("expert")
    z = lax.axis_index("etp")
    core = lax.rem(e_idx, 2)
    y = lax.rem(e_idx // 2, 4)
    x = e_idx // 8

    def dev(dx=0, dy=0, xx=None, yy=None, cc=None, zz=None):
        px = lax.rem(x + dx + 4, 4) if xx is None else xx
        py = lax.rem(y + dy + 4, 4) if yy is None else yy
        pc = core if cc is None else cc
        return ((px * 4 + py) * 2 + pc, z if zz is None else zz)

    xr, xl = dev(dx=1), dev(dx=-1)
    yr, yl = dev(dy=1), dev(dy=-1)
    zr, zl = dev(zz=lax.rem(z + 1, 8)), dev(zz=lax.rem(z + 7, 8))
    x_far, y_far = dev(dx=2), dev(dy=2)
    x_near = dev(xx=x + 1 - 2 * lax.rem(x, 2))
    y_near = dev(yy=y + 1 - 2 * lax.rem(y, 2))
    z1 = dev(zz=z + 1 - 2 * lax.rem(z, 2))
    z2 = dev(zz=z + 2 - 4 * lax.rem(z // 2, 2))
    z4 = dev(zz=lax.rem(z + 4, 8))
    sibling = dev(cc=1 - core)

    own_copies = [
        pltpu.make_async_copy(tok_in, buf.at[x, y, z, pl.ds(0, TOK)], loc_sem.at[0]),
        pltpu.make_async_copy(grad_in, buf.at[x, y, z, pl.ds(TOK, TOK)], loc_sem.at[1]),
    ]
    for j in range(2):
        ce = 2 * core + j
        own_copies.append(pltpu.make_async_copy(wg_in.at[j], wgu.at[ce, :, 0:H], loc_sem.at[2 + 3 * j]))
        own_copies.append(pltpu.make_async_copy(wu_in.at[j], wgu.at[ce, :, H : 2 * H], loc_sem.at[3 + 3 * j]))
        own_copies.append(pltpu.make_async_copy(wd_in.at[j], wd.at[ce], loc_sem.at[4 + 3 * j]))
    for c in own_copies:
        c.start()

    rt[x, y, 0:8, :] = ids_in[...].astype(F32)
    rt[x, y, 8:16, :] = gates_in[...].astype(F32)
    barrier = pltpu.get_barrier_semaphore()
    peers = (xr, xl, x_far, yr, yl, y_far, zr, zl, z2, z4, sibling)
    for p in peers:
        pl.semaphore_signal(barrier, inc=1, device_id=p, device_id_type=MESH)
    for c in own_copies[:2]:
        c.wait()
    pl.semaphore_wait(barrier, len(peers))

    net = Net(send_sem, recv_sem)

    sz = pl.ds
    ra, rb, rc = SPLIT_G
    ga, gb, gab, gc = sz(0, ra), sz(ra, rb), sz(0, ra + rb), sz(ra + rb, rc)
    hab, hc = half16(ra + rb), half16(rc)
    zs = [z] + [lax.rem(z + k + 8, 8) for k in (1, -1, 2, -2, 3, -3, 4)]
    stage = [zs[0:1], zs[1:3], zs[3:5], zs[5:7], zs[7:8]]

    xab = ring4_gather(
        net, x,
        lambda i: buf.at[i, y, z, gab],
        lambda i: buf.at[i, y, z, sz(0, hab)],
        lambda i: buf.at[i, y, z, sz(hab, ra + rb - hab)],
        xr, xl)
    yc = ring4_gather(
        net, y,
        lambda i: buf.at[x, i, z, gc],
        lambda i: buf.at[x, i, z, sz(ra + rb, hc)],
        lambda i: buf.at[x, i, z, sz(ra + rb + hc, rc - hc)],
        yr, yl)
    ya = ring4_gather(
        net, y,
        lambda i: buf.at[:, i, z, ga],
        lambda i: buf.at[sz(0, 2), i, z, ga],
        lambda i: buf.at[sz(2, 2), i, z, ga],
        yr, yl)
    za = ring8_gather(
        net, z,
        lambda i: buf.at[:, :, i, ga],
        lambda i: buf.at[sz(0, 2), :, i, ga],
        lambda i: buf.at[sz(2, 2), :, i, ga],
        zr, zl)
    zb = ring8_gather(
        net, z,
        lambda i: buf.at[:, y, i, gb],
        lambda i: buf.at[sz(0, 2), y, i, gb],
        lambda i: buf.at[sz(2, 2), y, i, gb],
        zr, zl)
    zc = ring8_gather(
        net, z,
        lambda i: buf.at[x, :, i, gc],
        lambda i: buf.at[x, sz(0, 2), i, gc],
        lambda i: buf.at[x, sz(2, 2), i, gc],
        zr, zl)

    def plane(zz):
        return (
            ring4_gather(
                net, x,
                lambda i: buf.at[i, :, zz, gc],
                lambda i: buf.at[i, sz(0, 2), zz, gc],
                lambda i: buf.at[i, sz(2, 2), zz, gc],
                xr, xl),
            ring4_gather(
                net, y,
                lambda i: buf.at[:, i, zz, gb],
                lambda i: buf.at[sz(0, 2), i, zz, gb],
                lambda i: buf.at[sz(2, 2), i, zz, gb],
                yr, yl),
        )

    planes = [[plane(zz) for zz in group] for group in stage]

    def step(groups):
        for pair in groups:
            run(*pair)

    def route_ring():
        c = net.send(rt.at[x, y], rt.at[x, y], y_near)
        yield
        c.wait_recv()
        yh = 2 * (y // 2)
        c = net.send(rt.at[x, sz(yh, 2)], rt.at[x, sz(yh, 2)], y_far)
        yield
        c.wait_recv()
        c = net.send(rt.at[x], rt.at[x], x_near)
        yield
        c.wait_recv()
        xh = 2 * (x // 2)
        c = net.send(rt.at[sz(xh, 2)], rt.at[sz(xh, 2)], x_far)
        yield
        c.wait_recv()
        yield

    routing = route_ring()
    run(xab, yc, routing)
    run(xab, yc, routing)
    run(xab, yc)
    run(ya, zb, zc)
    step(planes[0])
    run(routing, ya)
    for c in own_copies[2:]:
        c.wait()
    weight_copies = []
    for j in range(2):
        ce = 2 * core + j
        weight_copies.append(net.send(wgu.at[ce], wgu.at[ce], sibling))
        weight_copies.append(net.send(wd.at[ce], wd.at[ce], sibling))
    run(ya)
    run(routing)
    step(planes[0])
    run(routing)
    first_expert = 4 * (x * 4 + y)

    def route():
        for b in range(16):
            tile = rt[b // 4, b % 4]
            for e in range(E4):
                hit = tile[0:8, :] == (first_expert + e).astype(F32)
                member[e * 16 + b, :] = jnp.sum(jnp.where(hit, 1.0, 0.0), axis=0)
                gatev[e * 16 + b, :] = jnp.sum(jnp.where(hit, tile[8:16, :], 0.0), axis=0)
        tri = jnp.where(
            lax.broadcasted_iota(jnp.int32, (TOK, TOK), 0) < lax.broadcasted_iota(jnp.int32, (TOK, TOK), 1),
            1.0, 0.0).astype(BF)
        m = member[...]
        pos = jnp.dot(m.astype(BF), tri, preferred_element_type=F32)
        target[...] = jnp.where(m > 0.5, pos, -1.0)

        for p in range(PAIRS):
            row = lax.broadcasted_iota(jnp.int32, (CAP, TOK), 0).astype(F32)
            zero = jnp.zeros((CAP, TOK), F32)
            parts = []
            for e in range(E4):
                r0, r1 = e * 16 + 2 * p, e * 16 + 2 * p + 1
                s0 = jnp.where(row == target[r0 : r0 + 1, :], 1.0, 0.0)
                s1 = jnp.where(row == target[r1 : r1 + 1, :], 1.0, 0.0)
                parts.append(jnp.concatenate([s0, zero], axis=1))
                parts.append(jnp.concatenate([zero, s1], axis=1))
            full = jnp.concatenate(parts, axis=0)
            sel[p] = full.astype(BF)
            selt[p] = full.T.astype(BF)

    def pick(zz):
        def body(px, _):
            for q in range(2):
                p = 2 * px + q
                s = sel[p]
                for r0, dst in ((0, xs), (TOK, gxs)):
                    t = buf[px, 2 * q : 2 * q + 2, zz, r0 : r0 + TOK, :].reshape(2 * TOK, W)
                    o = jnp.dot(s, t, preferred_element_type=F32).astype(BF)
                    for e in range(E4):
                        dst[zz, e, pl.ds(pl.multiple_of(p * 48, 16), 48), :] = o[e * 48 : (e + 1) * 48]
            return 0

        lax.fori_loop(0, PAIRS // 2, body, 0)

    def accumulate(zz, first):
        f = pl.ds(pl.multiple_of(zz * W, W), W)

        def body(e):
            gu = jnp.dot(xs[zz, e], wgu[e, f, :], preferred_element_type=F32)
            raw = lax.dot_general(gxs[zz, e], wd[e, :, f], (((1,), (1,)), ((), ())), preferred_element_type=F32)
            if first:
                agu[e] = gu
                araw[e] = raw
            else:
                agu[e] += gu
                araw[e] += raw

        for e in range(E4):
            body(e)

    def consume(group, first=False):
        if COMPUTE:
            for zz in group:
                pick(zz)
                accumulate(zz, first)

    def forward(e):
        gu, raw = agu[e], araw[e]
        gate_pre, up_pre = gu[:, :H], gu[:, H:]
        sig = 1.0 / (1.0 + jnp.exp(-gate_pre))
        swish = gate_pre * sig
        hidden = swish * up_pre
        gp[e] = jnp.broadcast_to(jnp.sum(hidden * raw, axis=1, keepdims=True), (ROWS, H))
        cols = []
        for p in range(PAIRS):
            for k in range(2):
                s = sel[p, pl.ds(pl.multiple_of(e * 48, 16), 48), k * TOK : (k + 1) * TOK].astype(F32)
                g = gatev[pl.ds(e * 16 + 2 * p + k, 1), :]
                cols.append(jnp.sum((s * g)[k * CAP : (k + 1) * CAP], axis=1, keepdims=True))
        gate = jnp.concatenate(cols, axis=0)
        hg = gate * raw
        pgu[e, :, H:] = (hg * swish).astype(BF)
        pgu[e, :, :H] = (hg * up_pre * sig * (1.0 + gate_pre * (1.0 - sig))).astype(BF)
        sh[e] = (gate * hidden).astype(BF)

    def produce(zz):
        f = pl.ds(pl.multiple_of(zz * W, W), W)

        def products(e):
            o = lax.dot_general(pgu[e], wgu[e, f, :], (((1,), (1,)), ((), ())),
                                preferred_element_type=F32).astype(BF)
            for p in range(PAIRS):
                part[p, e * 48 : (e + 1) * 48, :] = o[p * 48 : (p + 1) * 48]

        def spread(p, _):
            for q in range(4):
                o = jnp.dot(selt[4 * p + q], part[4 * p + q], preferred_element_type=F32).astype(BF)
                buf[2 * p + q // 2, 2 * (q % 2) : 2 * (q % 2) + 2, zz, 0:TOK, :] = o.reshape(2, TOK, W)
            return 0

        if COMPUTE:
            for e in range(E4):
                products(e)
            lax.fori_loop(0, PAIRS // 4, spread, 0)

    def gate_terms(p):
        for k in range(2):
            rows = []
            px, py = p // 2, 2 * (p % 2) + k
            tile = rt[px, py][0:8, :]
            acc = jnp.zeros((8, TOK), F32)
            for e in range(E4):
                s = sel[p, e * 48 : (e + 1) * 48, k * TOK : (k + 1) * TOK].astype(F32)
                v = jnp.sum(s * gp[e, pl.ds(pl.multiple_of(p * 48, 16), 48), :], axis=0, keepdims=True)
                acc = acc + jnp.where(tile == (first_expert + e).astype(F32), v, 0.0)
            ggd[px, py] = acc

    def loop(n, f):
        def body(i, _):
            f(i)
            return 0

        lax.fori_loop(0, n, body, 0)

    if COMPUTE:
        route()
    for c in weight_copies:
        c.wait_recv()
    for k in range(1, 5):
        run(zb, zc)
        step(planes[k])
        step(planes[k - 1])
        run(za)
        consume(stage[k - 1], k == 1)
        step(planes[k])
    step(planes[4])
    run(za)
    consume(stage[4])
    net.drain()
    if COMPUTE:
        loop(E4, forward)

    ra, rb, rc = SPLIT_R
    sa, sb, sc = sz(0, ra), sz(ra, rb), sz(ra + rb, rc)
    ha, hb, hc = half16(ra), half16(rb), half16(rc)

    def rplane(k, zz):
        return (
            ring_scatter(
                net, 4, x,
                lambda i: buf.at[i, :, zz, sc],
                lambda i: buf.at[i, sz(0, 2), zz, sc],
                lambda i: buf.at[i, sz(2, 2), zz, sc],
                slots[2 * k], xr, xl),
            ring_scatter(
                net, 4, y,
                lambda i: buf.at[:, i, zz, sb],
                lambda i: buf.at[sz(0, 2), i, zz, sb],
                lambda i: buf.at[sz(2, 2), i, zz, sb],
                slots[2 * k + 1], yr, yl),
        )

    back = [rplane(k, zz) for k, zz in enumerate(zs)]
    back = [back[0:1], back[1:3], back[3:5], back[5:7], back[7:8]]
    slots = slots[16:]
    sza = ring_scatter(
        net, 8, z,
        lambda i: buf.at[:, :, i, sa],
        lambda i: buf.at[sz(0, 2), :, i, sa],
        lambda i: buf.at[sz(2, 2), :, i, sa],
        slots[0], zr, zl)
    szb = ring_scatter(
        net, 8, z,
        lambda i: buf.at[:, y, i, sb],
        lambda i: buf.at[sz(0, 2), y, i, sb],
        lambda i: buf.at[sz(2, 2), y, i, sb],
        slots[1], zr, zl)
    szc = ring_scatter(
        net, 8, z,
        lambda i: buf.at[x, :, i, sc],
        lambda i: buf.at[x, sz(0, 2), i, sc],
        lambda i: buf.at[x, sz(2, 2), i, sc],
        slots[2], zr, zl)
    sya = ring_scatter(
        net, 4, y,
        lambda i: buf.at[:, i, z, sa],
        lambda i: buf.at[sz(0, 2), i, z, sa],
        lambda i: buf.at[sz(2, 2), i, z, sa],
        slots[3], yr, yl)
    sxa = ring_scatter(
        net, 4, x,
        lambda i: buf.at[i, y, z, sa],
        lambda i: buf.at[i, y, z, sz(0, ha)],
        lambda i: buf.at[i, y, z, sz(ha, ra - ha)],
        slots[4], xr, xl)
    sxb = ring_scatter(
        net, 4, x,
        lambda i: buf.at[i, y, z, sb],
        lambda i: buf.at[i, y, z, sz(ra, hb)],
        lambda i: buf.at[i, y, z, sz(ra + hb, rb - hb)],
        slots[5], xr, xl)
    syc = ring_scatter(
        net, 4, y,
        lambda i: buf.at[x, i, z, sc],
        lambda i: buf.at[x, i, z, sz(ra + rb, hc)],
        lambda i: buf.at[x, i, z, sz(ra + rb + hc, rc - hc)],
        slots[6], yr, yl)

    def gate_ring():
        xo = 2 - 2 * (x // 2)
        c = net.send(ggd.at[sz(xo, 2)], gg_rx.at[sz(0, 2)], x_far)
        yield
        c.wait_recv()
        xm = 2 * (x // 2)
        for k in range(2):
            for j in range(4):
                ggd[xm + k, j] = ggd[xm + k, j] + gg_rx[k, j]
        xn = x + 1 - 2 * lax.rem(x, 2)
        c = net.send(ggd.at[xn], gg_rx.at[2], x_near)
        yield
        c.wait_recv()
        for j in range(4):
            ggd[x, j] = ggd[x, j] + gg_rx[2, j]
        yo = 2 - 2 * (y // 2)
        c = net.send(ggd.at[x, sz(yo, 2)], gg_rx.at[3, sz(0, 2)], y_far)
        yield
        c.wait_recv()
        ym = 2 * (y // 2)
        for k in range(2):
            ggd[x, ym + k] = ggd[x, ym + k] + gg_rx[3, k]
        yn = y + 1 - 2 * lax.rem(y, 2)
        c = net.send(ggd.at[x, yn], gg_rx.at[3, 2], y_near)
        yield
        c.wait_recv()
        gg_rz[0] = ggd[x, y] + gg_rx[3, 2]
        for k, d in enumerate((z1, z2, z4)):
            c = net.send(gg_rz.at[2 * k], gg_rz.at[2 * k + 1], d)
            yield
            c.wait_recv()
            gg_rz[2 * k + 2] = gg_rz[2 * k] + gg_rz[2 * k + 1]
        yield

    def launch(k):
        for zz in stage[k]:
            produce(zz)
        step(back[k])

    tn = (((0,), (0,)), ((), ()))

    def other_grads(j):
        e = 2 * (1 - core) + j

        def body(h, _):
            for q in range(2):
                m = 2 * h + q
                f = pl.ds(pl.multiple_of(m * W, W), W)
                osg[j, f, :] = lax.dot_general(xs[m, e], pgu[e], tn, preferred_element_type=F32).astype(BF)
                osd[j, :, f] = lax.dot_general(sh[e], gxs[m, e], tn, preferred_element_type=F32).astype(BF)
            return 0

        if COMPUTE:
            lax.fori_loop(0, NZ // 2, body, 0)
        return [net.send(osg.at[j], org.at[j], sibling), net.send(osd.at[j], ord_.at[j], sibling)]

    def own_grads(lo, hi):
        def outs(j, m, slot):
            f = pl.ds(pl.multiple_of(m * W, W), W)
            return [
                pltpu.make_async_copy(stg.at[slot], dgu_out.at[j, f, :], stg_sem.at[slot, 0]),
                pltpu.make_async_copy(std.at[slot], dd_out.at[j, :, f], stg_sem.at[slot, 1]),
            ]

        def body(t, _):
            for slot in range(2):
                j, m = t // (NZ // 2), 2 * (t % (NZ // 2)) + slot
                e = 2 * core + j
                f = pl.ds(pl.multiple_of(m * W, W), W)

                @pl.when(t >= 1)
                def _():
                    for c in outs(j, m, slot):
                        c.wait()

                a = lax.dot_general(xs[m, e], pgu[e], tn, preferred_element_type=F32)
                stg[slot] = (a + org[j, f, :].astype(F32)).astype(BF)
                b = lax.dot_general(sh[e], gxs[m, e], tn, preferred_element_type=F32)
                std[slot] = (b + ord_[j, :, f].astype(F32)).astype(BF)
                for c in outs(j, m, slot):
                    c.start()
            return 0

        if COMPUTE:
            lax.fori_loop(lo, hi, body, 0)
            if hi == NZ:
                for slot in range(2):
                    for c in outs(0, 0, slot):
                        c.wait()

    ring = gate_ring()
    launch(4)
    run(sza)
    launch(3)
    step(back[4])
    run(sza)
    launch(2)
    step(back[4])
    run(szb, szc)
    step(back[3])
    if COMPUTE:
        loop(PAIRS, gate_terms)
    run(ring)
    launch(1)
    step(back[3])
    run(szb, szc, sza)
    step(back[2])
    run(ring)
    launch(0)
    grad_copies = other_grads(0)
    step(back[2])
    run(szb, szc, sza)
    step(back[1])
    run(ring)
    grad_copies += other_grads(1)
    run(ring)
    step(back[1])
    run(szb, szc, sza)
    run(sya)
    step(back[0])
    run(ring)
    step(back[0])
    for c in grad_copies:
        c.wait_recv()
    own_grads(0, 3)
    run(szb, szc)
    run(sxb, syc)
    run(sya, ring)
    own_grads(3, 5)
    run(sya)
    run(sxa, sxb, syc)
    own_grads(5, 7)
    run(ring, sxa, sxb, syc)
    run(ring)
    own_grads(7, 8)
    run(sxa)

    tok_out[...] = buf[x, y, z, 0:TOK, :]
    gg_out[...] = gg_rz[6]
    net.drain()


def finish_kernel(tok, gg, dgu, dd, tok_out, gg_out, dg_out, du_out, dd_out):
    tok_out[...] = tok[...]
    gg_out[...] = gg[...]
    dg_out[...] = dgu[:, :, :H].astype(F32)
    du_out[...] = dgu[:, :, H:].astype(F32)
    dd_out[...] = dd[...].astype(F32)


def finish(tok, gg, dgu, dd):
    steps = 4
    n = D // steps
    whole = lambda i: (0, 0)
    rows = lambda i: (0, i, 0)
    cols = lambda i: (0, 0, i)
    return pl.pallas_call(
        finish_kernel,
        grid=(steps,),
        in_specs=[
            pl.BlockSpec((TOK, W), whole),
            pl.BlockSpec((8, TOK), whole),
            pl.BlockSpec((2, n, 2 * H), rows),
            pl.BlockSpec((2, H, n), cols),
        ],
        out_specs=[
            pl.BlockSpec((TOK, W), whole),
            pl.BlockSpec((8, TOK), whole),
            pl.BlockSpec((2, n, H), rows),
            pl.BlockSpec((2, n, H), rows),
            pl.BlockSpec((2, H, n), cols),
        ],
        out_shape=(
            jax.ShapeDtypeStruct((TOK, W), BF),
            jax.ShapeDtypeStruct((8, TOK), F32),
            jax.ShapeDtypeStruct((2, D, H), F32),
            jax.ShapeDtypeStruct((2, D, H), F32),
            jax.ShapeDtypeStruct((2, H, D), F32),
        ),
        compiler_params=pltpu.CompilerParams(vmem_limit_bytes=62 * 1024 * 1024),
    )(tok, gg, dgu, dd)


def local(tokens, grad_output, gates, ids, gate_weight, up_weight, down_weight):
    any_spec = pl.BlockSpec(memory_space=pl.ANY)
    vmem = pl.BlockSpec(memory_space=pltpu.VMEM)
    scratch = [
        pltpu.VMEM((NX, NY, NZ, 2 * TOK, W), BF),
        pltpu.VMEM((NZ, E4, ROWS, W), BF),
        pltpu.VMEM((NZ, E4, ROWS, W), BF),
        pltpu.VMEM((E4, D, 2 * H), BF),
        pltpu.VMEM((E4, H, D), BF),
        pltpu.VMEM((PAIRS, 192, 2 * TOK), BF),
        pltpu.VMEM((PAIRS, 2 * TOK, 192), BF),
        pltpu.VMEM((PAIRS, 192, W), BF),
        pltpu.VMEM((E4, ROWS, 2 * H), F32),
        pltpu.VMEM((E4, ROWS, H), F32),
        pltpu.VMEM((E4, ROWS, 2 * H), BF),
        pltpu.VMEM((E4, ROWS, H), BF),
        pltpu.VMEM((E4, ROWS, H), F32),
        pltpu.VMEM((64, TOK), F32),
        pltpu.VMEM((64, TOK), F32),
        pltpu.VMEM((64, TOK), F32),
        pltpu.VMEM((NX, NY, 16, TOK), F32),
        pltpu.VMEM((NX, NY, 8, TOK), F32),
        pltpu.VMEM((4, 4, 8, TOK), F32),
        pltpu.VMEM((7, 8, TOK), F32),
        pltpu.VMEM((2, D, 2 * H), BF),
        pltpu.VMEM((2, H, D), BF),
        pltpu.VMEM((2, D, 2 * H), BF),
        pltpu.VMEM((2, H, D), BF),
        pltpu.VMEM((2, W, 2 * H), BF),
        pltpu.VMEM((2, H, W), BF),
    ]
    for ring in scatter_slots():
        for pair in ring:
            for shape in pair:
                scratch.append(pltpu.VMEM(shape, BF))
    scratch += [
        pltpu.SemaphoreType.DMA((N_SEM,)),
        pltpu.SemaphoreType.DMA((N_SEM,)),
        pltpu.SemaphoreType.DMA((N_LOC,)),
        pltpu.SemaphoreType.DMA((2, 2)),
    ]
    outs = pl.pallas_call(
        kernel,
        out_shape=(
            jax.ShapeDtypeStruct((TOK, W), BF),
            jax.ShapeDtypeStruct((8, TOK), F32),
            jax.ShapeDtypeStruct((2, D, 2 * H), BF),
            jax.ShapeDtypeStruct((2, H, D), BF),
        ),
        in_specs=[any_spec, any_spec, vmem, vmem, any_spec, any_spec, any_spec],
        out_specs=(vmem, vmem, any_spec, any_spec),
        scratch_shapes=scratch,
        compiler_params=pltpu.CompilerParams(
            collective_id=0, has_side_effects=True, vmem_limit_bytes=63 * 1024 * 1024
        ),
    )(tokens, grad_output, ids.T, gates.T, gate_weight, up_weight, down_weight)
    grad_tokens, gate_grads, grad_gate, grad_up, grad_down = finish(*outs)
    return (grad_tokens, gate_grads.T, grad_gate, grad_up, grad_down)


def solution(mesh):
    return jax.shard_map(
        local,
        mesh=mesh,
        in_specs=(
            P("expert", "etp"),
            P("expert", "etp"),
            P("expert", None),
            P("expert", None),
            P("expert", None, "etp"),
            P("expert", None, "etp"),
            P("expert", "etp", None),
        ),
        out_specs=(
            P("expert", "etp"),
            P("expert", None),
            P("expert", None, "etp"),
            P("expert", None, "etp"),
            P("expert", "etp", None),
        ),
        check_vma=False,
    )
```

```python
import functools

import jax
import jax.numpy as jnp
from jax import lax
from jax.experimental import pallas as pl
from jax.experimental.pallas import tpu as pltpu
from jax.sharding import PartitionSpec as P

MESH = pl.DeviceIdType.MESH
BF = jnp.bfloat16
F32 = jnp.float32
NX, NY, NZ = 4, 4, 8
TOK = 128
W = 256
D = 2048
H = 128
TOP = 8
CAP = 24
E4 = 4
PAIRS = 8
ROWS = 2 * CAP * PAIRS
SPLIT_G = (48, 96, 112)
SPLIT_R = (32, 48, 48)

GATHER = (
    "xab", "yc", "zb0", "zc0", "wl", "rt", "zb0", "yc", "xab", "zb1", "zb2", "zc1", "zc2", "rt", "zc0", "-16", "wl",
    "yc", "zc3", "zb0", "xab", "zb3", "ya", "px0", "py0", "rt", "-7", "zb1", "zb2", "zc1", "-5", "zc2", "ya", "zc0",
    "-4", "zc3", "px1", "px2", "-8", "px0", "zb0", "rt", "-5", "py0", "zb3", "py1", "py2", "ya", "za", "zb1", "zb2",
    "-4", "zc1", "-4", "py0", "zc2", "px1", "-6", "zc0", "zc3", "px3", "px4", "zb0", "py1", "zb3", "py3", "py4",
    "px2", "px0", "py2", "-15", "rt", "route", "pick0", "py1", "acc0", "px1", "-4", "za", "pick1", "zb1", "acc1",
    "zb2", "py3", "-8", "zc1", "px3", "zc2", "-6", "zc0", "py4", "zc3", "px5", "px6", "zb3", "py5", "py6", "-8",
    "py2", "px4", "py3", "-6", "px2", "pick2", "py4", "acc2", "px3", "za", "pick3", "zb1", "zb2", "py5", "zc1",
    "acc3", "zc2", "-8", "zc3", "px5", "px7", "zb3", "py7", "-12", "py6", "py5", "-8", "px6", "px4", "pick4", "py7",
    "acc4", "za", "px5", "pick5", "py6", "acc5", "-8", "py7", "-6", "px7", "za", "-6", "px6", "pick6", "acc6",
    "px7", "pick7", "acc7",
)
SCATTER = (
    "make7", "sza", "rx7", "ry7", "make6", "rx6", "ry6", "make5", "rx7", "rx5", "ry7", "ry5", "make4", "sza", "rx6",
    "rx4", "ry6", "ry4", "make3", "rx7", "szc", "rx3", "ry7", "szb", "ry3", "make2", "rx5", "rx2", "ry5", "ry2",
    "rx6", "make1", "rx4", "rx1", "rx3", "ry6", "ry4", "ry3", "sza", "ry1", "make0", "rx5", "szc", "rx0", "ry5",
    "szb", "rx2", "ry2", "ry0", "gt", "rx4", "rx1", "ry4", "gr", "og0", "sza", "rx3", "rx0", "ry3", "ry1", "og1",
    "szc", "szb", "rx2", "ry2", "ry0", "-8", "rx1", "-16", "gr", "ry1", "-48", "wg0", "rx0", "gr", "wg1", "ry0",
    "wg2", "sza", "sya", "wg3", "wg4", "gr", "wg5", "szc", "wg6", "sya", "wg7", "gr", "szb", "-23", "gr", "szc",
    "sya", "syc", "sxa", "-6", "szb", "sxb", "gr", "-5", "sxa", "syc", "gr", "sxb", "-7", "sxa", "syc", "sxb",
)


class Net:
    def __init__(self, send, recv):
        self.send_sem, self.recv_sem = send, recv
        self.count = 0
        self.pending = []

    def send(self, src, dst, device):
        k = self.count
        self.count += 1
        copy = pltpu.make_async_remote_copy(
            src_ref=src,
            dst_ref=dst,
            send_sem=self.send_sem.at[k],
            recv_sem=self.recv_sem.at[k],
            device_id=device,
            device_id_type=MESH,
        )
        copy.start()
        self.pending.append(copy)
        return copy

    def drain(self, n=None):
        n = len(self.pending) if n is None else n
        for copy in self.pending[:n]:
            copy.wait_send()
        self.pending = self.pending[n:]


def half16(n):
    return (n // 2 + 15) // 16 * 16


def ring4_gather(net, i, full, h0, h1, right, left):
    a = net.send(full(i), full(i), right)
    b = net.send(full(i), full(i), left)
    yield a, b
    prev, following = lax.rem(i + 3, 4), lax.rem(i + 1, 4)
    a.wait_recv()
    c = net.send(h0(prev), h0(prev), right)
    b.wait_recv()
    d = net.send(h1(following), h1(following), left)
    yield c, d
    c.wait_recv()
    d.wait_recv()
    yield ()


def ring8_gather(net, i, full, h0, h1, right, left):
    a = net.send(full(i), full(i), right)
    b = net.send(full(i), full(i), left)
    yield a, b
    for step in (1, 2, 3):
        prev, following = lax.rem(i + 8 - step, 8), lax.rem(i + step, 8)
        va, vb = (full, full) if step < 3 else (h0, h1)
        a.wait_recv()
        a = net.send(va(prev), va(prev), right)
        b.wait_recv()
        b = net.send(vb(following), vb(following), left)
        yield a, b
    a.wait_recv()
    b.wait_recv()
    yield ()


def add_into(dst, src):
    dst[...] = (dst[...].astype(F32) + src[...].astype(F32)).astype(BF)


def ring_scatter(net, n, i, full, h0, h1, slots, right, left):
    far = lax.rem(i + n // 2, n)
    ra, rb = slots[0]
    a = net.send(h0(far), ra, right)
    b = net.send(h1(far), rb, left)
    yield a, b
    for step in range(1, n // 2):
        to_r, to_l = lax.rem(i + n // 2 - step, n), lax.rem(i + n // 2 + step, n)
        va, vb = (h0, h1) if step == 1 else (full, full)
        a.wait_recv()
        add_into(va(to_r), ra)
        ra, rb_next = slots[step]
        a = net.send(full(to_r), ra, right)
        b.wait_recv()
        add_into(vb(to_l), rb)
        rb = rb_next
        b = net.send(full(to_l), rb, left)
        yield a, b
    a.wait_recv()
    b.wait_recv()
    dst = full(i)
    dst[...] = (dst[...].astype(F32) + ra[...].astype(F32) + rb[...].astype(F32)).astype(BF)
    yield ()


def scatter_slots():
    ra, rb, rc = SPLIT_R
    h = half16
    out = []

    def ring(n, half0, half1, whole):
        out.append([(half0, half1)] + [(whole, whole)] * (n // 2 - 1))

    for _ in range(NZ):
        ring(4, (2, rc, W), (2, rc, W), (4, rc, W))
        ring(4, (2, rb, W), (2, rb, W), (4, rb, W))
    ring(8, (2, 4, ra, W), (2, 4, ra, W), (4, 4, ra, W))
    ring(8, (2, rb, W), (2, rb, W), (4, rb, W))
    ring(8, (2, rc, W), (2, rc, W), (4, rc, W))
    ring(4, (2, ra, W), (2, ra, W), (4, ra, W))
    ring(4, (h(ra), W), (ra - h(ra), W), (ra, W))
    ring(4, (h(rb), W), (rb - h(rb), W), (rb, W))
    ring(4, (h(rc), W), (rc - h(rc), W), (rc, W))
    return out


N_SEM = 320
N_LOC = 32


def kernel(*refs):
    it = iter(refs)
    take = lambda n: [next(it) for _ in range(n)]
    tok_in, grad_in, ids_in, gates_in, wg_in, wu_in, wd_in = take(7)
    tok_out, gg_out, dgu_out, dd_out = take(4)
    buf, xs, gxs, wgu, wd, sel, selt, part = take(8)
    agu, araw, pgu, sh, gp, member, target, gatev = take(8)
    rt, ggd, gg_rx, gg_rz = take(4)
    osg, osd, org, ord_ = take(4)
    stg, std = take(2)
    slots = [[tuple(take(2)) for _ in ring] for ring in scatter_slots()]
    send_sem, recv_sem, loc_sem, stg_sem = take(4)

    e_idx = lax.axis_index("expert")
    z = lax.axis_index("etp")
    core = lax.rem(e_idx, 2)
    y = lax.rem(e_idx // 2, 4)
    x = e_idx // 8

    def dev(dx=0, dy=0, xx=None, yy=None, cc=None, zz=None):
        px = lax.rem(x + dx + 4, 4) if xx is None else xx
        py = lax.rem(y + dy + 4, 4) if yy is None else yy
        pc = core if cc is None else cc
        return ((px * 4 + py) * 2 + pc, z if zz is None else zz)

    xr, xl = dev(dx=1), dev(dx=-1)
    yr, yl = dev(dy=1), dev(dy=-1)
    zr, zl = dev(zz=lax.rem(z + 1, 8)), dev(zz=lax.rem(z + 7, 8))
    x_far, y_far = dev(dx=2), dev(dy=2)
    x_near = dev(xx=x + 1 - 2 * lax.rem(x, 2))
    y_near = dev(yy=y + 1 - 2 * lax.rem(y, 2))
    z1 = dev(zz=z + 1 - 2 * lax.rem(z, 2))
    z2 = dev(zz=z + 2 - 4 * lax.rem(z // 2, 2))
    z4 = dev(zz=lax.rem(z + 4, 8))
    sibling = dev(cc=1 - core)

    own_copies = [
        pltpu.make_async_copy(tok_in, buf.at[x, y, z, pl.ds(0, TOK)], loc_sem.at[0]),
        pltpu.make_async_copy(grad_in, buf.at[x, y, z, pl.ds(TOK, TOK)], loc_sem.at[1]),
    ]
    for j in range(2):
        ce = 2 * core + j
        own_copies.append(pltpu.make_async_copy(wg_in.at[j], wgu.at[ce, :, 0:H], loc_sem.at[2 + 3 * j]))
        own_copies.append(pltpu.make_async_copy(wu_in.at[j], wgu.at[ce, :, H : 2 * H], loc_sem.at[3 + 3 * j]))
        own_copies.append(pltpu.make_async_copy(wd_in.at[j], wd.at[ce], loc_sem.at[4 + 3 * j]))
    for c in own_copies:
        c.start()

    rt[x, y, 0:8, :] = ids_in[...].astype(F32)
    rt[x, y, 8:16, :] = gates_in[...].astype(F32)
    barrier = pltpu.get_barrier_semaphore()
    peers = (xr, xl, x_far, yr, yl, y_far, zr, zl, z2, z4, sibling)
    for p in peers:
        pl.semaphore_signal(barrier, inc=1, device_id=p, device_id_type=MESH)
    for c in own_copies[:2]:
        c.wait()
    pl.semaphore_wait(barrier, len(peers))

    net = Net(send_sem, recv_sem)

    sz = pl.ds
    ra, rb, rc = SPLIT_G
    ga, gb, gab, gc = sz(0, ra), sz(ra, rb), sz(0, ra + rb), sz(ra + rb, rc)
    hab, hb, hc = half16(ra + rb), half16(rb), half16(rc)
    zs = [z] + [lax.rem(z + k + 8, 8) for k in (1, -1, 2, -2, 3, -3, 4)]
    stage = [zs[0:1], zs[1:3], zs[3:5], zs[5:7], zs[7:8]]

    xab = ring4_gather(
        net, x,
        lambda i: buf.at[i, y, z, gab],
        lambda i: buf.at[i, y, z, sz(0, hab)],
        lambda i: buf.at[i, y, z, sz(hab, ra + rb - hab)],
        xr, xl)
    yc = ring4_gather(
        net, y,
        lambda i: buf.at[x, i, z, gc],
        lambda i: buf.at[x, i, z, sz(ra + rb, hc)],
        lambda i: buf.at[x, i, z, sz(ra + rb + hc, rc - hc)],
        yr, yl)
    ya = ring4_gather(
        net, y,
        lambda i: buf.at[:, i, z, ga],
        lambda i: buf.at[sz(0, 2), i, z, ga],
        lambda i: buf.at[sz(2, 2), i, z, ga],
        yr, yl)
    za = ring8_gather(
        net, z,
        lambda i: buf.at[:, :, i, ga],
        lambda i: buf.at[sz(0, 2), :, i, ga],
        lambda i: buf.at[sz(2, 2), :, i, ga],
        zr, zl)
    def column_b(px):
        return ring8_gather(
            net, z,
            lambda i: buf.at[px, y, i, gb],
            lambda i: buf.at[px, y, i, sz(ra, hb)],
            lambda i: buf.at[px, y, i, sz(ra + hb, rb - hb)],
            zr, zl)

    def column_c(py):
        return ring8_gather(
            net, z,
            lambda i: buf.at[x, py, i, gc],
            lambda i: buf.at[x, py, i, sz(ra + rb, hc)],
            lambda i: buf.at[x, py, i, sz(ra + rb + hc, rc - hc)],
            zr, zl)

    def plane(zz):
        return (
            ring4_gather(
                net, x,
                lambda i: buf.at[i, :, zz, gc],
                lambda i: buf.at[i, sz(0, 2), zz, gc],
                lambda i: buf.at[i, sz(2, 2), zz, gc],
                xr, xl),
            ring4_gather(
                net, y,
                lambda i: buf.at[:, i, zz, gb],
                lambda i: buf.at[sz(0, 2), i, zz, gb],
                lambda i: buf.at[sz(2, 2), i, zz, gb],
                yr, yl),
        )

    def route_ring():
        c = net.send(rt.at[x, y], rt.at[x, y], y_near)
        yield (c,)
        c.wait_recv()
        yh = 2 * (y // 2)
        c = net.send(rt.at[x, sz(yh, 2)], rt.at[x, sz(yh, 2)], y_far)
        yield (c,)
        c.wait_recv()
        c = net.send(rt.at[x], rt.at[x], x_near)
        yield (c,)
        c.wait_recv()
        xh = 2 * (x // 2)
        c = net.send(rt.at[sz(xh, 2)], rt.at[sz(xh, 2)], x_far)
        yield (c,)
        c.wait_recv()
        yield ()

    def load_weights():
        for c in own_copies[2:]:
            c.wait()
        copies = []
        for j in range(2):
            ce = 2 * core + j
            copies.append(net.send(wgu.at[ce], wgu.at[ce], sibling))
            copies.append(net.send(wd.at[ce], wd.at[ce], sibling))
        yield copies
        for c in copies:
            c.wait_recv()
        yield ()

    tasks = {}

    def ring_task(name, steps):
        tasks[name] = lambda: next(steps)

    ring_task("xab", xab)
    ring_task("yc", yc)
    ring_task("ya", ya)
    ring_task("za", za)
    for k, d in enumerate((0, 1, 3, 2)):
        ring_task(f"zb{k}", column_b(lax.rem(x + d, 4)))
        ring_task(f"zc{k}", column_c(lax.rem(y + d, 4)))
    for k, zz in enumerate(zs):
        gx, gy = plane(zz)
        ring_task(f"px{k}", gx)
        ring_task(f"py{k}", gy)
    ring_task("rt", route_ring())
    ring_task("wl", load_weights())
    first_expert = 4 * (x * 4 + y)

    def route():
        for b in range(16):
            tile = rt[b // 4, b % 4]
            for e in range(E4):
                hit = tile[0:8, :] == (first_expert + e).astype(F32)
                member[e * 16 + b, :] = jnp.sum(jnp.where(hit, 1.0, 0.0), axis=0)
                gatev[e * 16 + b, :] = jnp.sum(jnp.where(hit, tile[8:16, :], 0.0), axis=0)
        tri = jnp.where(
            lax.broadcasted_iota(jnp.int32, (TOK, TOK), 0) < lax.broadcasted_iota(jnp.int32, (TOK, TOK), 1),
            1.0, 0.0).astype(BF)
        m = member[...]
        pos = jnp.dot(m.astype(BF), tri, preferred_element_type=F32)
        target[...] = jnp.where(m > 0.5, pos, -1.0)

        for p in range(PAIRS):
            row = lax.broadcasted_iota(jnp.int32, (CAP, TOK), 0).astype(F32)
            zero = jnp.zeros((CAP, TOK), F32)
            parts = []
            for e in range(E4):
                r0, r1 = e * 16 + 2 * p, e * 16 + 2 * p + 1
                s0 = jnp.where(row == target[r0 : r0 + 1, :], 1.0, 0.0)
                s1 = jnp.where(row == target[r1 : r1 + 1, :], 1.0, 0.0)
                parts.append(jnp.concatenate([s0, zero], axis=1))
                parts.append(jnp.concatenate([zero, s1], axis=1))
            full = jnp.concatenate(parts, axis=0)
            sel[p] = full.astype(BF)
            selt[p] = full.T.astype(BF)

    def pick(zz):
        def body(px, _):
            for q in range(2):
                p = 2 * px + q
                s = sel[p]
                for r0, dst in ((0, xs), (TOK, gxs)):
                    t = buf[px, 2 * q : 2 * q + 2, zz, r0 : r0 + TOK, :].reshape(2 * TOK, W)
                    o = jnp.dot(s, t, preferred_element_type=F32).astype(BF)
                    for e in range(E4):
                        dst[zz, e, pl.ds(pl.multiple_of(p * 48, 16), 48), :] = o[e * 48 : (e + 1) * 48]
            return 0

        lax.fori_loop(0, PAIRS // 2, body, 0)

    def accumulate(zz, first):
        f = pl.ds(pl.multiple_of(zz * W, W), W)

        def body(e):
            gu = jnp.dot(xs[zz, e], wgu[e, f, :], preferred_element_type=F32)
            raw = lax.dot_general(gxs[zz, e], wd[e, :, f], (((1,), (1,)), ((), ())), preferred_element_type=F32)
            if first:
                agu[e] = gu
                araw[e] = raw
            else:
                agu[e] += gu
                araw[e] += raw

        for e in range(E4):
            body(e)

    def forward(e):
        gu, raw = agu[e], araw[e]
        gate_pre, up_pre = gu[:, :H], gu[:, H:]
        sig = 1.0 / (1.0 + jnp.exp(-gate_pre))
        swish = gate_pre * sig
        hidden = swish * up_pre
        gp[e] = jnp.broadcast_to(jnp.sum(hidden * raw, axis=1, keepdims=True), (ROWS, H))
        cols = []
        for p in range(PAIRS):
            for k in range(2):
                s = sel[p, pl.ds(pl.multiple_of(e * 48, 16), 48), k * TOK : (k + 1) * TOK].astype(F32)
                g = gatev[pl.ds(e * 16 + 2 * p + k, 1), :]
                cols.append(jnp.sum((s * g)[k * CAP : (k + 1) * CAP], axis=1, keepdims=True))
        gate = jnp.concatenate(cols, axis=0)
        hg = gate * raw
        pgu[e, :, H:] = (hg * swish).astype(BF)
        pgu[e, :, :H] = (hg * up_pre * sig * (1.0 + gate_pre * (1.0 - sig))).astype(BF)
        sh[e] = (gate * hidden).astype(BF)

    def produce(zz):
        f = pl.ds(pl.multiple_of(zz * W, W), W)

        def products(e):
            o = lax.dot_general(pgu[e], wgu[e, f, :], (((1,), (1,)), ((), ())),
                                preferred_element_type=F32).astype(BF)
            for p in range(PAIRS):
                part[p, e * 48 : (e + 1) * 48, :] = o[p * 48 : (p + 1) * 48]

        def spread(p, _):
            for q in range(4):
                o = jnp.dot(selt[4 * p + q], part[4 * p + q], preferred_element_type=F32).astype(BF)
                buf[2 * p + q // 2, 2 * (q % 2) : 2 * (q % 2) + 2, zz, 0:TOK, :] = o.reshape(2, TOK, W)
            return 0

        for e in range(E4):
            products(e)
        lax.fori_loop(0, PAIRS // 4, spread, 0)

    def gate_terms(p):
        for k in range(2):
            rows = []
            px, py = p // 2, 2 * (p % 2) + k
            tile = rt[px, py][0:8, :]
            acc = jnp.zeros((8, TOK), F32)
            for e in range(E4):
                s = sel[p, e * 48 : (e + 1) * 48, k * TOK : (k + 1) * TOK].astype(F32)
                v = jnp.sum(s * gp[e, pl.ds(pl.multiple_of(p * 48, 16), 48), :], axis=0, keepdims=True)
                acc = acc + jnp.where(tile == (first_expert + e).astype(F32), v, 0.0)
            ggd[px, py] = acc

    def loop(n, f):
        def body(i, _):
            f(i)
            return 0

        lax.fori_loop(0, n, body, 0)

    def do(order):
        for name in order:
            if name[0] == "-":
                net.drain(int(name[1:]))
            else:
                tasks[name]()

    tasks["route"] = route
    for k, zz in enumerate(zs):
        tasks[f"pick{k}"] = functools.partial(pick, zz)
        tasks[f"acc{k}"] = functools.partial(accumulate, zz, k == 0)
    do(GATHER)
    net.drain()
    loop(E4, forward)

    ra, rb, rc = SPLIT_R
    sa, sb, sc = sz(0, ra), sz(ra, rb), sz(ra + rb, rc)
    ha, hb, hc = half16(ra), half16(rb), half16(rc)

    def rplane(k, zz):
        return (
            ring_scatter(
                net, 4, x,
                lambda i: buf.at[i, :, zz, sc],
                lambda i: buf.at[i, sz(0, 2), zz, sc],
                lambda i: buf.at[i, sz(2, 2), zz, sc],
                slots[2 * k], xr, xl),
            ring_scatter(
                net, 4, y,
                lambda i: buf.at[:, i, zz, sb],
                lambda i: buf.at[sz(0, 2), i, zz, sb],
                lambda i: buf.at[sz(2, 2), i, zz, sb],
                slots[2 * k + 1], yr, yl),
        )

    for k, zz in enumerate(zs):
        gx, gy = rplane(k, zz)
        ring_task(f"rx{k}", gx)
        ring_task(f"ry{k}", gy)
        tasks[f"make{k}"] = functools.partial(produce, zz)
    slots = slots[16:]
    sza = ring_scatter(
        net, 8, z,
        lambda i: buf.at[:, :, i, sa],
        lambda i: buf.at[sz(0, 2), :, i, sa],
        lambda i: buf.at[sz(2, 2), :, i, sa],
        slots[0], zr, zl)
    szb = ring_scatter(
        net, 8, z,
        lambda i: buf.at[:, y, i, sb],
        lambda i: buf.at[sz(0, 2), y, i, sb],
        lambda i: buf.at[sz(2, 2), y, i, sb],
        slots[1], zr, zl)
    szc = ring_scatter(
        net, 8, z,
        lambda i: buf.at[x, :, i, sc],
        lambda i: buf.at[x, sz(0, 2), i, sc],
        lambda i: buf.at[x, sz(2, 2), i, sc],
        slots[2], zr, zl)
    sya = ring_scatter(
        net, 4, y,
        lambda i: buf.at[:, i, z, sa],
        lambda i: buf.at[sz(0, 2), i, z, sa],
        lambda i: buf.at[sz(2, 2), i, z, sa],
        slots[3], yr, yl)
    sxa = ring_scatter(
        net, 4, x,
        lambda i: buf.at[i, y, z, sa],
        lambda i: buf.at[i, y, z, sz(0, ha)],
        lambda i: buf.at[i, y, z, sz(ha, ra - ha)],
        slots[4], xr, xl)
    sxb = ring_scatter(
        net, 4, x,
        lambda i: buf.at[i, y, z, sb],
        lambda i: buf.at[i, y, z, sz(ra, hb)],
        lambda i: buf.at[i, y, z, sz(ra + hb, rb - hb)],
        slots[5], xr, xl)
    syc = ring_scatter(
        net, 4, y,
        lambda i: buf.at[x, i, z, sc],
        lambda i: buf.at[x, i, z, sz(ra + rb, hc)],
        lambda i: buf.at[x, i, z, sz(ra + rb + hc, rc - hc)],
        slots[6], yr, yl)

    def gate_ring():
        xo = 2 - 2 * (x // 2)
        c = net.send(ggd.at[sz(xo, 2)], gg_rx.at[sz(0, 2)], x_far)
        yield (c,)
        c.wait_recv()
        xm = 2 * (x // 2)
        for k in range(2):
            for j in range(4):
                ggd[xm + k, j] = ggd[xm + k, j] + gg_rx[k, j]
        xn = x + 1 - 2 * lax.rem(x, 2)
        c = net.send(ggd.at[xn], gg_rx.at[2], x_near)
        yield (c,)
        c.wait_recv()
        for j in range(4):
            ggd[x, j] = ggd[x, j] + gg_rx[2, j]
        yo = 2 - 2 * (y // 2)
        c = net.send(ggd.at[x, sz(yo, 2)], gg_rx.at[3, sz(0, 2)], y_far)
        yield (c,)
        c.wait_recv()
        ym = 2 * (y // 2)
        for k in range(2):
            ggd[x, ym + k] = ggd[x, ym + k] + gg_rx[3, k]
        yn = y + 1 - 2 * lax.rem(y, 2)
        c = net.send(ggd.at[x, yn], gg_rx.at[3, 2], y_near)
        yield (c,)
        c.wait_recv()
        gg_rz[0] = ggd[x, y] + gg_rx[3, 2]
        for k, d in enumerate((z1, z2, z4)):
            c = net.send(gg_rz.at[2 * k], gg_rz.at[2 * k + 1], d)
            yield (c,)
            c.wait_recv()
            gg_rz[2 * k + 2] = gg_rz[2 * k] + gg_rz[2 * k + 1]
        yield ()

    tn = (((0,), (0,)), ((), ()))

    grad_copies = []

    def other_grads(j):
        e = 2 * (1 - core) + j

        def body(h, _):
            for q in range(2):
                m = 2 * h + q
                f = pl.ds(pl.multiple_of(m * W, W), W)
                osg[j, f, :] = lax.dot_general(xs[m, e], pgu[e], tn, preferred_element_type=F32).astype(BF)
                osd[j, :, f] = lax.dot_general(sh[e], gxs[m, e], tn, preferred_element_type=F32).astype(BF)
            return 0

        lax.fori_loop(0, NZ // 2, body, 0)
        grad_copies.extend([net.send(osg.at[j], org.at[j], sibling), net.send(osd.at[j], ord_.at[j], sibling)])

    def own_grads(lo, hi):
        def outs(j, m, slot):
            f = pl.ds(pl.multiple_of(m * W, W), W)
            return [
                pltpu.make_async_copy(stg.at[slot], dgu_out.at[j, f, :], stg_sem.at[slot, 0]),
                pltpu.make_async_copy(std.at[slot], dd_out.at[j, :, f], stg_sem.at[slot, 1]),
            ]

        def body(t, _):
            for slot in range(2):
                j, m = t // (NZ // 2), 2 * (t % (NZ // 2)) + slot
                e = 2 * core + j
                f = pl.ds(pl.multiple_of(m * W, W), W)

                @pl.when(t >= 1)
                def _():
                    for c in outs(j, m, slot):
                        c.wait()

                a = lax.dot_general(xs[m, e], pgu[e], tn, preferred_element_type=F32)
                stg[slot] = (a + org[j, f, :].astype(F32)).astype(BF)
                b = lax.dot_general(sh[e], gxs[m, e], tn, preferred_element_type=F32)
                std[slot] = (b + ord_[j, :, f].astype(F32)).astype(BF)
                for c in outs(j, m, slot):
                    c.start()
            return 0

        if lo == 0:
            for c in grad_copies:
                c.wait_recv()
        lax.fori_loop(lo, hi, body, 0)
        if hi == NZ:
            for slot in range(2):
                for c in outs(0, 0, slot):
                    c.wait()

    for name, steps in (("sza", sza), ("szb", szb), ("szc", szc), ("sya", sya),
                        ("sxa", sxa), ("sxb", sxb), ("syc", syc), ("gr", gate_ring())):
        ring_task(name, steps)
    tasks["gt"] = lambda: loop(PAIRS, gate_terms)
    for j in range(2):
        tasks[f"og{j}"] = functools.partial(other_grads, j)
    for t in range(NZ):
        tasks[f"wg{t}"] = functools.partial(own_grads, t, t + 1)
    do(SCATTER)

    tok_out[...] = buf[x, y, z, 0:TOK, :]
    gg_out[...] = gg_rz[6]
    net.drain()


def finish_kernel(tok, gg, dgu, dd, tok_out, gg_out, dg_out, du_out, dd_out):
    tok_out[...] = tok[...]
    gg_out[...] = gg[...]
    dg_out[...] = dgu[:, :, :H].astype(F32)
    du_out[...] = dgu[:, :, H:].astype(F32)
    dd_out[...] = dd[...].astype(F32)


def finish(tok, gg, dgu, dd):
    steps = 4
    n = D // steps
    whole = lambda i: (0, 0)
    rows = lambda i: (0, i, 0)
    cols = lambda i: (0, 0, i)
    return pl.pallas_call(
        finish_kernel,
        grid=(steps,),
        in_specs=[
            pl.BlockSpec((TOK, W), whole),
            pl.BlockSpec((8, TOK), whole),
            pl.BlockSpec((2, n, 2 * H), rows),
            pl.BlockSpec((2, H, n), cols),
        ],
        out_specs=[
            pl.BlockSpec((TOK, W), whole),
            pl.BlockSpec((8, TOK), whole),
            pl.BlockSpec((2, n, H), rows),
            pl.BlockSpec((2, n, H), rows),
            pl.BlockSpec((2, H, n), cols),
        ],
        out_shape=(
            jax.ShapeDtypeStruct((TOK, W), BF),
            jax.ShapeDtypeStruct((8, TOK), F32),
            jax.ShapeDtypeStruct((2, D, H), F32),
            jax.ShapeDtypeStruct((2, D, H), F32),
            jax.ShapeDtypeStruct((2, H, D), F32),
        ),
        compiler_params=pltpu.CompilerParams(vmem_limit_bytes=62 * 1024 * 1024),
    )(tok, gg, dgu, dd)


def local(tokens, grad_output, gates, ids, gate_weight, up_weight, down_weight):
    any_spec = pl.BlockSpec(memory_space=pl.ANY)
    vmem = pl.BlockSpec(memory_space=pltpu.VMEM)
    scratch = [
        pltpu.VMEM((NX, NY, NZ, 2 * TOK, W), BF),
        pltpu.VMEM((NZ, E4, ROWS, W), BF),
        pltpu.VMEM((NZ, E4, ROWS, W), BF),
        pltpu.VMEM((E4, D, 2 * H), BF),
        pltpu.VMEM((E4, H, D), BF),
        pltpu.VMEM((PAIRS, 192, 2 * TOK), BF),
        pltpu.VMEM((PAIRS, 2 * TOK, 192), BF),
        pltpu.VMEM((PAIRS, 192, W), BF),
        pltpu.VMEM((E4, ROWS, 2 * H), F32),
        pltpu.VMEM((E4, ROWS, H), F32),
        pltpu.VMEM((E4, ROWS, 2 * H), BF),
        pltpu.VMEM((E4, ROWS, H), BF),
        pltpu.VMEM((E4, ROWS, H), F32),
        pltpu.VMEM((64, TOK), F32),
        pltpu.VMEM((64, TOK), F32),
        pltpu.VMEM((64, TOK), F32),
        pltpu.VMEM((NX, NY, 16, TOK), F32),
        pltpu.VMEM((NX, NY, 8, TOK), F32),
        pltpu.VMEM((4, 4, 8, TOK), F32),
        pltpu.VMEM((7, 8, TOK), F32),
        pltpu.VMEM((2, D, 2 * H), BF),
        pltpu.VMEM((2, H, D), BF),
        pltpu.VMEM((2, D, 2 * H), BF),
        pltpu.VMEM((2, H, D), BF),
        pltpu.VMEM((2, W, 2 * H), BF),
        pltpu.VMEM((2, H, W), BF),
    ]
    for ring in scatter_slots():
        for pair in ring:
            for shape in pair:
                scratch.append(pltpu.VMEM(shape, BF))
    scratch += [
        pltpu.SemaphoreType.DMA((N_SEM,)),
        pltpu.SemaphoreType.DMA((N_SEM,)),
        pltpu.SemaphoreType.DMA((N_LOC,)),
        pltpu.SemaphoreType.DMA((2, 2)),
    ]
    outs = pl.pallas_call(
        kernel,
        out_shape=(
            jax.ShapeDtypeStruct((TOK, W), BF),
            jax.ShapeDtypeStruct((8, TOK), F32),
            jax.ShapeDtypeStruct((2, D, 2 * H), BF),
            jax.ShapeDtypeStruct((2, H, D), BF),
        ),
        in_specs=[any_spec, any_spec, vmem, vmem, any_spec, any_spec, any_spec],
        out_specs=(vmem, vmem, any_spec, any_spec),
        scratch_shapes=scratch,
        compiler_params=pltpu.CompilerParams(
            collective_id=0, has_side_effects=True, vmem_limit_bytes=63 * 1024 * 1024
        ),
    )(tokens, grad_output, ids.T, gates.T, gate_weight, up_weight, down_weight)
    grad_tokens, gate_grads, grad_gate, grad_up, grad_down = finish(*outs)
    return (grad_tokens, gate_grads.T, grad_gate, grad_up, grad_down)


def solution(mesh):
    return jax.shard_map(
        local,
        mesh=mesh,
        in_specs=(
            P("expert", "etp"),
            P("expert", "etp"),
            P("expert", None),
            P("expert", None),
            P("expert", None, "etp"),
            P("expert", None, "etp"),
            P("expert", "etp", None),
        ),
        out_specs=(
            P("expert", "etp"),
            P("expert", None),
            P("expert", None, "etp"),
            P("expert", None, "etp"),
            P("expert", "etp", None),
        ),
        check_vma=False,
    )
```

```python
import functools

import jax
import jax.numpy as jnp
from jax import lax
from jax.experimental import pallas as pl
from jax.experimental.pallas import tpu as pltpu
from jax.sharding import PartitionSpec as P

MESH = pl.DeviceIdType.MESH
BF = jnp.bfloat16
F32 = jnp.float32
NX, NY, NZ = 4, 4, 8
TOK = 128
W = 256
D = 2048
H = 128
TOP = 8
CAP = 24
E4 = 4
PAIRS = 8
ROWS = 2 * CAP * PAIRS
SPLIT_G = (48, 96, 112)
SPLIT_R = (32, 48, 48)

GATHER = (
    "yc", "zb0", "wl", "zc0", "xab", "rt", "yc", "zb0", "zc1", "zc2", "-8", "yc", "px0", "zc3", "zc0", "xab", "zb2",
    "zb1", "wl", "rt", "xab", "zb3", "ya", "py0", "zb0", "-13", "zc1", "rt", "zc2", "zc3", "px1", "ya", "px2", "-8",
    "px0", "zc0", "rt", "zb2", "ya", "-8", "zb1", "zb3", "za", "py2", "py1", "zb0", "-8", "py0", "zc1", "-5", "px1",
    "zc2", "zc3", "px4", "px3", "zc0", "zb2", "py2", "zb1", "px2", "zb3", "py4", "py3", "-13", "px0", "py1", "rt",
    "route", "py0", "pick0", "px1", "acc0", "-6", "py2", "za", "zb0", "-8", "zc1", "px4", "py4", "-6", "zc2", "zc3",
    "px5", "px6", "zc0", "-8", "zb2", "py3", "zb1", "px3", "-8", "zb3", "py5", "py6", "py1", "pick1", "px2",
    "pick2", "py4", "acc1", "acc2", "px4", "-4", "py3", "za", "px5", "zc1", "pick4", "zc2", "py5", "zc3", "px8",
    "px7", "zb2", "acc4", "zb1", "zb3", "py8", "py7", "-16", "py6", "px6", "-14", "py5", "px3", "pick3", "acc3",
    "py8", "px5", "-6", "py7", "za", "pick5", "px8", "py6", "acc5", "py8", "-8", "px7", "py7", "-8", "px6", "pick6",
    "acc6", "px8", "za", "-6", "px7", "pick7", "acc7",
)
SCATTER = (
    "make7", "sza", "ry7", "rx7", "make6", "ry6", "rx6", "make5", "sza", "ry5", "rx5", "make4", "ry7", "ry4", "rx7",
    "rx4", "make3", "sza", "ry6", "ry5", "ry3", "rx6", "rx5", "rx3", "make2", "ry2", "rx2", "ry7", "szb", "make1",
    "ry4", "ry1", "rx7", "szc", "rx4", "rx1", "sza", "make0", "ry6", "ry0", "rx6", "rx0", "gt", "ry5", "szb", "ry3",
    "ry2", "gr", "rx5", "szc", "rx3", "rx2", "og0", "sza", "ry4", "ry1", "ry0", "gr", "rx4", "rx1", "ry3", "szb",
    "rx0", "og1", "ry2", "gr", "rx3", "szc", "ry1", "rx2", "-16", "rx1", "-8", "ry0", "-8", "gr", "-8", "sza",
    "sya", "rx0", "wg0", "wg1", "wg2", "szb", "gr", "wg3", "wg4", "szc", "wg5", "wg6", "sya", "sxa", "wg7", "gr",
    "szb", "sxb", "-32", "sxa", "szc", "syc", "gr", "-16", "sxb", "-24", "gr", "syc",
)


class Net:
    def __init__(self, send, recv):
        self.send_sem, self.recv_sem = send, recv
        self.count = 0
        self.pending = []

    def send(self, src, dst, device):
        k = self.count
        self.count += 1
        copy = pltpu.make_async_remote_copy(
            src_ref=src,
            dst_ref=dst,
            send_sem=self.send_sem.at[k],
            recv_sem=self.recv_sem.at[k],
            device_id=device,
            device_id_type=MESH,
        )
        copy.start()
        self.pending.append(copy)
        return copy

    def drain(self, n=None):
        n = len(self.pending) if n is None else n
        for copy in self.pending[:n]:
            copy.wait_send()
        self.pending = self.pending[n:]


def half16(n):
    return (n // 2 + 15) // 16 * 16


def ring4_gather(net, i, full, h0, h1, right, left):
    a = net.send(full(i), full(i), right)
    b = net.send(full(i), full(i), left)
    yield a, b
    prev, following = lax.rem(i + 3, 4), lax.rem(i + 1, 4)
    a.wait_recv()
    c = net.send(h0(prev), h0(prev), right)
    b.wait_recv()
    d = net.send(h1(following), h1(following), left)
    yield c, d
    c.wait_recv()
    d.wait_recv()
    yield ()


def direct_gather(net, i, full, right, left, far):
    a = net.send(full(i), full(i), right)
    b = net.send(full(i), full(i), left)
    c = net.send(full(i), full(i), far)
    yield a, b
    a.wait_recv()
    b.wait_recv()
    yield (c,)
    c.wait_recv()
    yield ()


def direct_scatter(net, i, full, slots, right, left, far):
    prev, following, other = lax.rem(i + 3, 4), lax.rem(i + 1, 4), lax.rem(i + 2, 4)
    a = net.send(full(other), slots[0][0], far)
    b = net.send(full(following), slots[0][1], right)
    c = net.send(full(prev), slots[1][0], left)
    yield a, b, c
    total = full(i)[...].astype(F32)
    for copy, slot in ((b, slots[0][1]), (c, slots[1][0]), (a, slots[0][0])):
        copy.wait_recv()
        total = total + slot[...].astype(F32)
    full(i)[...] = total.astype(BF)
    yield ()


def ring8_gather(net, i, full, h0, h1, right, left):
    a = net.send(full(i), full(i), right)
    b = net.send(full(i), full(i), left)
    yield a, b
    for step in (1, 2, 3):
        prev, following = lax.rem(i + 8 - step, 8), lax.rem(i + step, 8)
        va, vb = (full, full) if step < 3 else (h0, h1)
        a.wait_recv()
        a = net.send(va(prev), va(prev), right)
        b.wait_recv()
        b = net.send(vb(following), vb(following), left)
        yield a, b
    a.wait_recv()
    b.wait_recv()
    yield ()


def add_into(dst, src):
    dst[...] = (dst[...].astype(F32) + src[...].astype(F32)).astype(BF)


def ring_scatter(net, n, i, full, h0, h1, slots, right, left, early=False):
    far = lax.rem(i + n // 2, n)
    ra, rb = slots[0]
    a = net.send(h0(far), ra, right)
    b = net.send(h1(far), rb, left)
    yield () if early else (a, b)
    if early:
        to_r, to_l = lax.rem(far + n - 1, n), lax.rem(far + 1, n)
        na, nb = slots[1]
        a1 = net.send(h1(to_r), na.at[pl.ds(2, 2)], right)
        b1 = net.send(h0(to_l), nb.at[pl.ds(0, 2)], left)
        yield a, b
    for step in range(1, n // 2):
        to_r, to_l = lax.rem(i + n // 2 - step, n), lax.rem(i + n // 2 + step, n)
        halves = step == 1
        if early and step == 2:
            a1.wait_recv()
            b1.wait_recv()
        va, vb = (h0, h1) if halves else (full, full)
        a.wait_recv()
        add_into(va(to_r), ra)
        ra, rb_next = slots[step]
        if early and halves:
            a = net.send(h0(to_r), ra.at[pl.ds(0, 2)], right)
        else:
            a = net.send(full(to_r), ra, right)
        b.wait_recv()
        add_into(vb(to_l), rb)
        rb = rb_next
        if early and halves:
            b = net.send(h1(to_l), rb.at[pl.ds(2, 2)], left)
        else:
            b = net.send(full(to_l), rb, left)
        yield a, b
    a.wait_recv()
    b.wait_recv()
    dst = full(i)
    dst[...] = (dst[...].astype(F32) + ra[...].astype(F32) + rb[...].astype(F32)).astype(BF)
    yield ()


def scatter_slots():
    ra, rb, rc = SPLIT_R
    out = []

    def ring(n, half0, half1, whole):
        out.append([(half0, half1)] + [(whole, whole)] * (n // 2 - 1))

    for _ in range(NZ):
        ring(4, (2, rc, W), (2, rc, W), (4, rc, W))
        ring(4, (2, rb, W), (2, rb, W), (4, rb, W))
    ring(8, (2, 4, ra, W), (2, 4, ra, W), (4, 4, ra, W))
    ring(8, (2, rb, W), (2, rb, W), (4, rb, W))
    ring(8, (2, rc, W), (2, rc, W), (4, rc, W))
    for shape in ((4, ra, W), (ra, W), (rb, W), (rc, W)):
        out.append([(shape, shape), (shape,)])
    return out


N_SEM = 320
N_LOC = 32


def kernel(*refs):
    it = iter(refs)
    take = lambda n: [next(it) for _ in range(n)]
    tok_in, grad_in, ids_in, gates_in, wg_in, wu_in, wd_in = take(7)
    tok_out, gg_out, dgu_out, dd_out = take(4)
    buf, xs, gxs, wgu, wd, sel, selt, part = take(8)
    agu, araw, pgu, sh, gp, member, target, gatev = take(8)
    rt, ggd, gg_rx, gg_rz = take(4)
    osg, osd, org, ord_ = take(4)
    stg, std = take(2)
    slots = [[tuple(take(len(pair))) for pair in ring] for ring in scatter_slots()]
    send_sem, recv_sem, loc_sem, stg_sem = take(4)

    e_idx = lax.axis_index("expert")
    z = lax.axis_index("etp")
    core = lax.rem(e_idx, 2)
    y = lax.rem(e_idx // 2, 4)
    x = e_idx // 8

    def dev(dx=0, dy=0, xx=None, yy=None, cc=None, zz=None):
        px = lax.rem(x + dx + 4, 4) if xx is None else xx
        py = lax.rem(y + dy + 4, 4) if yy is None else yy
        pc = core if cc is None else cc
        return ((px * 4 + py) * 2 + pc, z if zz is None else zz)

    xr, xl = dev(dx=1), dev(dx=-1)
    yr, yl = dev(dy=1), dev(dy=-1)
    zr, zl = dev(zz=lax.rem(z + 1, 8)), dev(zz=lax.rem(z + 7, 8))
    x_far, y_far = dev(dx=2), dev(dy=2)
    x_near = dev(xx=x + 1 - 2 * lax.rem(x, 2))
    y_near = dev(yy=y + 1 - 2 * lax.rem(y, 2))
    z1 = dev(zz=z + 1 - 2 * lax.rem(z, 2))
    z2 = dev(zz=z + 2 - 4 * lax.rem(z // 2, 2))
    z4 = dev(zz=lax.rem(z + 4, 8))
    sibling = dev(cc=1 - core)

    own_copies = [
        pltpu.make_async_copy(tok_in, buf.at[x, y, z, pl.ds(0, TOK)], loc_sem.at[0]),
        pltpu.make_async_copy(grad_in, buf.at[x, y, z, pl.ds(TOK, TOK)], loc_sem.at[1]),
    ]
    for j in range(2):
        ce = 2 * core + j
        own_copies.append(pltpu.make_async_copy(wg_in.at[j], wgu.at[ce, :, 0:H], loc_sem.at[2 + 3 * j]))
        own_copies.append(pltpu.make_async_copy(wu_in.at[j], wgu.at[ce, :, H : 2 * H], loc_sem.at[3 + 3 * j]))
        own_copies.append(pltpu.make_async_copy(wd_in.at[j], wd.at[ce], loc_sem.at[4 + 3 * j]))
    for c in own_copies:
        c.start()

    rt[x, y, 0:8, :] = ids_in[...].astype(F32)
    rt[x, y, 8:16, :] = gates_in[...].astype(F32)
    barrier = pltpu.get_barrier_semaphore()
    peers = (xr, xl, x_far, yr, yl, y_far, zr, zl, z2, z4, sibling)
    for p in peers:
        pl.semaphore_signal(barrier, inc=1, device_id=p, device_id_type=MESH)
    for c in own_copies[:2]:
        c.wait()
    pl.semaphore_wait(barrier, len(peers))

    net = Net(send_sem, recv_sem)

    sz = pl.ds
    ra, rb, rc = SPLIT_G
    ga, gb, gab, gc = sz(0, ra), sz(ra, rb), sz(0, ra + rb), sz(ra + rb, rc)
    hab, hb, hc = half16(ra + rb), half16(rb), half16(rc)
    zs = [z] + [lax.rem(z + k + 8, 8) for k in (1, -1, 2, -2, 3, -3, 4)]
    stage = [zs[0:1], zs[1:3], zs[3:5], zs[5:7], zs[7:8]]

    xab = direct_gather(net, x, lambda i: buf.at[i, y, z, gab], xr, xl, x_far)
    yc = direct_gather(net, y, lambda i: buf.at[x, i, z, gc], yr, yl, y_far)
    ya = direct_gather(net, y, lambda i: buf.at[:, i, z, ga], yr, yl, y_far)
    za = ring8_gather(
        net, z,
        lambda i: buf.at[:, :, i, ga],
        lambda i: buf.at[sz(0, 2), :, i, ga],
        lambda i: buf.at[sz(2, 2), :, i, ga],
        zr, zl)
    def column_b(px):
        return ring8_gather(
            net, z,
            lambda i: buf.at[px, y, i, gb],
            lambda i: buf.at[px, y, i, sz(ra, hb)],
            lambda i: buf.at[px, y, i, sz(ra + hb, rb - hb)],
            zr, zl)

    def column_c(py):
        return ring8_gather(
            net, z,
            lambda i: buf.at[x, py, i, gc],
            lambda i: buf.at[x, py, i, sz(ra + rb, hc)],
            lambda i: buf.at[x, py, i, sz(ra + rb + hc, rc - hc)],
            zr, zl)

    def plane(zz):
        return (
            ring4_gather(
                net, x,
                lambda i: buf.at[i, :, zz, gc],
                lambda i: buf.at[i, sz(0, 2), zz, gc],
                lambda i: buf.at[i, sz(2, 2), zz, gc],
                xr, xl),
            ring4_gather(
                net, y,
                lambda i: buf.at[:, i, zz, gb],
                lambda i: buf.at[sz(0, 2), i, zz, gb],
                lambda i: buf.at[sz(2, 2), i, zz, gb],
                yr, yl),
        )

    def half_plane(zz, k):
        lo = 2 * k
        return (
            ring4_gather(
                net, x,
                lambda i: buf.at[i, sz(lo, 2), zz, gc],
                lambda i: buf.at[i, sz(lo, 1), zz, gc],
                lambda i: buf.at[i, sz(lo + 1, 1), zz, gc],
                xr, xl),
            ring4_gather(
                net, y,
                lambda i: buf.at[sz(lo, 2), i, zz, gb],
                lambda i: buf.at[sz(lo, 1), i, zz, gb],
                lambda i: buf.at[sz(lo + 1, 1), i, zz, gb],
                yr, yl),
        )

    def route_ring():
        c = net.send(rt.at[x, y], rt.at[x, y], y_near)
        yield (c,)
        c.wait_recv()
        yh = 2 * (y // 2)
        c = net.send(rt.at[x, sz(yh, 2)], rt.at[x, sz(yh, 2)], y_far)
        yield (c,)
        c.wait_recv()
        c = net.send(rt.at[x], rt.at[x], x_near)
        yield (c,)
        c.wait_recv()
        xh = 2 * (x // 2)
        c = net.send(rt.at[sz(xh, 2)], rt.at[sz(xh, 2)], x_far)
        yield (c,)
        c.wait_recv()
        yield ()

    def load_weights():
        for c in own_copies[2:]:
            c.wait()
        copies = []
        for j in range(2):
            ce = 2 * core + j
            copies.append(net.send(wgu.at[ce], wgu.at[ce], sibling))
            copies.append(net.send(wd.at[ce], wd.at[ce], sibling))
        yield copies
        for c in copies:
            c.wait_recv()
        yield ()

    tasks = {}

    def ring_task(name, steps):
        tasks[name] = lambda: next(steps)

    ring_task("xab", xab)
    ring_task("yc", yc)
    ring_task("ya", ya)
    ring_task("za", za)
    for k, d in enumerate((0, 1, 3, 2)):
        ring_task(f"zb{k}", column_b(lax.rem(x + d, 4)))
        ring_task(f"zc{k}", column_c(lax.rem(y + d, 4)))
    for k, zz in enumerate(zs):
        for h in range(1 + k // 7):
            gx, gy = half_plane(zz, h) if k == 7 else plane(zz)
            ring_task(f"px{k + h}", gx)
            ring_task(f"py{k + h}", gy)
    ring_task("rt", route_ring())
    ring_task("wl", load_weights())
    first_expert = 4 * (x * 4 + y)

    def route():
        for b in range(16):
            tile = rt[b // 4, b % 4]
            for e in range(E4):
                hit = tile[0:8, :] == (first_expert + e).astype(F32)
                member[e * 16 + b, :] = jnp.sum(jnp.where(hit, 1.0, 0.0), axis=0)
                gatev[e * 16 + b, :] = jnp.sum(jnp.where(hit, tile[8:16, :], 0.0), axis=0)
        tri = jnp.where(
            lax.broadcasted_iota(jnp.int32, (TOK, TOK), 0) < lax.broadcasted_iota(jnp.int32, (TOK, TOK), 1),
            1.0, 0.0).astype(BF)
        m = member[...]
        pos = jnp.dot(m.astype(BF), tri, preferred_element_type=F32)
        target[...] = jnp.where(m > 0.5, pos, -1.0)

        for p in range(PAIRS):
            row = lax.broadcasted_iota(jnp.int32, (CAP, TOK), 0).astype(F32)
            zero = jnp.zeros((CAP, TOK), F32)
            parts = []
            for e in range(E4):
                r0, r1 = e * 16 + 2 * p, e * 16 + 2 * p + 1
                s0 = jnp.where(row == target[r0 : r0 + 1, :], 1.0, 0.0)
                s1 = jnp.where(row == target[r1 : r1 + 1, :], 1.0, 0.0)
                parts.append(jnp.concatenate([s0, zero], axis=1))
                parts.append(jnp.concatenate([zero, s1], axis=1))
            full = jnp.concatenate(parts, axis=0)
            sel[p] = full.astype(BF)
            selt[p] = full.T.astype(BF)

    def pick(zz):
        def body(px, _):
            for q in range(2):
                p = 2 * px + q
                s = sel[p]
                for r0, dst in ((0, xs), (TOK, gxs)):
                    t = buf[px, 2 * q : 2 * q + 2, zz, r0 : r0 + TOK, :].reshape(2 * TOK, W)
                    o = jnp.dot(s, t, preferred_element_type=F32).astype(BF)
                    for e in range(E4):
                        dst[zz, e, pl.ds(pl.multiple_of(p * 48, 16), 48), :] = o[e * 48 : (e + 1) * 48]
            return 0

        lax.fori_loop(0, PAIRS // 2, body, 0)

    def accumulate(zz, first):
        f = pl.ds(pl.multiple_of(zz * W, W), W)

        def body(e):
            gu = jnp.dot(xs[zz, e], wgu[e, f, :], preferred_element_type=F32)
            raw = lax.dot_general(gxs[zz, e], wd[e, :, f], (((1,), (1,)), ((), ())), preferred_element_type=F32)
            if first:
                agu[e] = gu
                araw[e] = raw
            else:
                agu[e] += gu
                araw[e] += raw

        for e in range(E4):
            body(e)

    def forward(e):
        gu, raw = agu[e], araw[e]
        gate_pre, up_pre = gu[:, :H], gu[:, H:]
        sig = 1.0 / (1.0 + jnp.exp(-gate_pre))
        swish = gate_pre * sig
        hidden = swish * up_pre
        gp[e] = jnp.broadcast_to(jnp.sum(hidden * raw, axis=1, keepdims=True), (ROWS, H))
        cols = []
        for p in range(PAIRS):
            for k in range(2):
                s = sel[p, pl.ds(pl.multiple_of(e * 48, 16), 48), k * TOK : (k + 1) * TOK].astype(F32)
                g = gatev[pl.ds(e * 16 + 2 * p + k, 1), :]
                cols.append(jnp.sum((s * g)[k * CAP : (k + 1) * CAP], axis=1, keepdims=True))
        gate = jnp.concatenate(cols, axis=0)
        hg = gate * raw
        pgu[e, :, H:] = (hg * swish).astype(BF)
        pgu[e, :, :H] = (hg * up_pre * sig * (1.0 + gate_pre * (1.0 - sig))).astype(BF)
        sh[e] = (gate * hidden).astype(BF)

    def produce(zz):
        f = pl.ds(pl.multiple_of(zz * W, W), W)

        def products(e):
            o = lax.dot_general(pgu[e], wgu[e, f, :], (((1,), (1,)), ((), ())),
                                preferred_element_type=F32).astype(BF)
            for p in range(PAIRS):
                part[p, e * 48 : (e + 1) * 48, :] = o[p * 48 : (p + 1) * 48]

        def spread(p, _):
            for q in range(4):
                o = jnp.dot(selt[4 * p + q], part[4 * p + q], preferred_element_type=F32).astype(BF)
                buf[2 * p + q // 2, 2 * (q % 2) : 2 * (q % 2) + 2, zz, 0:TOK, :] = o.reshape(2, TOK, W)
            return 0

        for e in range(E4):
            products(e)
        lax.fori_loop(0, PAIRS // 4, spread, 0)

    def gate_terms(p):
        for k in range(2):
            rows = []
            px, py = p // 2, 2 * (p % 2) + k
            tile = rt[px, py][0:8, :]
            acc = jnp.zeros((8, TOK), F32)
            for e in range(E4):
                s = sel[p, e * 48 : (e + 1) * 48, k * TOK : (k + 1) * TOK].astype(F32)
                v = jnp.sum(s * gp[e, pl.ds(pl.multiple_of(p * 48, 16), 48), :], axis=0, keepdims=True)
                acc = acc + jnp.where(tile == (first_expert + e).astype(F32), v, 0.0)
            ggd[px, py] = acc

    def loop(n, f):
        def body(i, _):
            f(i)
            return 0

        lax.fori_loop(0, n, body, 0)

    def do(order):
        for name in order:
            if name[0] == "-":
                net.drain(int(name[1:]))
            else:
                tasks[name]()

    tasks["route"] = route
    for k, zz in enumerate(zs):
        tasks[f"pick{k}"] = functools.partial(pick, zz)
        tasks[f"acc{k}"] = functools.partial(accumulate, zz, k == 0)
    do(GATHER)
    net.drain()
    loop(E4, forward)

    ra, rb, rc = SPLIT_R
    sa, sb, sc = sz(0, ra), sz(ra, rb), sz(ra + rb, rc)

    def rplane(k, zz):
        return (
            ring_scatter(
                net, 4, x,
                lambda i: buf.at[i, :, zz, sc],
                lambda i: buf.at[i, sz(0, 2), zz, sc],
                lambda i: buf.at[i, sz(2, 2), zz, sc],
                slots[2 * k], xr, xl),
            ring_scatter(
                net, 4, y,
                lambda i: buf.at[:, i, zz, sb],
                lambda i: buf.at[sz(0, 2), i, zz, sb],
                lambda i: buf.at[sz(2, 2), i, zz, sb],
                slots[2 * k + 1], yr, yl),
        )

    for k, zz in enumerate(zs):
        gx, gy = rplane(k, zz)
        ring_task(f"rx{k}", gx)
        ring_task(f"ry{k}", gy)
        tasks[f"make{k}"] = functools.partial(produce, zz)
    slots = slots[16:]
    sza = ring_scatter(
        net, 8, z,
        lambda i: buf.at[:, :, i, sa],
        lambda i: buf.at[sz(0, 2), :, i, sa],
        lambda i: buf.at[sz(2, 2), :, i, sa],
        slots[0], zr, zl, early=True)
    szb = ring_scatter(
        net, 8, z,
        lambda i: buf.at[:, y, i, sb],
        lambda i: buf.at[sz(0, 2), y, i, sb],
        lambda i: buf.at[sz(2, 2), y, i, sb],
        slots[1], zr, zl)
    szc = ring_scatter(
        net, 8, z,
        lambda i: buf.at[x, :, i, sc],
        lambda i: buf.at[x, sz(0, 2), i, sc],
        lambda i: buf.at[x, sz(2, 2), i, sc],
        slots[2], zr, zl)
    sya = direct_scatter(net, y, lambda i: buf.at[:, i, z, sa], slots[3], yr, yl, y_far)
    sxa = direct_scatter(net, x, lambda i: buf.at[i, y, z, sa], slots[4], xr, xl, x_far)
    sxb = direct_scatter(net, x, lambda i: buf.at[i, y, z, sb], slots[5], xr, xl, x_far)
    syc = direct_scatter(net, y, lambda i: buf.at[x, i, z, sc], slots[6], yr, yl, y_far)

    def gate_ring():
        xo = 2 - 2 * (x // 2)
        c = net.send(ggd.at[sz(xo, 2)], gg_rx.at[sz(0, 2)], x_far)
        yield (c,)
        c.wait_recv()
        xm = 2 * (x // 2)
        for k in range(2):
            for j in range(4):
                ggd[xm + k, j] = ggd[xm + k, j] + gg_rx[k, j]
        xn = x + 1 - 2 * lax.rem(x, 2)
        c = net.send(ggd.at[xn], gg_rx.at[2], x_near)
        yield (c,)
        c.wait_recv()
        for j in range(4):
            ggd[x, j] = ggd[x, j] + gg_rx[2, j]
        yo = 2 - 2 * (y // 2)
        c = net.send(ggd.at[x, sz(yo, 2)], gg_rx.at[3, sz(0, 2)], y_far)
        yield (c,)
        c.wait_recv()
        ym = 2 * (y // 2)
        for k in range(2):
            ggd[x, ym + k] = ggd[x, ym + k] + gg_rx[3, k]
        yn = y + 1 - 2 * lax.rem(y, 2)
        c = net.send(ggd.at[x, yn], gg_rx.at[3, 2], y_near)
        yield (c,)
        c.wait_recv()
        gg_rz[0] = ggd[x, y] + gg_rx[3, 2]
        for k, d in enumerate((z1, z2, z4)):
            c = net.send(gg_rz.at[2 * k], gg_rz.at[2 * k + 1], d)
            yield (c,)
            c.wait_recv()
            gg_rz[2 * k + 2] = gg_rz[2 * k] + gg_rz[2 * k + 1]
        yield ()

    tn = (((0,), (0,)), ((), ()))

    grad_copies = []

    def other_grads(j):
        e = 2 * (1 - core) + j

        def body(h, _):
            for q in range(2):
                m = 2 * h + q
                f = pl.ds(pl.multiple_of(m * W, W), W)
                osg[j, f, :] = lax.dot_general(xs[m, e], pgu[e], tn, preferred_element_type=F32).astype(BF)
                osd[j, :, f] = lax.dot_general(sh[e], gxs[m, e], tn, preferred_element_type=F32).astype(BF)
            return 0

        lax.fori_loop(0, NZ // 2, body, 0)
        grad_copies.extend([net.send(osg.at[j], org.at[j], sibling), net.send(osd.at[j], ord_.at[j], sibling)])

    def own_grads(lo, hi):
        def outs(j, m, slot):
            f = pl.ds(pl.multiple_of(m * W, W), W)
            return [
                pltpu.make_async_copy(stg.at[slot], dgu_out.at[j, f, :], stg_sem.at[slot, 0]),
                pltpu.make_async_copy(std.at[slot], dd_out.at[j, :, f], stg_sem.at[slot, 1]),
            ]

        def body(t, _):
            for slot in range(2):
                j, m = t // (NZ // 2), 2 * (t % (NZ // 2)) + slot
                e = 2 * core + j
                f = pl.ds(pl.multiple_of(m * W, W), W)

                @pl.when(t >= 1)
                def _():
                    for c in outs(j, m, slot):
                        c.wait()

                a = lax.dot_general(xs[m, e], pgu[e], tn, preferred_element_type=F32)
                stg[slot] = (a + org[j, f, :].astype(F32)).astype(BF)
                b = lax.dot_general(sh[e], gxs[m, e], tn, preferred_element_type=F32)
                std[slot] = (b + ord_[j, :, f].astype(F32)).astype(BF)
                for c in outs(j, m, slot):
                    c.start()
            return 0

        if lo == 0:
            for c in grad_copies:
                c.wait_recv()
        lax.fori_loop(lo, hi, body, 0)
        if hi == NZ:
            for slot in range(2):
                for c in outs(0, 0, slot):
                    c.wait()

    for name, steps in (("sza", sza), ("szb", szb), ("szc", szc), ("sya", sya),
                        ("sxa", sxa), ("sxb", sxb), ("syc", syc), ("gr", gate_ring())):
        ring_task(name, steps)
    tasks["gt"] = lambda: loop(PAIRS, gate_terms)
    for j in range(2):
        tasks[f"og{j}"] = functools.partial(other_grads, j)
    for t in range(NZ):
        tasks[f"wg{t}"] = functools.partial(own_grads, t, t + 1)
    do(SCATTER)

    tok_out[...] = buf[x, y, z, 0:TOK, :]
    gg_out[...] = gg_rz[6]
    net.drain()


def finish_kernel(tok, gg, dgu, dd, tok_out, gg_out, dg_out, du_out, dd_out):
    tok_out[...] = tok[...]
    gg_out[...] = gg[...]
    dg_out[...] = dgu[:, :, :H].astype(F32)
    du_out[...] = dgu[:, :, H:].astype(F32)
    dd_out[...] = dd[...].astype(F32)


def finish(tok, gg, dgu, dd):
    steps = 4
    n = D // steps
    whole = lambda i: (0, 0)
    rows = lambda i: (0, i, 0)
    cols = lambda i: (0, 0, i)
    return pl.pallas_call(
        finish_kernel,
        grid=(steps,),
        in_specs=[
            pl.BlockSpec((TOK, W), whole),
            pl.BlockSpec((8, TOK), whole),
            pl.BlockSpec((2, n, 2 * H), rows),
            pl.BlockSpec((2, H, n), cols),
        ],
        out_specs=[
            pl.BlockSpec((TOK, W), whole),
            pl.BlockSpec((8, TOK), whole),
            pl.BlockSpec((2, n, H), rows),
            pl.BlockSpec((2, n, H), rows),
            pl.BlockSpec((2, H, n), cols),
        ],
        out_shape=(
            jax.ShapeDtypeStruct((TOK, W), BF),
            jax.ShapeDtypeStruct((8, TOK), F32),
            jax.ShapeDtypeStruct((2, D, H), F32),
            jax.ShapeDtypeStruct((2, D, H), F32),
            jax.ShapeDtypeStruct((2, H, D), F32),
        ),
        compiler_params=pltpu.CompilerParams(vmem_limit_bytes=62 * 1024 * 1024),
    )(tok, gg, dgu, dd)


def local(tokens, grad_output, gates, ids, gate_weight, up_weight, down_weight):
    any_spec = pl.BlockSpec(memory_space=pl.ANY)
    vmem = pl.BlockSpec(memory_space=pltpu.VMEM)
    scratch = [
        pltpu.VMEM((NX, NY, NZ, 2 * TOK, W), BF),
        pltpu.VMEM((NZ, E4, ROWS, W), BF),
        pltpu.VMEM((NZ, E4, ROWS, W), BF),
        pltpu.VMEM((E4, D, 2 * H), BF),
        pltpu.VMEM((E4, H, D), BF),
        pltpu.VMEM((PAIRS, 192, 2 * TOK), BF),
        pltpu.VMEM((PAIRS, 2 * TOK, 192), BF),
        pltpu.VMEM((PAIRS, 192, W), BF),
        pltpu.VMEM((E4, ROWS, 2 * H), F32),
        pltpu.VMEM((E4, ROWS, H), F32),
        pltpu.VMEM((E4, ROWS, 2 * H), BF),
        pltpu.VMEM((E4, ROWS, H), BF),
        pltpu.VMEM((E4, ROWS, H), F32),
        pltpu.VMEM((64, TOK), F32),
        pltpu.VMEM((64, TOK), F32),
        pltpu.VMEM((64, TOK), F32),
        pltpu.VMEM((NX, NY, 16, TOK), F32),
        pltpu.VMEM((NX, NY, 8, TOK), F32),
        pltpu.VMEM((4, 4, 8, TOK), F32),
        pltpu.VMEM((7, 8, TOK), F32),
        pltpu.VMEM((2, D, 2 * H), BF),
        pltpu.VMEM((2, H, D), BF),
        pltpu.VMEM((2, D, 2 * H), BF),
        pltpu.VMEM((2, H, D), BF),
        pltpu.VMEM((2, W, 2 * H), BF),
        pltpu.VMEM((2, H, W), BF),
    ]
    for ring in scatter_slots():
        for pair in ring:
            for shape in pair:
                scratch.append(pltpu.VMEM(shape, BF))
    scratch += [
        pltpu.SemaphoreType.DMA((N_SEM,)),
        pltpu.SemaphoreType.DMA((N_SEM,)),
        pltpu.SemaphoreType.DMA((N_LOC,)),
        pltpu.SemaphoreType.DMA((2, 2)),
    ]
    outs = pl.pallas_call(
        kernel,
        out_shape=(
            jax.ShapeDtypeStruct((TOK, W), BF),
            jax.ShapeDtypeStruct((8, TOK), F32),
            jax.ShapeDtypeStruct((2, D, 2 * H), BF),
            jax.ShapeDtypeStruct((2, H, D), BF),
        ),
        in_specs=[any_spec, any_spec, vmem, vmem, any_spec, any_spec, any_spec],
        out_specs=(vmem, vmem, any_spec, any_spec),
        scratch_shapes=scratch,
        compiler_params=pltpu.CompilerParams(
            collective_id=0, has_side_effects=True, vmem_limit_bytes=63 * 1024 * 1024
        ),
    )(tokens, grad_output, ids.T, gates.T, gate_weight, up_weight, down_weight)
    grad_tokens, gate_grads, grad_gate, grad_up, grad_down = finish(*outs)
    return (grad_tokens, gate_grads.T, grad_gate, grad_up, grad_down)


def solution(mesh):
    return jax.shard_map(
        local,
        mesh=mesh,
        in_specs=(
            P("expert", "etp"),
            P("expert", "etp"),
            P("expert", None),
            P("expert", None),
            P("expert", None, "etp"),
            P("expert", None, "etp"),
            P("expert", "etp", None),
        ),
        out_specs=(
            P("expert", "etp"),
            P("expert", None),
            P("expert", None, "etp"),
            P("expert", None, "etp"),
            P("expert", "etp", None),
        ),
        check_vma=False,
    )
```

```python
import functools

import jax
import jax.numpy as jnp
from jax import lax
from jax.experimental import pallas as pl
from jax.experimental.pallas import tpu as pltpu
from jax.sharding import PartitionSpec as P

MESH = pl.DeviceIdType.MESH
BF = jnp.bfloat16
F32 = jnp.float32
NX, NY, NZ = 4, 4, 8
TOK = 128
W = 256
D = 2048
H = 128
TOP = 8
CAP = 24
E4 = 4
PAIRS = 8
ROWS = 2 * CAP * PAIRS
SPLIT_G = (48, 96, 112)
SPLIT_R = (32, 48, 48)

GATHER = (
    "zb0", "yc", "zc0", "pq0", "xab", "wl", "rt", "zb0", "yc", "pq1", "pq2", "zc2", "pq0", "zc0", "yc", "pq3",
    "zc1", "zc3", "rt", "xab", "zb2", "zb1", "wl", "-8", "zb0", "xab", "zb3", "ya", "py0", "zc2", "pq1", "rt", "-8",
    "zc0", "pq2", "-8", "pq0", "zc1", "-14", "pq3", "zc3", "px1", "pq1", "ya", "px2", "rt", "zb2", "-4", "pq2",
    "zb1", "ya", "-5", "pq3", "zb0", "zb3", "za", "py2", "py1", "-8", "zc2", "-4", "py0", "zc0", "-7", "zc1", "px1",
    "zc3", "px4", "px3", "zb2", "zb1", "py2", "zb0", "zb3", "px2", "py3", "py4", "-8", "rt", "route", "gcol", "py1",
    "px1", "py0", "pick0", "acc0", "-8", "py2", "za", "px4", "-11", "zc2", "zc0", "py3", "zc1", "-8", "zc3", "px6",
    "px5", "-4", "px3", "zb2", "-8", "zb1", "py4", "zb3", "py6", "py5", "px2", "pick2", "acc2", "py1", "pick1",
    "acc1", "py3", "px4", "py4", "px6", "-8", "za", "pick4", "acc4", "zc2", "zc1", "py6", "zc3", "px7", "zb2",
    "px8", "zb1", "-8", "zb3", "py7", "py8", "px5", "-16", "py5", "px3", "pick3", "acc3", "py6", "px6", "py7", "-8",
    "px7", "za", "py8", "pick6", "acc6", "px8", "py5", "-12", "py7", "px5", "py8", "pick5", "acc5", "px7", "-8",
    "px8", "za", "pick7", "acc7",
)
SCATTER = (
    "make7", "sza", "ry7", "rx7", "make6", "ry6", "rx6", "make5", "sza", "ry5", "rx5", "make4", "ry7", "ry4", "rx7",
    "rx4", "make3", "sza", "ry6", "ry5", "ry3", "rx6", "rx5", "rx3", "make2", "ry2", "rx2", "ry7", "szb", "make1",
    "ry4", "ry1", "rx7", "szc", "rx4", "rx1", "sza", "make0", "ry6", "ry0", "rx6", "rx0", "gt", "ry5", "szb", "ry3",
    "ry2", "gr", "rx5", "szc", "rx3", "rx2", "og0", "sza", "ry4", "ry1", "ry0", "gr", "rx4", "rx1", "ry3", "szb",
    "rx0", "og1", "ry2", "gr", "rx3", "szc", "ry1", "rx2", "-16", "rx1", "-8", "ry0", "-8", "gr", "-8", "sza",
    "sya", "rx0", "wg0", "wg1", "wg2", "szb", "gr", "wg3", "wg4", "szc", "wg5", "wg6", "sya", "sxa", "wg7", "gr",
    "szb", "sxb", "-32", "sxa", "szc", "syc", "gr", "-16", "sxb", "-24", "gr", "syc",
)


class Net:
    def __init__(self, send, recv):
        self.send_sem, self.recv_sem = send, recv
        self.count = 0
        self.pending = []

    def send(self, src, dst, device):
        k = self.count
        self.count += 1
        copy = pltpu.make_async_remote_copy(
            src_ref=src,
            dst_ref=dst,
            send_sem=self.send_sem.at[k],
            recv_sem=self.recv_sem.at[k],
            device_id=device,
            device_id_type=MESH,
        )
        copy.start()
        self.pending.append(copy)
        return copy

    def drain(self, n=None):
        n = len(self.pending) if n is None else n
        for copy in self.pending[:n]:
            copy.wait_send()
        self.pending = self.pending[n:]


def half16(n):
    return (n // 2 + 15) // 16 * 16


def ring4_gather(net, i, full, h0, h1, right, left):
    a = net.send(full(i), full(i), right)
    b = net.send(full(i), full(i), left)
    yield a, b
    prev, following = lax.rem(i + 3, 4), lax.rem(i + 1, 4)
    a.wait_recv()
    c = net.send(h0(prev), h0(prev), right)
    b.wait_recv()
    d = net.send(h1(following), h1(following), left)
    yield c, d
    c.wait_recv()
    d.wait_recv()
    yield ()


def direct_gather(net, i, full, right, left, far):
    a = net.send(full(i), full(i), right)
    b = net.send(full(i), full(i), left)
    c = net.send(full(i), full(i), far)
    yield a, b
    a.wait_recv()
    b.wait_recv()
    yield (c,)
    c.wait_recv()
    yield ()


def direct_scatter(net, i, full, slots, right, left, far):
    prev, following, other = lax.rem(i + 3, 4), lax.rem(i + 1, 4), lax.rem(i + 2, 4)
    a = net.send(full(other), slots[0][0], far)
    b = net.send(full(following), slots[0][1], right)
    c = net.send(full(prev), slots[1][0], left)
    yield a, b, c
    total = full(i)[...].astype(F32)
    for copy, slot in ((b, slots[0][1]), (c, slots[1][0]), (a, slots[0][0])):
        copy.wait_recv()
        total = total + slot[...].astype(F32)
    full(i)[...] = total.astype(BF)
    yield ()


def ring8_gather(net, i, full, h0, h1, right, left):
    a = net.send(full(i), full(i), right)
    b = net.send(full(i), full(i), left)
    yield a, b
    for step in (1, 2, 3):
        prev, following = lax.rem(i + 8 - step, 8), lax.rem(i + step, 8)
        va, vb = (full, full) if step < 3 else (h0, h1)
        a.wait_recv()
        a = net.send(va(prev), va(prev), right)
        b.wait_recv()
        b = net.send(vb(following), vb(following), left)
        yield a, b
    a.wait_recv()
    b.wait_recv()
    yield ()


def add_into(dst, src):
    dst[...] = (dst[...].astype(F32) + src[...].astype(F32)).astype(BF)


def ring_scatter(net, n, i, full, h0, h1, slots, right, left, early=False):
    far = lax.rem(i + n // 2, n)
    ra, rb = slots[0]
    a = net.send(h0(far), ra, right)
    b = net.send(h1(far), rb, left)
    yield () if early else (a, b)
    if early:
        to_r, to_l = lax.rem(far + n - 1, n), lax.rem(far + 1, n)
        na, nb = slots[1]
        a1 = net.send(h1(to_r), na.at[pl.ds(2, 2)], right)
        b1 = net.send(h0(to_l), nb.at[pl.ds(0, 2)], left)
        yield a, b
    for step in range(1, n // 2):
        to_r, to_l = lax.rem(i + n // 2 - step, n), lax.rem(i + n // 2 + step, n)
        halves = step == 1
        if early and step == 2:
            a1.wait_recv()
            b1.wait_recv()
        va, vb = (h0, h1) if halves else (full, full)
        a.wait_recv()
        add_into(va(to_r), ra)
        ra, rb_next = slots[step]
        if early and halves:
            a = net.send(h0(to_r), ra.at[pl.ds(0, 2)], right)
        else:
            a = net.send(full(to_r), ra, right)
        b.wait_recv()
        add_into(vb(to_l), rb)
        rb = rb_next
        if early and halves:
            b = net.send(h1(to_l), rb.at[pl.ds(2, 2)], left)
        else:
            b = net.send(full(to_l), rb, left)
        yield a, b
    a.wait_recv()
    b.wait_recv()
    dst = full(i)
    dst[...] = (dst[...].astype(F32) + ra[...].astype(F32) + rb[...].astype(F32)).astype(BF)
    yield ()


def scatter_slots():
    ra, rb, rc = SPLIT_R
    out = []

    def ring(n, half0, half1, whole):
        out.append([(half0, half1)] + [(whole, whole)] * (n // 2 - 1))

    for _ in range(NZ):
        ring(4, (2, rc, W), (2, rc, W), (4, rc, W))
        ring(4, (2, rb, W), (2, rb, W), (4, rb, W))
    ring(8, (2, 4, ra, W), (2, 4, ra, W), (4, 4, ra, W))
    ring(8, (2, rb, W), (2, rb, W), (4, rb, W))
    ring(8, (2, rc, W), (2, rc, W), (4, rc, W))
    for shape in ((4, ra, W), (ra, W), (rb, W), (rc, W)):
        out.append([(shape, shape), (shape,)])
    return out


N_SEM = 340
N_LOC = 32


def kernel(*refs):
    it = iter(refs)
    take = lambda n: [next(it) for _ in range(n)]
    tok_in, grad_in, ids_in, gates_in, wg_in, wu_in, wd_in = take(7)
    tok_out, gg_out, dgu_out, dd_out = take(4)
    buf, xs, gxs, wgu, wd, sel, selt, part = take(8)
    agu, araw, pgu, sh, gp, gatecol, member, target, gatev = take(9)
    rt, ggd, gg_rx, gg_rz = take(4)
    osg, osd, org, ord_ = take(4)
    stg, std = take(2)
    slots = [[tuple(take(len(pair))) for pair in ring] for ring in scatter_slots()]
    send_sem, recv_sem, loc_sem, stg_sem = take(4)

    e_idx = lax.axis_index("expert")
    z = lax.axis_index("etp")
    core = lax.rem(e_idx, 2)
    y = lax.rem(e_idx // 2, 4)
    x = e_idx // 8

    def dev(dx=0, dy=0, xx=None, yy=None, cc=None, zz=None):
        px = lax.rem(x + dx + 4, 4) if xx is None else xx
        py = lax.rem(y + dy + 4, 4) if yy is None else yy
        pc = core if cc is None else cc
        return ((px * 4 + py) * 2 + pc, z if zz is None else zz)

    xr, xl = dev(dx=1), dev(dx=-1)
    yr, yl = dev(dy=1), dev(dy=-1)
    zr, zl = dev(zz=lax.rem(z + 1, 8)), dev(zz=lax.rem(z + 7, 8))
    x_far, y_far = dev(dx=2), dev(dy=2)
    x_near = dev(xx=x + 1 - 2 * lax.rem(x, 2))
    y_near = dev(yy=y + 1 - 2 * lax.rem(y, 2))
    z1 = dev(zz=z + 1 - 2 * lax.rem(z, 2))
    z2 = dev(zz=z + 2 - 4 * lax.rem(z // 2, 2))
    z4 = dev(zz=lax.rem(z + 4, 8))
    sibling = dev(cc=1 - core)

    own_copies = [
        pltpu.make_async_copy(tok_in, buf.at[x, y, z, pl.ds(0, TOK)], loc_sem.at[0]),
        pltpu.make_async_copy(grad_in, buf.at[x, y, z, pl.ds(TOK, TOK)], loc_sem.at[1]),
    ]
    for j in range(2):
        ce = 2 * core + j
        own_copies.append(pltpu.make_async_copy(wg_in.at[j], wgu.at[ce, :, 0:H], loc_sem.at[2 + 3 * j]))
        own_copies.append(pltpu.make_async_copy(wu_in.at[j], wgu.at[ce, :, H : 2 * H], loc_sem.at[3 + 3 * j]))
        own_copies.append(pltpu.make_async_copy(wd_in.at[j], wd.at[ce], loc_sem.at[4 + 3 * j]))
    for c in own_copies:
        c.start()

    rt[x, y, 0:8, :] = ids_in[...].astype(F32)
    rt[x, y, 8:16, :] = gates_in[...].astype(F32)
    barrier = pltpu.get_barrier_semaphore()
    peers = (xr, xl, x_far, yr, yl, y_far, zr, zl, z2, z4, sibling)
    for p in peers:
        pl.semaphore_signal(barrier, inc=1, device_id=p, device_id_type=MESH)
    for c in own_copies[:2]:
        c.wait()
    pl.semaphore_wait(barrier, len(peers))

    net = Net(send_sem, recv_sem)

    sz = pl.ds
    ra, rb, rc = SPLIT_G
    ga, gb, gab, gc = sz(0, ra), sz(ra, rb), sz(0, ra + rb), sz(ra + rb, rc)
    hab, hb, hc = half16(ra + rb), half16(rb), half16(rc)
    zs = [z] + [lax.rem(z + k + 8, 8) for k in (1, -1, 2, -2, 3, -3, 4)]
    stage = [zs[0:1], zs[1:3], zs[3:5], zs[5:7], zs[7:8]]

    xab = direct_gather(net, x, lambda i: buf.at[i, y, z, gab], xr, xl, x_far)
    yc = direct_gather(net, y, lambda i: buf.at[x, i, z, gc], yr, yl, y_far)
    ya = direct_gather(net, y, lambda i: buf.at[:, i, z, ga], yr, yl, y_far)
    za = ring8_gather(
        net, z,
        lambda i: buf.at[:, :, i, ga],
        lambda i: buf.at[sz(0, 2), :, i, ga],
        lambda i: buf.at[sz(2, 2), :, i, ga],
        zr, zl)
    def column_b(px):
        return ring8_gather(
            net, z,
            lambda i: buf.at[px, y, i, gb],
            lambda i: buf.at[px, y, i, sz(ra, hb)],
            lambda i: buf.at[px, y, i, sz(ra + hb, rb - hb)],
            zr, zl)

    def column_c(py):
        return ring8_gather(
            net, z,
            lambda i: buf.at[x, py, i, gc],
            lambda i: buf.at[x, py, i, sz(ra + rb, hc)],
            lambda i: buf.at[x, py, i, sz(ra + rb + hc, rc - hc)],
            zr, zl)

    def plane(zz):
        return (
            ring4_gather(
                net, x,
                lambda i: buf.at[i, :, zz, gc],
                lambda i: buf.at[i, sz(0, 2), zz, gc],
                lambda i: buf.at[i, sz(2, 2), zz, gc],
                xr, xl),
            ring4_gather(
                net, y,
                lambda i: buf.at[:, i, zz, gb],
                lambda i: buf.at[sz(0, 2), i, zz, gb],
                lambda i: buf.at[sz(2, 2), i, zz, gb],
                yr, yl),
        )

    def half_plane(zz, k):
        lo = 2 * k
        return (
            ring4_gather(
                net, x,
                lambda i: buf.at[i, sz(lo, 2), zz, gc],
                lambda i: buf.at[i, sz(lo, 1), zz, gc],
                lambda i: buf.at[i, sz(lo + 1, 1), zz, gc],
                xr, xl),
            ring4_gather(
                net, y,
                lambda i: buf.at[sz(lo, 2), i, zz, gb],
                lambda i: buf.at[sz(lo, 1), i, zz, gb],
                lambda i: buf.at[sz(lo + 1, 1), i, zz, gb],
                yr, yl),
        )

    def route_ring():
        c = net.send(rt.at[x, y], rt.at[x, y], y_near)
        yield (c,)
        c.wait_recv()
        yh = 2 * (y // 2)
        c = net.send(rt.at[x, sz(yh, 2)], rt.at[x, sz(yh, 2)], y_far)
        yield (c,)
        c.wait_recv()
        c = net.send(rt.at[x], rt.at[x], x_near)
        yield (c,)
        c.wait_recv()
        xh = 2 * (x // 2)
        c = net.send(rt.at[sz(xh, 2)], rt.at[sz(xh, 2)], x_far)
        yield (c,)
        c.wait_recv()
        yield ()

    def load_weights():
        for c in own_copies[2:]:
            c.wait()
        copies = []
        for j in range(2):
            ce = 2 * core + j
            copies.append(net.send(wgu.at[ce], wgu.at[ce], sibling))
            copies.append(net.send(wd.at[ce], wd.at[ce], sibling))
        yield copies
        for c in copies:
            c.wait_recv()
        yield ()

    tasks = {}

    def ring_task(name, steps):
        tasks[name] = lambda: next(steps)

    ring_task("xab", xab)
    ring_task("yc", yc)
    ring_task("ya", ya)
    ring_task("za", za)
    for k, d in enumerate((0, 1, 3, 2)):
        ring_task(f"zb{k}", column_b(lax.rem(x + d, 4)))
        ring_task(f"zc{k}", column_c(lax.rem(y + d, 4)))
    for k, d in enumerate((0, 1, 3, 2)):
        py = lax.rem(y + d, 4)
        ring_task(f"pq{k}", ring4_gather(
            net, x,
            lambda i, py=py: buf.at[i, py, z, gc],
            lambda i, py=py: buf.at[i, py, z, sz(ra + rb, hc)],
            lambda i, py=py: buf.at[i, py, z, sz(ra + rb + hc, rc - hc)],
            xr, xl))
    for k, zz in enumerate(zs):
        for h in range(1 + k // 7):
            gx, gy = half_plane(zz, h) if k == 7 else plane(zz)
            if k > 0:
                ring_task(f"px{k + h}", gx)
            ring_task(f"py{k + h}", gy)
    ring_task("rt", route_ring())
    ring_task("wl", load_weights())
    first_expert = 4 * (x * 4 + y)

    def route():
        for b in range(16):
            tile = rt[b // 4, b % 4]
            for e in range(E4):
                hit = tile[0:8, :] == (first_expert + e).astype(F32)
                member[e * 16 + b, :] = jnp.sum(jnp.where(hit, 1.0, 0.0), axis=0)
                gatev[e * 16 + b, :] = jnp.sum(jnp.where(hit, tile[8:16, :], 0.0), axis=0)
        tri = jnp.where(
            lax.broadcasted_iota(jnp.int32, (TOK, TOK), 0) < lax.broadcasted_iota(jnp.int32, (TOK, TOK), 1),
            1.0, 0.0).astype(BF)
        m = member[...]
        pos = jnp.dot(m.astype(BF), tri, preferred_element_type=F32)
        target[...] = jnp.where(m > 0.5, pos, -1.0)

        for p in range(PAIRS):
            row = lax.broadcasted_iota(jnp.int32, (CAP, TOK), 0).astype(F32)
            zero = jnp.zeros((CAP, TOK), F32)
            parts = []
            for e in range(E4):
                r0, r1 = e * 16 + 2 * p, e * 16 + 2 * p + 1
                s0 = jnp.where(row == target[r0 : r0 + 1, :], 1.0, 0.0)
                s1 = jnp.where(row == target[r1 : r1 + 1, :], 1.0, 0.0)
                parts.append(jnp.concatenate([s0, zero], axis=1))
                parts.append(jnp.concatenate([zero, s1], axis=1))
            full = jnp.concatenate(parts, axis=0)
            sel[p] = full.astype(BF)
            selt[p] = full.T.astype(BF)

    def pick(zz):
        def body(px, _):
            for q in range(2):
                p = 2 * px + q
                s = sel[p]
                for r0, dst in ((0, xs), (TOK, gxs)):
                    t = buf[px, 2 * q : 2 * q + 2, zz, r0 : r0 + TOK, :].reshape(2 * TOK, W)
                    o = jnp.dot(s, t, preferred_element_type=F32).astype(BF)
                    for e in range(E4):
                        dst[zz, e, pl.ds(pl.multiple_of(p * 48, 16), 48), :] = o[e * 48 : (e + 1) * 48]
            return 0

        lax.fori_loop(0, PAIRS // 2, body, 0)

    def accumulate(zz, first):
        f = pl.ds(pl.multiple_of(zz * W, W), W)

        def body(e):
            gu = jnp.dot(xs[zz, e], wgu[e, f, :], preferred_element_type=F32)
            raw = lax.dot_general(gxs[zz, e], wd[e, :, f], (((1,), (1,)), ((), ())), preferred_element_type=F32)
            if first:
                agu[e] = gu
                araw[e] = raw
            else:
                agu[e] += gu
                araw[e] += raw

        for e in range(E4):
            body(e)

    def gate_columns(e):
        for p in range(PAIRS):
            for k in range(2):
                s = sel[p, pl.ds(pl.multiple_of(e * 48, 16), 48), k * TOK : (k + 1) * TOK].astype(F32)
                g = gatev[pl.ds(e * 16 + 2 * p + k, 1), :]
                col = jnp.sum((s * g)[k * CAP : (k + 1) * CAP], axis=1, keepdims=True)
                gatecol[e, pl.ds(p * 48 + k * CAP, CAP), :] = jnp.broadcast_to(col, (CAP, H))

    def forward(e):
        gu, raw = agu[e], araw[e]
        gate_pre, up_pre = gu[:, :H], gu[:, H:]
        sig = 1.0 / (1.0 + jnp.exp(-gate_pre))
        swish = gate_pre * sig
        hidden = swish * up_pre
        gp[e] = jnp.broadcast_to(jnp.sum(hidden * raw, axis=1, keepdims=True), (ROWS, H))
        gate = gatecol[e]
        hg = gate * raw
        pgu[e, :, H:] = (hg * swish).astype(BF)
        pgu[e, :, :H] = (hg * up_pre * sig * (1.0 + gate_pre * (1.0 - sig))).astype(BF)
        sh[e] = (gate * hidden).astype(BF)

    def produce(zz):
        f = pl.ds(pl.multiple_of(zz * W, W), W)

        def products(e):
            o = lax.dot_general(pgu[e], wgu[e, f, :], (((1,), (1,)), ((), ())),
                                preferred_element_type=F32).astype(BF)
            for p in range(PAIRS):
                part[p, e * 48 : (e + 1) * 48, :] = o[p * 48 : (p + 1) * 48]

        def spread(p, _):
            for q in range(4):
                o = jnp.dot(selt[4 * p + q], part[4 * p + q], preferred_element_type=F32).astype(BF)
                buf[2 * p + q // 2, 2 * (q % 2) : 2 * (q % 2) + 2, zz, 0:TOK, :] = o.reshape(2, TOK, W)
            return 0

        for e in range(E4):
            products(e)
        lax.fori_loop(0, PAIRS // 4, spread, 0)

    def gate_terms(p):
        for k in range(2):
            rows = []
            px, py = p // 2, 2 * (p % 2) + k
            tile = rt[px, py][0:8, :]
            acc = jnp.zeros((8, TOK), F32)
            for e in range(E4):
                s = sel[p, e * 48 : (e + 1) * 48, k * TOK : (k + 1) * TOK].astype(F32)
                v = jnp.sum(s * gp[e, pl.ds(pl.multiple_of(p * 48, 16), 48), :], axis=0, keepdims=True)
                acc = acc + jnp.where(tile == (first_expert + e).astype(F32), v, 0.0)
            ggd[px, py] = acc

    def loop(n, f):
        def body(i, _):
            f(i)
            return 0

        lax.fori_loop(0, n, body, 0)

    def do(order):
        for name in order:
            if name[0] == "-":
                net.drain(int(name[1:]))
            else:
                tasks[name]()

    tasks["route"] = route
    tasks["gcol"] = lambda: loop(E4, gate_columns)
    for k, zz in enumerate(zs):
        tasks[f"pick{k}"] = functools.partial(pick, zz)
        tasks[f"acc{k}"] = functools.partial(accumulate, zz, k == 0)
    do(GATHER)
    net.drain()
    loop(E4, forward)

    ra, rb, rc = SPLIT_R
    sa, sb, sc = sz(0, ra), sz(ra, rb), sz(ra + rb, rc)

    def rplane(k, zz):
        return (
            ring_scatter(
                net, 4, x,
                lambda i: buf.at[i, :, zz, sc],
                lambda i: buf.at[i, sz(0, 2), zz, sc],
                lambda i: buf.at[i, sz(2, 2), zz, sc],
                slots[2 * k], xr, xl),
            ring_scatter(
                net, 4, y,
                lambda i: buf.at[:, i, zz, sb],
                lambda i: buf.at[sz(0, 2), i, zz, sb],
                lambda i: buf.at[sz(2, 2), i, zz, sb],
                slots[2 * k + 1], yr, yl),
        )

    for k, zz in enumerate(zs):
        gx, gy = rplane(k, zz)
        ring_task(f"rx{k}", gx)
        ring_task(f"ry{k}", gy)
        tasks[f"make{k}"] = functools.partial(produce, zz)
    slots = slots[16:]
    sza = ring_scatter(
        net, 8, z,
        lambda i: buf.at[:, :, i, sa],
        lambda i: buf.at[sz(0, 2), :, i, sa],
        lambda i: buf.at[sz(2, 2), :, i, sa],
        slots[0], zr, zl, early=True)
    szb = ring_scatter(
        net, 8, z,
        lambda i: buf.at[:, y, i, sb],
        lambda i: buf.at[sz(0, 2), y, i, sb],
        lambda i: buf.at[sz(2, 2), y, i, sb],
        slots[1], zr, zl)
    szc = ring_scatter(
        net, 8, z,
        lambda i: buf.at[x, :, i, sc],
        lambda i: buf.at[x, sz(0, 2), i, sc],
        lambda i: buf.at[x, sz(2, 2), i, sc],
        slots[2], zr, zl)
    sya = direct_scatter(net, y, lambda i: buf.at[:, i, z, sa], slots[3], yr, yl, y_far)
    sxa = direct_scatter(net, x, lambda i: buf.at[i, y, z, sa], slots[4], xr, xl, x_far)
    sxb = direct_scatter(net, x, lambda i: buf.at[i, y, z, sb], slots[5], xr, xl, x_far)
    syc = direct_scatter(net, y, lambda i: buf.at[x, i, z, sc], slots[6], yr, yl, y_far)

    def gate_ring():
        xo = 2 - 2 * (x // 2)
        c = net.send(ggd.at[sz(xo, 2)], gg_rx.at[sz(0, 2)], x_far)
        yield (c,)
        c.wait_recv()
        xm = 2 * (x // 2)
        for k in range(2):
            for j in range(4):
                ggd[xm + k, j] = ggd[xm + k, j] + gg_rx[k, j]
        xn = x + 1 - 2 * lax.rem(x, 2)
        c = net.send(ggd.at[xn], gg_rx.at[2], x_near)
        yield (c,)
        c.wait_recv()
        for j in range(4):
            ggd[x, j] = ggd[x, j] + gg_rx[2, j]
        yo = 2 - 2 * (y // 2)
        c = net.send(ggd.at[x, sz(yo, 2)], gg_rx.at[3, sz(0, 2)], y_far)
        yield (c,)
        c.wait_recv()
        ym = 2 * (y // 2)
        for k in range(2):
            ggd[x, ym + k] = ggd[x, ym + k] + gg_rx[3, k]
        yn = y + 1 - 2 * lax.rem(y, 2)
        c = net.send(ggd.at[x, yn], gg_rx.at[3, 2], y_near)
        yield (c,)
        c.wait_recv()
        gg_rz[0] = ggd[x, y] + gg_rx[3, 2]
        for k, d in enumerate((z1, z2, z4)):
            c = net.send(gg_rz.at[2 * k], gg_rz.at[2 * k + 1], d)
            yield (c,)
            c.wait_recv()
            gg_rz[2 * k + 2] = gg_rz[2 * k] + gg_rz[2 * k + 1]
        yield ()

    tn = (((0,), (0,)), ((), ()))

    grad_copies = []

    def other_grads(j):
        e = 2 * (1 - core) + j

        def body(h, _):
            for q in range(2):
                m = 2 * h + q
                f = pl.ds(pl.multiple_of(m * W, W), W)
                osg[j, f, :] = lax.dot_general(xs[m, e], pgu[e], tn, preferred_element_type=F32).astype(BF)
                osd[j, :, f] = lax.dot_general(sh[e], gxs[m, e], tn, preferred_element_type=F32).astype(BF)
            return 0

        lax.fori_loop(0, NZ // 2, body, 0)
        grad_copies.extend([net.send(osg.at[j], org.at[j], sibling), net.send(osd.at[j], ord_.at[j], sibling)])

    def own_grads(lo, hi):
        def outs(j, m, slot):
            f = pl.ds(pl.multiple_of(m * W, W), W)
            return [
                pltpu.make_async_copy(stg.at[slot], dgu_out.at[j, f, :], stg_sem.at[slot, 0]),
                pltpu.make_async_copy(std.at[slot], dd_out.at[j, :, f], stg_sem.at[slot, 1]),
            ]

        def body(t, _):
            for slot in range(2):
                j, m = t // (NZ // 2), 2 * (t % (NZ // 2)) + slot
                e = 2 * core + j
                f = pl.ds(pl.multiple_of(m * W, W), W)

                @pl.when(t >= 1)
                def _():
                    for c in outs(j, m, slot):
                        c.wait()

                a = lax.dot_general(xs[m, e], pgu[e], tn, preferred_element_type=F32)
                stg[slot] = (a + org[j, f, :].astype(F32)).astype(BF)
                b = lax.dot_general(sh[e], gxs[m, e], tn, preferred_element_type=F32)
                std[slot] = (b + ord_[j, :, f].astype(F32)).astype(BF)
                for c in outs(j, m, slot):
                    c.start()
            return 0

        if lo == 0:
            for c in grad_copies:
                c.wait_recv()
        lax.fori_loop(lo, hi, body, 0)
        if hi == NZ:
            for slot in range(2):
                for c in outs(0, 0, slot):
                    c.wait()

    for name, steps in (("sza", sza), ("szb", szb), ("szc", szc), ("sya", sya),
                        ("sxa", sxa), ("sxb", sxb), ("syc", syc), ("gr", gate_ring())):
        ring_task(name, steps)
    tasks["gt"] = lambda: loop(PAIRS, gate_terms)
    for j in range(2):
        tasks[f"og{j}"] = functools.partial(other_grads, j)
    for t in range(NZ):
        tasks[f"wg{t}"] = functools.partial(own_grads, t, t + 1)
    do(SCATTER)

    tok_out[...] = buf[x, y, z, 0:TOK, :]
    gg_out[...] = gg_rz[6]
    net.drain()


def finish_kernel(tok, gg, dgu, dd, tok_out, gg_out, dg_out, du_out, dd_out):
    tok_out[...] = tok[...]
    gg_out[...] = gg[...]
    dg_out[...] = dgu[:, :, :H].astype(F32)
    du_out[...] = dgu[:, :, H:].astype(F32)
    dd_out[...] = dd[...].astype(F32)


def finish(tok, gg, dgu, dd):
    steps = 8
    n = D // steps
    whole = lambda i: (0, 0)
    rows = lambda i: (0, i, 0)
    cols = lambda i: (0, 0, i)
    return pl.pallas_call(
        finish_kernel,
        grid=(steps,),
        in_specs=[
            pl.BlockSpec((TOK, W), whole),
            pl.BlockSpec((8, TOK), whole),
            pl.BlockSpec((2, n, 2 * H), rows),
            pl.BlockSpec((2, H, n), cols),
        ],
        out_specs=[
            pl.BlockSpec((TOK, W), whole),
            pl.BlockSpec((8, TOK), whole),
            pl.BlockSpec((2, n, H), rows),
            pl.BlockSpec((2, n, H), rows),
            pl.BlockSpec((2, H, n), cols),
        ],
        out_shape=(
            jax.ShapeDtypeStruct((TOK, W), BF),
            jax.ShapeDtypeStruct((8, TOK), F32),
            jax.ShapeDtypeStruct((2, D, H), F32),
            jax.ShapeDtypeStruct((2, D, H), F32),
            jax.ShapeDtypeStruct((2, H, D), F32),
        ),
        compiler_params=pltpu.CompilerParams(vmem_limit_bytes=62 * 1024 * 1024),
    )(tok, gg, dgu, dd)


def local(tokens, grad_output, gates, ids, gate_weight, up_weight, down_weight):
    any_spec = pl.BlockSpec(memory_space=pl.ANY)
    vmem = pl.BlockSpec(memory_space=pltpu.VMEM)
    scratch = [
        pltpu.VMEM((NX, NY, NZ, 2 * TOK, W), BF),
        pltpu.VMEM((NZ, E4, ROWS, W), BF),
        pltpu.VMEM((NZ, E4, ROWS, W), BF),
        pltpu.VMEM((E4, D, 2 * H), BF),
        pltpu.VMEM((E4, H, D), BF),
        pltpu.VMEM((PAIRS, 192, 2 * TOK), BF),
        pltpu.VMEM((PAIRS, 2 * TOK, 192), BF),
        pltpu.VMEM((PAIRS, 192, W), BF),
        pltpu.VMEM((E4, ROWS, 2 * H), F32),
        pltpu.VMEM((E4, ROWS, H), F32),
        pltpu.VMEM((E4, ROWS, 2 * H), BF),
        pltpu.VMEM((E4, ROWS, H), BF),
        pltpu.VMEM((E4, ROWS, H), F32),
        pltpu.VMEM((E4, ROWS, H), F32),
        pltpu.VMEM((64, TOK), F32),
        pltpu.VMEM((64, TOK), F32),
        pltpu.VMEM((64, TOK), F32),
        pltpu.VMEM((NX, NY, 16, TOK), F32),
        pltpu.VMEM((NX, NY, 8, TOK), F32),
        pltpu.VMEM((4, 4, 8, TOK), F32),
        pltpu.VMEM((7, 8, TOK), F32),
        pltpu.VMEM((2, D, 2 * H), BF),
        pltpu.VMEM((2, H, D), BF),
        pltpu.VMEM((2, D, 2 * H), BF),
        pltpu.VMEM((2, H, D), BF),
        pltpu.VMEM((2, W, 2 * H), BF),
        pltpu.VMEM((2, H, W), BF),
    ]
    for ring in scatter_slots():
        for pair in ring:
            for shape in pair:
                scratch.append(pltpu.VMEM(shape, BF))
    scratch += [
        pltpu.SemaphoreType.DMA((N_SEM,)),
        pltpu.SemaphoreType.DMA((N_SEM,)),
        pltpu.SemaphoreType.DMA((N_LOC,)),
        pltpu.SemaphoreType.DMA((2, 2)),
    ]
    outs = pl.pallas_call(
        kernel,
        out_shape=(
            jax.ShapeDtypeStruct((TOK, W), BF),
            jax.ShapeDtypeStruct((8, TOK), F32),
            jax.ShapeDtypeStruct((2, D, 2 * H), BF),
            jax.ShapeDtypeStruct((2, H, D), BF),
        ),
        in_specs=[any_spec, any_spec, vmem, vmem, any_spec, any_spec, any_spec],
        out_specs=(vmem, vmem, any_spec, any_spec),
        scratch_shapes=scratch,
        compiler_params=pltpu.CompilerParams(
            collective_id=0, has_side_effects=True, vmem_limit_bytes=63 * 1024 * 1024
        ),
    )(tokens, grad_output, ids.T, gates.T, gate_weight, up_weight, down_weight)
    grad_tokens, gate_grads, grad_gate, grad_up, grad_down = finish(*outs)
    return (grad_tokens, gate_grads.T, grad_gate, grad_up, grad_down)


def solution(mesh):
    return jax.shard_map(
        local,
        mesh=mesh,
        in_specs=(
            P("expert", "etp"),
            P("expert", "etp"),
            P("expert", None),
            P("expert", None),
            P("expert", None, "etp"),
            P("expert", None, "etp"),
            P("expert", "etp", None),
        ),
        out_specs=(
            P("expert", "etp"),
            P("expert", None),
            P("expert", None, "etp"),
            P("expert", None, "etp"),
            P("expert", "etp", None),
        ),
        check_vma=False,
    )
```

```python
import functools

import jax
import jax.numpy as jnp
from jax import lax
from jax.experimental import pallas as pl
from jax.experimental.pallas import tpu as pltpu
from jax.sharding import PartitionSpec as P

MESH = pl.DeviceIdType.MESH
BF = jnp.bfloat16
F32 = jnp.float32
NX, NY, NZ = 4, 4, 8
TOK = 128
W = 256
D = 2048
H = 128
TOP = 8
CAP = 24
E4 = 4
PAIRS = 8
ROWS = 2 * CAP * PAIRS
SPLIT_G = (48, 96, 112)
SPLIT_R = (32, 48, 48)

GATHER = (
    "zb0", "yc", "zc0", "pq0", "xab", "wl", "rt", "zb0", "yc", "pq1", "pq2", "zc2", "pq0", "zc0", "yc", "pq3",
    "zc1", "zc3", "rt", "xab", "zb2", "zb1", "wl", "-8", "zb0", "xab", "zb3", "ya", "py0", "zc2", "pq1", "rt", "-8",
    "zc0", "pq2", "-8", "pq0", "zc1", "-14", "pq3", "zc3", "px1", "pq1", "ya", "px2", "rt", "zb2", "-4", "pq2",
    "zb1", "ya", "-5", "pq3", "zb0", "zb3", "za", "py2", "py1", "-8", "zc2", "-4", "py0", "zc0", "-7", "zc1", "px1",
    "zc3", "px4", "px3", "zb2", "zb1", "py2", "zb0", "zb3", "px2", "py3", "py4", "-8", "rt", "route", "gcol", "py1",
    "px1", "py0", "pick0", "acc0", "-8", "py2", "za", "px4", "-11", "zc2", "zc0", "py3", "zc1", "-8", "zc3", "px6",
    "px5", "-4", "px3", "zb2", "-8", "zb1", "py4", "zb3", "py6", "py5", "px2", "pick2", "acc2", "py1", "pick1",
    "acc1", "py3", "px4", "py4", "px6", "-8", "za", "pick4", "acc4", "zc2", "zc1", "py6", "zc3", "px7", "zb2",
    "px8", "zb1", "-8", "zb3", "py7", "py8", "px5", "-16", "py5", "px3", "pick3", "acc3", "py6", "px6", "py7", "-8",
    "px7", "za", "py8", "pick6", "acc6", "px8", "py5", "-12", "py7", "px5", "py8", "pick5", "acc5", "px7", "-8",
    "px8", "za", "pick7", "acc7",
)
SCATTER = (
    "make7", "sza", "ry7", "rx7", "make6", "ry6", "rx6", "make5", "sza", "ry5", "rx5", "make4", "ry7", "ry4", "rx7",
    "rx4", "make3", "sza", "ry6", "ry5", "ry3", "rx6", "rx5", "rx3", "make2", "ry2", "rx2", "ry7", "szb", "make1",
    "ry4", "ry1", "rx7", "szc", "rx4", "rx1", "sza", "make0", "ry6", "ry0", "rx6", "rx0", "gt", "ry5", "szb", "ry3",
    "ry2", "gr", "rx5", "szc", "rx3", "rx2", "og0", "sza", "ry4", "ry1", "ry0", "gr", "rx4", "rx1", "ry3", "szb",
    "rx0", "og1", "ry2", "gr", "rx3", "szc", "ry1", "rx2", "-16", "rx1", "-8", "ry0", "-8", "gr", "-8", "sza",
    "sya", "rx0", "wg0", "wg1", "wg2", "szb", "gr", "wg3", "wg4", "szc", "wg5", "wg6", "sya", "sxa", "wg7", "gr",
    "szb", "sxb", "-32", "sxa", "szc", "syc", "gr", "-16", "sxb", "-24", "gr", "syc",
)


class Net:
    def __init__(self, send, recv):
        self.send_sem, self.recv_sem = send, recv
        self.count = 0
        self.pending = []

    def send(self, src, dst, device):
        k = self.count
        self.count += 1
        copy = pltpu.make_async_remote_copy(
            src_ref=src,
            dst_ref=dst,
            send_sem=self.send_sem.at[k],
            recv_sem=self.recv_sem.at[k],
            device_id=device,
            device_id_type=MESH,
        )
        copy.start()
        self.pending.append(copy)
        return copy

    def drain(self, n=None):
        n = len(self.pending) if n is None else n
        for copy in self.pending[:n]:
            copy.wait_send()
        self.pending = self.pending[n:]


def half16(n):
    return (n // 2 + 15) // 16 * 16


def ring4_gather(net, i, full, h0, h1, right, left):
    a = net.send(full(i), full(i), right)
    b = net.send(full(i), full(i), left)
    yield a, b
    prev, following = lax.rem(i + 3, 4), lax.rem(i + 1, 4)
    a.wait_recv()
    c = net.send(h0(prev), h0(prev), right)
    b.wait_recv()
    d = net.send(h1(following), h1(following), left)
    yield c, d
    c.wait_recv()
    d.wait_recv()
    yield ()


def direct_gather(net, i, full, right, left, far):
    a = net.send(full(i), full(i), right)
    b = net.send(full(i), full(i), left)
    c = net.send(full(i), full(i), far)
    yield a, b
    a.wait_recv()
    b.wait_recv()
    yield (c,)
    c.wait_recv()
    yield ()


def direct_scatter(net, i, full, slots, right, left, far):
    prev, following, other = lax.rem(i + 3, 4), lax.rem(i + 1, 4), lax.rem(i + 2, 4)
    a = net.send(full(other), slots[0][0], far)
    b = net.send(full(following), slots[0][1], right)
    c = net.send(full(prev), slots[1][0], left)
    yield a, b, c
    total = full(i)[...].astype(F32)
    for copy, slot in ((b, slots[0][1]), (c, slots[1][0]), (a, slots[0][0])):
        copy.wait_recv()
        total = total + slot[...].astype(F32)
    full(i)[...] = total.astype(BF)
    yield ()


def ring8_gather(net, i, full, h0, h1, right, left):
    a = net.send(full(i), full(i), right)
    b = net.send(full(i), full(i), left)
    yield a, b
    for step in (1, 2, 3):
        prev, following = lax.rem(i + 8 - step, 8), lax.rem(i + step, 8)
        va, vb = (full, full) if step < 3 else (h0, h1)
        a.wait_recv()
        a = net.send(va(prev), va(prev), right)
        b.wait_recv()
        b = net.send(vb(following), vb(following), left)
        yield a, b
    a.wait_recv()
    b.wait_recv()
    yield ()


def add_into(dst, src):
    dst[...] = (dst[...].astype(F32) + src[...].astype(F32)).astype(BF)


def ring_scatter(net, n, i, full, h0, h1, slots, right, left, early=False):
    far = lax.rem(i + n // 2, n)
    ra, rb = slots[0]
    a = net.send(h0(far), ra, right)
    b = net.send(h1(far), rb, left)
    yield () if early else (a, b)
    if early:
        to_r, to_l = lax.rem(far + n - 1, n), lax.rem(far + 1, n)
        na, nb = slots[1]
        a1 = net.send(h1(to_r), na.at[pl.ds(2, 2)], right)
        b1 = net.send(h0(to_l), nb.at[pl.ds(0, 2)], left)
        yield a, b
    for step in range(1, n // 2):
        to_r, to_l = lax.rem(i + n // 2 - step, n), lax.rem(i + n // 2 + step, n)
        halves = step == 1
        if early and step == 2:
            a1.wait_recv()
            b1.wait_recv()
        va, vb = (h0, h1) if halves else (full, full)
        a.wait_recv()
        add_into(va(to_r), ra)
        ra, rb_next = slots[step]
        if early and halves:
            a = net.send(h0(to_r), ra.at[pl.ds(0, 2)], right)
        else:
            a = net.send(full(to_r), ra, right)
        b.wait_recv()
        add_into(vb(to_l), rb)
        rb = rb_next
        if early and halves:
            b = net.send(h1(to_l), rb.at[pl.ds(2, 2)], left)
        else:
            b = net.send(full(to_l), rb, left)
        yield a, b
    a.wait_recv()
    b.wait_recv()
    dst = full(i)
    dst[...] = (dst[...].astype(F32) + ra[...].astype(F32) + rb[...].astype(F32)).astype(BF)
    yield ()


def scatter_slots():
    ra, rb, rc = SPLIT_R
    out = []

    def ring(n, half0, half1, whole):
        out.append([(half0, half1)] + [(whole, whole)] * (n // 2 - 1))

    for _ in range(NZ):
        ring(4, (2, rc, W), (2, rc, W), (4, rc, W))
        ring(4, (2, rb, W), (2, rb, W), (4, rb, W))
    ring(8, (2, 4, ra, W), (2, 4, ra, W), (4, 4, ra, W))
    ring(8, (2, rb, W), (2, rb, W), (4, rb, W))
    ring(8, (2, rc, W), (2, rc, W), (4, rc, W))
    for shape in ((4, ra, W), (ra, W), (rb, W), (rc, W)):
        out.append([(shape, shape), (shape,)])
    return out


N_SEM = 340
N_LOC = 32


def kernel(*refs):
    it = iter(refs)
    take = lambda n: [next(it) for _ in range(n)]
    tok_in, grad_in, ids_in, gates_in, wg_in, wu_in, wd_in = take(7)
    tok_out, gg_out, dgu_out, dd_out = take(4)
    buf, xs, gxs, wgu, wd, sel, selt, part = take(8)
    agu, araw, pgu, sh, gp, gatecol, member, target, gatev = take(9)
    rt, ggd, gg_rx, gg_rz = take(4)
    osg, osd, org, ord_ = take(4)
    stg, std = take(2)
    slots = [[tuple(take(len(pair))) for pair in ring] for ring in scatter_slots()]
    send_sem, recv_sem, loc_sem, stg_sem = take(4)

    e_idx = lax.axis_index("expert")
    z = lax.axis_index("etp")
    core = lax.rem(e_idx, 2)
    y = lax.rem(e_idx // 2, 4)
    x = e_idx // 8

    def dev(dx=0, dy=0, xx=None, yy=None, cc=None, zz=None):
        px = lax.rem(x + dx + 4, 4) if xx is None else xx
        py = lax.rem(y + dy + 4, 4) if yy is None else yy
        pc = core if cc is None else cc
        return ((px * 4 + py) * 2 + pc, z if zz is None else zz)

    xr, xl = dev(dx=1), dev(dx=-1)
    yr, yl = dev(dy=1), dev(dy=-1)
    zr, zl = dev(zz=lax.rem(z + 1, 8)), dev(zz=lax.rem(z + 7, 8))
    x_far, y_far = dev(dx=2), dev(dy=2)
    x_near = dev(xx=x + 1 - 2 * lax.rem(x, 2))
    y_near = dev(yy=y + 1 - 2 * lax.rem(y, 2))
    z1 = dev(zz=z + 1 - 2 * lax.rem(z, 2))
    z2 = dev(zz=z + 2 - 4 * lax.rem(z // 2, 2))
    z4 = dev(zz=lax.rem(z + 4, 8))
    sibling = dev(cc=1 - core)

    own_copies = [
        pltpu.make_async_copy(tok_in, buf.at[x, y, z, pl.ds(0, TOK)], loc_sem.at[0]),
        pltpu.make_async_copy(grad_in, buf.at[x, y, z, pl.ds(TOK, TOK)], loc_sem.at[1]),
    ]
    for j in range(2):
        ce = 2 * core + j
        own_copies.append(pltpu.make_async_copy(wg_in.at[j], wgu.at[ce, :, 0:H], loc_sem.at[2 + 3 * j]))
        own_copies.append(pltpu.make_async_copy(wu_in.at[j], wgu.at[ce, :, H : 2 * H], loc_sem.at[3 + 3 * j]))
        own_copies.append(pltpu.make_async_copy(wd_in.at[j], wd.at[ce], loc_sem.at[4 + 3 * j]))
    for c in own_copies:
        c.start()

    rt[x, y, 0:8, :] = ids_in[...].astype(F32)
    rt[x, y, 8:16, :] = gates_in[...].astype(F32)
    barrier = pltpu.get_barrier_semaphore()
    peers = (xr, xl, x_far, yr, yl, y_far, zr, zl, z2, z4, sibling)
    for p in peers:
        pl.semaphore_signal(barrier, inc=1, device_id=p, device_id_type=MESH)
    for c in own_copies[:2]:
        c.wait()
    pl.semaphore_wait(barrier, len(peers))

    net = Net(send_sem, recv_sem)

    sz = pl.ds
    ra, rb, rc = SPLIT_G
    ga, gb, gab, gc = sz(0, ra), sz(ra, rb), sz(0, ra + rb), sz(ra + rb, rc)
    hab, hb, hc = half16(ra + rb), half16(rb), half16(rc)
    zs = [z] + [lax.rem(z + k + 8, 8) for k in (1, -1, 2, -2, 3, -3, 4)]
    stage = [zs[0:1], zs[1:3], zs[3:5], zs[5:7], zs[7:8]]

    xab = direct_gather(net, x, lambda i: buf.at[i, y, z, gab], xr, xl, x_far)
    yc = direct_gather(net, y, lambda i: buf.at[x, i, z, gc], yr, yl, y_far)
    ya = direct_gather(net, y, lambda i: buf.at[:, i, z, ga], yr, yl, y_far)
    za = ring8_gather(
        net, z,
        lambda i: buf.at[:, :, i, ga],
        lambda i: buf.at[sz(0, 2), :, i, ga],
        lambda i: buf.at[sz(2, 2), :, i, ga],
        zr, zl)
    def column_b(px):
        return ring8_gather(
            net, z,
            lambda i: buf.at[px, y, i, gb],
            lambda i: buf.at[px, y, i, sz(ra, hb)],
            lambda i: buf.at[px, y, i, sz(ra + hb, rb - hb)],
            zr, zl)

    def column_c(py):
        return ring8_gather(
            net, z,
            lambda i: buf.at[x, py, i, gc],
            lambda i: buf.at[x, py, i, sz(ra + rb, hc)],
            lambda i: buf.at[x, py, i, sz(ra + rb + hc, rc - hc)],
            zr, zl)

    def plane(zz):
        return (
            ring4_gather(
                net, x,
                lambda i: buf.at[i, :, zz, gc],
                lambda i: buf.at[i, sz(0, 2), zz, gc],
                lambda i: buf.at[i, sz(2, 2), zz, gc],
                xr, xl),
            ring4_gather(
                net, y,
                lambda i: buf.at[:, i, zz, gb],
                lambda i: buf.at[sz(0, 2), i, zz, gb],
                lambda i: buf.at[sz(2, 2), i, zz, gb],
                yr, yl),
        )

    def half_plane(zz, k):
        lo = 2 * k
        return (
            ring4_gather(
                net, x,
                lambda i: buf.at[i, sz(lo, 2), zz, gc],
                lambda i: buf.at[i, sz(lo, 1), zz, gc],
                lambda i: buf.at[i, sz(lo + 1, 1), zz, gc],
                xr, xl),
            ring4_gather(
                net, y,
                lambda i: buf.at[sz(lo, 2), i, zz, gb],
                lambda i: buf.at[sz(lo, 1), i, zz, gb],
                lambda i: buf.at[sz(lo + 1, 1), i, zz, gb],
                yr, yl),
        )

    def route_ring():
        c = net.send(rt.at[x, y], rt.at[x, y], y_near)
        yield (c,)
        c.wait_recv()
        yh = 2 * (y // 2)
        c = net.send(rt.at[x, sz(yh, 2)], rt.at[x, sz(yh, 2)], y_far)
        yield (c,)
        c.wait_recv()
        c = net.send(rt.at[x], rt.at[x], x_near)
        yield (c,)
        c.wait_recv()
        xh = 2 * (x // 2)
        c = net.send(rt.at[sz(xh, 2)], rt.at[sz(xh, 2)], x_far)
        yield (c,)
        c.wait_recv()
        yield ()

    def load_weights():
        for c in own_copies[2:]:
            c.wait()
        copies = []
        for j in range(2):
            ce = 2 * core + j
            copies.append(net.send(wgu.at[ce], wgu.at[ce], sibling))
            copies.append(net.send(wd.at[ce], wd.at[ce], sibling))
        yield copies
        for c in copies:
            c.wait_recv()
        yield ()

    tasks = {}

    def ring_task(name, steps):
        tasks[name] = lambda: next(steps)

    ring_task("xab", xab)
    ring_task("yc", yc)
    ring_task("ya", ya)
    ring_task("za", za)
    for k, d in enumerate((0, 1, 3, 2)):
        ring_task(f"zb{k}", column_b(lax.rem(x + d, 4)))
        ring_task(f"zc{k}", column_c(lax.rem(y + d, 4)))
    for k, d in enumerate((0, 1, 3, 2)):
        py = lax.rem(y + d, 4)
        ring_task(f"pq{k}", ring4_gather(
            net, x,
            lambda i, py=py: buf.at[i, py, z, gc],
            lambda i, py=py: buf.at[i, py, z, sz(ra + rb, hc)],
            lambda i, py=py: buf.at[i, py, z, sz(ra + rb + hc, rc - hc)],
            xr, xl))
    for k, zz in enumerate(zs):
        for h in range(1 + k // 7):
            gx, gy = half_plane(zz, h) if k == 7 else plane(zz)
            if k > 0:
                ring_task(f"px{k + h}", gx)
            ring_task(f"py{k + h}", gy)
    ring_task("rt", route_ring())
    ring_task("wl", load_weights())
    first_expert = 4 * (x * 4 + y)

    def route():
        for b in range(16):
            tile = rt[b // 4, b % 4]
            for e in range(E4):
                hit = tile[0:8, :] == (first_expert + e).astype(F32)
                member[e * 16 + b, :] = jnp.sum(jnp.where(hit, 1.0, 0.0), axis=0)
                gatev[e * 16 + b, :] = jnp.sum(jnp.where(hit, tile[8:16, :], 0.0), axis=0)
        tri = jnp.where(
            lax.broadcasted_iota(jnp.int32, (TOK, TOK), 0) < lax.broadcasted_iota(jnp.int32, (TOK, TOK), 1),
            1.0, 0.0).astype(BF)
        m = member[...]
        pos = jnp.dot(m.astype(BF), tri, preferred_element_type=F32)
        target[...] = jnp.where(m > 0.5, pos, -1.0)

        for p in range(PAIRS):
            row = lax.broadcasted_iota(jnp.int32, (CAP, TOK), 0).astype(F32)
            zero = jnp.zeros((CAP, TOK), F32)
            parts = []
            for e in range(E4):
                r0, r1 = e * 16 + 2 * p, e * 16 + 2 * p + 1
                s0 = jnp.where(row == target[r0 : r0 + 1, :], 1.0, 0.0)
                s1 = jnp.where(row == target[r1 : r1 + 1, :], 1.0, 0.0)
                parts.append(jnp.concatenate([s0, zero], axis=1))
                parts.append(jnp.concatenate([zero, s1], axis=1))
            full = jnp.concatenate(parts, axis=0)
            sel[p] = full.astype(BF)
            selt[p] = full.T.astype(BF)

    def pick(zz):
        def body(px, _):
            for q in range(2):
                p = 2 * px + q
                s = sel[p]
                for r0, dst in ((0, xs), (TOK, gxs)):
                    t = buf[px, 2 * q : 2 * q + 2, zz, r0 : r0 + TOK, :].reshape(2 * TOK, W)
                    o = jnp.dot(s, t, preferred_element_type=F32).astype(BF)
                    for e in range(E4):
                        dst[zz, e, pl.ds(pl.multiple_of(p * 48, 16), 48), :] = o[e * 48 : (e + 1) * 48]
            return 0

        lax.fori_loop(0, PAIRS // 2, body, 0)

    def accumulate(zz, first):
        f = pl.ds(pl.multiple_of(zz * W, W), W)

        def body(e):
            gu = jnp.dot(xs[zz, e], wgu[e, f, :], preferred_element_type=F32)
            raw = lax.dot_general(gxs[zz, e], wd[e, :, f], (((1,), (1,)), ((), ())), preferred_element_type=F32)
            if first:
                agu[e] = gu
                araw[e] = raw
            else:
                agu[e] += gu
                araw[e] += raw

        for e in range(E4):
            body(e)

    def gate_columns(e):
        for p in range(PAIRS):
            for k in range(2):
                s = sel[p, pl.ds(pl.multiple_of(e * 48, 16), 48), k * TOK : (k + 1) * TOK].astype(F32)
                g = gatev[pl.ds(e * 16 + 2 * p + k, 1), :]
                col = jnp.sum((s * g)[k * CAP : (k + 1) * CAP], axis=1, keepdims=True)
                gatecol[e, pl.ds(p * 48 + k * CAP, CAP), :] = jnp.broadcast_to(col, (CAP, H))

    def forward(e):
        gu, raw = agu[e], araw[e]
        gate_pre, up_pre = gu[:, :H], gu[:, H:]
        sig = 1.0 / (1.0 + jnp.exp(-gate_pre))
        swish = gate_pre * sig
        hidden = swish * up_pre
        gp[e] = jnp.broadcast_to(jnp.sum(hidden * raw, axis=1, keepdims=True), (ROWS, H))
        gate = gatecol[e]
        hg = gate * raw
        pgu[e, :, H:] = (hg * swish).astype(BF)
        pgu[e, :, :H] = (hg * up_pre * sig * (1.0 + gate_pre * (1.0 - sig))).astype(BF)
        sh[e] = (gate * hidden).astype(BF)

    def produce(zz):
        f = pl.ds(pl.multiple_of(zz * W, W), W)

        def products(e):
            o = lax.dot_general(pgu[e], wgu[e, f, :], (((1,), (1,)), ((), ())),
                                preferred_element_type=F32).astype(BF)
            for p in range(PAIRS):
                part[p, e * 48 : (e + 1) * 48, :] = o[p * 48 : (p + 1) * 48]

        def spread(p, _):
            for q in range(4):
                o = jnp.dot(selt[4 * p + q], part[4 * p + q], preferred_element_type=F32).astype(BF)
                buf[2 * p + q // 2, 2 * (q % 2) : 2 * (q % 2) + 2, zz, 0:TOK, :] = o.reshape(2, TOK, W)
            return 0

        for e in range(E4):
            products(e)
        lax.fori_loop(0, PAIRS // 4, spread, 0)

    def gate_terms(p):
        for k in range(2):
            rows = []
            px, py = p // 2, 2 * (p % 2) + k
            tile = rt[px, py][0:8, :]
            acc = jnp.zeros((8, TOK), F32)
            for e in range(E4):
                s = sel[p, e * 48 : (e + 1) * 48, k * TOK : (k + 1) * TOK].astype(F32)
                v = jnp.sum(s * gp[e, pl.ds(pl.multiple_of(p * 48, 16), 48), :], axis=0, keepdims=True)
                acc = acc + jnp.where(tile == (first_expert + e).astype(F32), v, 0.0)
            ggd[px, py] = acc

    def loop(n, f):
        def body(i, _):
            f(i)
            return 0

        lax.fori_loop(0, n, body, 0)

    def do(order):
        for name in order:
            if name[0] == "-":
                net.drain(int(name[1:]))
            else:
                tasks[name]()

    tasks["route"] = route
    tasks["gcol"] = lambda: loop(E4, gate_columns)
    for k, zz in enumerate(zs):
        tasks[f"pick{k}"] = functools.partial(pick, zz)
        tasks[f"acc{k}"] = functools.partial(accumulate, zz, k == 0)
    do(GATHER)
    net.drain()
    loop(E4, forward)

    ra, rb, rc = SPLIT_R
    sa, sb, sc = sz(0, ra), sz(ra, rb), sz(ra + rb, rc)

    def rplane(k, zz):
        return (
            ring_scatter(
                net, 4, x,
                lambda i: buf.at[i, :, zz, sc],
                lambda i: buf.at[i, sz(0, 2), zz, sc],
                lambda i: buf.at[i, sz(2, 2), zz, sc],
                slots[2 * k], xr, xl),
            ring_scatter(
                net, 4, y,
                lambda i: buf.at[:, i, zz, sb],
                lambda i: buf.at[sz(0, 2), i, zz, sb],
                lambda i: buf.at[sz(2, 2), i, zz, sb],
                slots[2 * k + 1], yr, yl),
        )

    for k, zz in enumerate(zs):
        gx, gy = rplane(k, zz)
        ring_task(f"rx{k}", gx)
        ring_task(f"ry{k}", gy)
        tasks[f"make{k}"] = functools.partial(produce, zz)
    slots = slots[16:]
    sza = ring_scatter(
        net, 8, z,
        lambda i: buf.at[:, :, i, sa],
        lambda i: buf.at[sz(0, 2), :, i, sa],
        lambda i: buf.at[sz(2, 2), :, i, sa],
        slots[0], zr, zl, early=True)
    szb = ring_scatter(
        net, 8, z,
        lambda i: buf.at[:, y, i, sb],
        lambda i: buf.at[sz(0, 2), y, i, sb],
        lambda i: buf.at[sz(2, 2), y, i, sb],
        slots[1], zr, zl)
    szc = ring_scatter(
        net, 8, z,
        lambda i: buf.at[x, :, i, sc],
        lambda i: buf.at[x, sz(0, 2), i, sc],
        lambda i: buf.at[x, sz(2, 2), i, sc],
        slots[2], zr, zl)
    sya = direct_scatter(net, y, lambda i: buf.at[:, i, z, sa], slots[3], yr, yl, y_far)
    sxa = direct_scatter(net, x, lambda i: buf.at[i, y, z, sa], slots[4], xr, xl, x_far)
    sxb = direct_scatter(net, x, lambda i: buf.at[i, y, z, sb], slots[5], xr, xl, x_far)
    syc = direct_scatter(net, y, lambda i: buf.at[x, i, z, sc], slots[6], yr, yl, y_far)

    def gate_ring():
        xo = 2 - 2 * (x // 2)
        c = net.send(ggd.at[sz(xo, 2)], gg_rx.at[sz(0, 2)], x_far)
        yield (c,)
        c.wait_recv()
        xm = 2 * (x // 2)
        for k in range(2):
            for j in range(4):
                ggd[xm + k, j] = ggd[xm + k, j] + gg_rx[k, j]
        xn = x + 1 - 2 * lax.rem(x, 2)
        c = net.send(ggd.at[xn], gg_rx.at[2], x_near)
        yield (c,)
        c.wait_recv()
        for j in range(4):
            ggd[x, j] = ggd[x, j] + gg_rx[2, j]
        yo = 2 - 2 * (y // 2)
        c = net.send(ggd.at[x, sz(yo, 2)], gg_rx.at[3, sz(0, 2)], y_far)
        yield (c,)
        c.wait_recv()
        ym = 2 * (y // 2)
        for k in range(2):
            ggd[x, ym + k] = ggd[x, ym + k] + gg_rx[3, k]
        yn = y + 1 - 2 * lax.rem(y, 2)
        c = net.send(ggd.at[x, yn], gg_rx.at[3, 2], y_near)
        yield (c,)
        c.wait_recv()
        gg_rz[0] = ggd[x, y] + gg_rx[3, 2]
        for k, d in enumerate((z1, z2, z4)):
            c = net.send(gg_rz.at[2 * k], gg_rz.at[2 * k + 1], d)
            yield (c,)
            c.wait_recv()
            gg_rz[2 * k + 2] = gg_rz[2 * k] + gg_rz[2 * k + 1]
        yield ()

    tn = (((0,), (0,)), ((), ()))

    grad_copies = []

    def other_grads(j):
        e = 2 * (1 - core) + j

        def body(h, _):
            for q in range(2):
                m = 2 * h + q
                f = pl.ds(pl.multiple_of(m * W, W), W)
                osg[j, f, :] = lax.dot_general(xs[m, e], pgu[e], tn, preferred_element_type=F32).astype(BF)
                osd[j, :, f] = lax.dot_general(sh[e], gxs[m, e], tn, preferred_element_type=F32).astype(BF)
            return 0

        lax.fori_loop(0, NZ // 2, body, 0)
        grad_copies.extend([net.send(osg.at[j], org.at[j], sibling), net.send(osd.at[j], ord_.at[j], sibling)])

    def own_grads(lo, hi):
        def outs(j, m, slot):
            f = pl.ds(pl.multiple_of(m * W, W), W)
            return [
                pltpu.make_async_copy(stg.at[slot], dgu_out.at[j, f, :], stg_sem.at[slot, 0]),
                pltpu.make_async_copy(std.at[slot], dd_out.at[j, :, f], stg_sem.at[slot, 1]),
            ]

        def body(t, _):
            for slot in range(2):
                j, m = t // (NZ // 2), 2 * (t % (NZ // 2)) + slot
                e = 2 * core + j
                f = pl.ds(pl.multiple_of(m * W, W), W)

                @pl.when(t >= 1)
                def _():
                    for c in outs(j, m, slot):
                        c.wait()

                a = lax.dot_general(xs[m, e], pgu[e], tn, preferred_element_type=F32)
                stg[slot] = (a + org[j, f, :].astype(F32)).astype(BF)
                b = lax.dot_general(sh[e], gxs[m, e], tn, preferred_element_type=F32)
                std[slot] = (b + ord_[j, :, f].astype(F32)).astype(BF)
                for c in outs(j, m, slot):
                    c.start()
            return 0

        if lo == 0:
            for c in grad_copies:
                c.wait_recv()
        lax.fori_loop(lo, hi, body, 0)
        if hi == NZ:
            for slot in range(2):
                for c in outs(0, 0, slot):
                    c.wait()

    for name, steps in (("sza", sza), ("szb", szb), ("szc", szc), ("sya", sya),
                        ("sxa", sxa), ("sxb", sxb), ("syc", syc), ("gr", gate_ring())):
        ring_task(name, steps)
    tasks["gt"] = lambda: loop(PAIRS, gate_terms)
    for j in range(2):
        tasks[f"og{j}"] = functools.partial(other_grads, j)
    for t in range(NZ):
        tasks[f"wg{t}"] = functools.partial(own_grads, t, t + 1)
    do(SCATTER)

    tok_out[...] = buf[x, y, z, 0:TOK, :]
    gg_out[...] = gg_rz[6]
    net.drain()


CHUNKS = 4


def finish_kernel(tok, gg, dgu, dd, tok_out, gg_out, dg_out, du_out, dd_out, in_gu, in_d, out_g, out_u, out_d, in_sem, out_sem):
    n = D // CHUNKS
    small = [
        pltpu.make_async_copy(tok, tok_out, out_sem.at[CHUNKS, 0]),
        pltpu.make_async_copy(gg, gg_out, out_sem.at[CHUNKS, 1]),
    ]
    loads, stores = [], []
    for m in range(CHUNKS):
        f = slice(m * n, (m + 1) * n)
        loads.append((
            pltpu.make_async_copy(dgu.at[:, f, :], in_gu.at[m], in_sem.at[m, 0]),
            pltpu.make_async_copy(dd.at[:, :, f], in_d.at[m], in_sem.at[m, 1]),
        ))
        stores.append((
            pltpu.make_async_copy(out_g.at[m], dg_out.at[:, f, :], out_sem.at[m, 0]),
            pltpu.make_async_copy(out_u.at[m], du_out.at[:, f, :], out_sem.at[m, 1]),
            pltpu.make_async_copy(out_d.at[m], dd_out.at[:, :, f], out_sem.at[m, 2]),
        ))
    for pair in loads:
        for c in pair:
            c.start()
    for c in small:
        c.start()
    for m in range(CHUNKS):
        loads[m][0].wait()
        out_g[m] = in_gu[m, :, :, :H].astype(F32)
        stores[m][0].start()
        out_u[m] = in_gu[m, :, :, H:].astype(F32)
        stores[m][1].start()
        loads[m][1].wait()
        out_d[m] = in_d[m].astype(F32)
        stores[m][2].start()
    for c in small:
        c.wait()
    for group in stores:
        for c in group:
            c.wait()


def finish(tok, gg, dgu, dd):
    n = D // CHUNKS
    any_spec = pl.BlockSpec(memory_space=pl.ANY)
    return pl.pallas_call(
        finish_kernel,
        in_specs=[any_spec] * 4,
        out_specs=[any_spec] * 5,
        out_shape=(
            jax.ShapeDtypeStruct((TOK, W), BF),
            jax.ShapeDtypeStruct((8, TOK), F32),
            jax.ShapeDtypeStruct((2, D, H), F32),
            jax.ShapeDtypeStruct((2, D, H), F32),
            jax.ShapeDtypeStruct((2, H, D), F32),
        ),
        scratch_shapes=[
            pltpu.VMEM((CHUNKS, 2, n, 2 * H), BF),
            pltpu.VMEM((CHUNKS, 2, H, n), BF),
            pltpu.VMEM((CHUNKS, 2, n, H), F32),
            pltpu.VMEM((CHUNKS, 2, n, H), F32),
            pltpu.VMEM((CHUNKS, 2, H, n), F32),
            pltpu.SemaphoreType.DMA((CHUNKS, 2)),
            pltpu.SemaphoreType.DMA((CHUNKS + 1, 3)),
        ],
        compiler_params=pltpu.CompilerParams(vmem_limit_bytes=62 * 1024 * 1024),
    )(tok, gg, dgu, dd)


def local(tokens, grad_output, gates, ids, gate_weight, up_weight, down_weight):
    any_spec = pl.BlockSpec(memory_space=pl.ANY)
    vmem = pl.BlockSpec(memory_space=pltpu.VMEM)
    scratch = [
        pltpu.VMEM((NX, NY, NZ, 2 * TOK, W), BF),
        pltpu.VMEM((NZ, E4, ROWS, W), BF),
        pltpu.VMEM((NZ, E4, ROWS, W), BF),
        pltpu.VMEM((E4, D, 2 * H), BF),
        pltpu.VMEM((E4, H, D), BF),
        pltpu.VMEM((PAIRS, 192, 2 * TOK), BF),
        pltpu.VMEM((PAIRS, 2 * TOK, 192), BF),
        pltpu.VMEM((PAIRS, 192, W), BF),
        pltpu.VMEM((E4, ROWS, 2 * H), F32),
        pltpu.VMEM((E4, ROWS, H), F32),
        pltpu.VMEM((E4, ROWS, 2 * H), BF),
        pltpu.VMEM((E4, ROWS, H), BF),
        pltpu.VMEM((E4, ROWS, H), F32),
        pltpu.VMEM((E4, ROWS, H), F32),
        pltpu.VMEM((64, TOK), F32),
        pltpu.VMEM((64, TOK), F32),
        pltpu.VMEM((64, TOK), F32),
        pltpu.VMEM((NX, NY, 16, TOK), F32),
        pltpu.VMEM((NX, NY, 8, TOK), F32),
        pltpu.VMEM((4, 4, 8, TOK), F32),
        pltpu.VMEM((7, 8, TOK), F32),
        pltpu.VMEM((2, D, 2 * H), BF),
        pltpu.VMEM((2, H, D), BF),
        pltpu.VMEM((2, D, 2 * H), BF),
        pltpu.VMEM((2, H, D), BF),
        pltpu.VMEM((2, W, 2 * H), BF),
        pltpu.VMEM((2, H, W), BF),
    ]
    for ring in scatter_slots():
        for pair in ring:
            for shape in pair:
                scratch.append(pltpu.VMEM(shape, BF))
    scratch += [
        pltpu.SemaphoreType.DMA((N_SEM,)),
        pltpu.SemaphoreType.DMA((N_SEM,)),
        pltpu.SemaphoreType.DMA((N_LOC,)),
        pltpu.SemaphoreType.DMA((2, 2)),
    ]
    outs = pl.pallas_call(
        kernel,
        out_shape=(
            jax.ShapeDtypeStruct((TOK, W), BF),
            jax.ShapeDtypeStruct((8, TOK), F32),
            jax.ShapeDtypeStruct((2, D, 2 * H), BF),
            jax.ShapeDtypeStruct((2, H, D), BF),
        ),
        in_specs=[any_spec, any_spec, vmem, vmem, any_spec, any_spec, any_spec],
        out_specs=(vmem, vmem, any_spec, any_spec),
        scratch_shapes=scratch,
        compiler_params=pltpu.CompilerParams(
            collective_id=0, has_side_effects=True, vmem_limit_bytes=63 * 1024 * 1024
        ),
    )(tokens, grad_output, ids.T, gates.T, gate_weight, up_weight, down_weight)
    grad_tokens, gate_grads, grad_gate, grad_up, grad_down = finish(*outs)
    return (grad_tokens, gate_grads.T, grad_gate, grad_up, grad_down)


def solution(mesh):
    return jax.shard_map(
        local,
        mesh=mesh,
        in_specs=(
            P("expert", "etp"),
            P("expert", "etp"),
            P("expert", None),
            P("expert", None),
            P("expert", None, "etp"),
            P("expert", None, "etp"),
            P("expert", "etp", None),
        ),
        out_specs=(
            P("expert", "etp"),
            P("expert", None),
            P("expert", None, "etp"),
            P("expert", None, "etp"),
            P("expert", "etp", None),
        ),
        check_vma=False,
    )
```
